256 devices in a mesh: section: 4 (over z_lo, core), dp: 4 (over x), mp: 16 (over y, z_hi).
Axes of the slice: x: 4, y: 4, z: 8 (z_hi: 4, z_lo: 2; z = z_hi * 2 + z_lo), core: 2. Of those that a mesh axis runs over, the one named last changes fastest.
Arguments:
- caption_tokens: bfloat16 [16, 64, 4096], P('dp', None, 'mp'), may hold values from -6 to 6
- caption_lengths: int32 [16], P('dp'), may hold values from 1 to 64, as said below
- group_ids: int32 [16], replicated, may hold values from 0 to 3, as said below
- text_gain: float32 [4, 4096], P('section'), may hold values from 0.5 to 1.5
- text_gate: bfloat16 [4, 4096, 14336], P('section', 'dp', 'mp'), may hold values from -0.09375 to 0.09375
- text_up: bfloat16 [4, 4096, 14336], P('section', 'dp', 'mp'), may hold values from -0.09375 to 0.09375
- text_down: bfloat16 [4, 14336, 4096], P('section', 'mp', 'dp'), may hold values from -0.0625 to 0.0625
- text_proj: bfloat16 [4096, 768], P('mp'), may hold values from -0.09375 to 0.09375
- image_patches: bfloat16 [4, 256, 1024], P('dp', 'section'), may hold values from -6 to 6
- image_gain: float32 [1024], replicated, may hold values from 0.5 to 1.5
- image_fc1: bfloat16 [1024, 4096], P(None, 'mp'), may hold values from -0.1875 to 0.1875
- image_fc2: bfloat16 [4096, 1024], P('mp'), may hold values from -0.09375 to 0.09375
- image_proj: bfloat16 [1024, 768], replicated, may hold values from -0.1875 to 0.1875
Outputs:
- loss_mean: float32 [], replicated
- grad_captions: float32 [16, 768], P('dp')
- grad_images: float32 [4, 768], P('dp')
The draws below stay inside these ranges and needn't reach their ends.
Inputs may be any that keep to these rules, and one draw needn't show every extreme that they name: `caption_lengths`: every caption has at least one token; some caption has exactly 64. `group_ids`: each image index is named by exactly four captions.
All inputs are finite; a program needn't handle non-finite values.
Results may differ from the reference program's by a relative error of at most 0.035.
Values may be sent and summed in bfloat16 or wider, within the bound.
A program may use at most 128 MiB of HBM per device.

```python
import jax
import jax.numpy as jnp
from jax import lax

D = 4096
FF = 14336
L = 64
DV = 1024
FV = 4096
P_SIZE = 256
E = 768
NCAP = 16
NIMG = 4
LAYERS = 4
N_MP = 16


def draw_caption_lengths(key, part):
    key = jax.random.fold_in(key, 11)
    first, second = jax.random.split(key)
    values = jax.random.randint(first, (NCAP,), 1, L + 1, dtype=jnp.int32)
    where_full = jax.random.randint(second, (), 0, NCAP, dtype=jnp.int32)
    return values.at[where_full].set(L)


def draw_group_ids(key, part):
    key = jax.random.fold_in(key, 23)
    order = jax.random.permutation(key, NCAP).astype(jnp.int32)
    return (order // 4).astype(jnp.int32)


def spiked(values, key, source, target, parts, factor):
    def block_of(dim):
        return (jnp.arange(values.shape[dim]) // (values.shape[dim] // parts)).reshape((-1,) + (1,) * (values.ndim - 1 - dim))

    one_side = jax.random.permutation(key, parts)[block_of(target)]
    other_side = (block_of(target) + parts // 2) % parts
    return jnp.where((block_of(source) == one_side) | (block_of(source) == other_side), factor * values, values)


def levels(own_key, shape, pieces, smallest, high):
    level, own = 1.0, jax.random.fold_in(own_key, 6)
    for axis_at, parts in pieces:
        draws = jnp.exp(jax.random.uniform(jax.random.fold_in(own, axis_at), (parts,), jnp.float32, smallest / len(pieces), high / len(pieces)))
        level = level * jnp.repeat(draws, shape[axis_at] // parts).reshape([-1 if axis == axis_at else 1 for axis in range(len(shape))])
    return level


def centred(own_key, extent, scale, most, cuts=(), kind=jnp.bfloat16):
    loudness = levels(own_key, extent, cuts, -0.22, 0.18) if cuts else 1.0
    drawn = jax.random.normal(own_key, extent, jnp.float32) * scale * loudness
    return jnp.minimum(jnp.maximum(drawn, -most), most).astype(kind)


def noise_with(key, extent, spread, reach, pieces, heavy, kind=jnp.bfloat16):
    result = spread * jax.random.normal(key, extent, jnp.float32)
    if pieces:
        result = result * levels(key, extent, pieces, -0.22, 0.18)
    return jnp.clip(spiked(result, jax.random.fold_in(key, 3), *heavy), -reach, reach).astype(kind)


def setup_inputs(seed: int = 0) -> dict:
    splits = jax.random.split(jax.random.key(seed), 14)
    return {
        "caption_tokens": centred(splits[0], (NCAP, L, D), 1.0, 6.0, ((0, 4), (2, 16))),
        "caption_lengths": draw_caption_lengths(jax.random.fold_in(splits[13], 71), 0),
        "group_ids": draw_group_ids(jax.random.fold_in(splits[13], 71), 0),
        "text_gain": jnp.clip(1.0 + 0.1 * jax.random.normal(splits[3], (LAYERS, D), jnp.float32), 0.5, 1.5),
        "text_gate": centred(splits[4], (LAYERS, D, FF), D ** -0.5, 0.09375, ((0, 4), (1, 4), (2, 16))),
        "text_up": centred(splits[5], (LAYERS, D, FF), D ** -0.5, 0.09375, ((0, 4), (1, 4), (2, 16))),
        "text_down": noise_with(splits[6], (LAYERS, FF, D), FF ** -0.5, 0.0625, ((0, 4), (1, 16), (2, 4)), (1, 2, 16, 2.0)),
        "text_proj": centred(splits[7], (D, E), D ** -0.5, 0.09375, ((0, 16),)),
        "image_patches": centred(splits[8], (NIMG, P_SIZE, DV), 1.0, 6.0, ((0, 4), (1, 4))),
        "image_gain": jnp.clip(1.0 + 0.1 * jax.random.normal(splits[9], (DV,), jnp.float32), 0.5, 1.5),
        "image_fc1": centred(splits[10], (DV, FV), DV ** -0.5, 0.1875, ((1, 16),)),
        "image_fc2": centred(splits[11], (FV, DV), FV ** -0.5, 0.09375, ((0, 16),)),
        "image_proj": centred(splits[12], (DV, E), DV ** -0.5, 0.1875),
    }


def text_layer(hidden, gain, gate_w, up_w, down_w):
    values = hidden.astype(jnp.float32)
    normed = (values * lax.rsqrt(lax.optimization_barrier(jnp.mean(values * values, -1, keepdims=True)) + 1e-05) * gain).astype(jnp.bfloat16)
    gate = jnp.dot(normed, gate_w, preferred_element_type=jnp.float32)
    upper = jnp.dot(normed, up_w, preferred_element_type=jnp.float32)
    inner = (jax.nn.silu(gate) * upper).astype(jnp.bfloat16)
    width = FF // N_MP

    def add_block(total, index):
        piece = lax.dynamic_slice_in_dim(inner, index * width, width, 1)
        rows_w = lax.dynamic_slice_in_dim(down_w, index * width, width, 0)
        rounded = jnp.dot(piece, rows_w, preferred_element_type=jnp.float32).astype(jnp.bfloat16)
        rounded = lax.optimization_barrier(rounded)
        return (total + rounded.astype(jnp.float32), None)
    start = jnp.zeros(values.shape, jnp.float32)
    branch, _ = lax.scan(add_block, start, jnp.arange(N_MP, dtype=jnp.int32))
    return (values + branch).astype(jnp.bfloat16)

def contrast_total(caption_unit, image_unit, group_ids):
    logits = 10.0 * jnp.dot(caption_unit, image_unit.T, precision=lax.Precision.HIGHEST)
    matches = (group_ids[:, None] == jnp.arange(image_unit.shape[0], dtype=jnp.int32)[None, :]).astype(jnp.float32)
    expo = jnp.exp(logits)
    forward = jnp.log(lax.optimization_barrier(jnp.sum(expo, 1))) - lax.optimization_barrier(jnp.sum(logits * matches, 1))
    backward = jnp.log(lax.optimization_barrier(jnp.sum(expo, 0))) - jnp.log(lax.optimization_barrier(jnp.sum(expo * matches, 0)))
    total = 0.5 * (jnp.sum(forward) + jnp.sum(backward))
    return (total, 0.5 * (jnp.mean(forward) + jnp.mean(backward)))

def unit_rows(matrix):
    return matrix * lax.rsqrt(lax.optimization_barrier(jnp.sum(matrix * matrix, -1, keepdims=True)) + 1e-06)

def reference(caption_tokens, caption_lengths, group_ids, text_gain, text_gate, text_up, text_down, text_proj, image_patches, image_gain, image_fc1, image_fc2, image_proj):
    hidden = caption_tokens.reshape(NCAP * L, D)
    for layer in range(LAYERS):
        hidden = text_layer(hidden, text_gain[layer], text_gate[layer], text_up[layer], text_down[layer])
    encoded = hidden.reshape(NCAP, L, D).astype(jnp.float32)
    positions = lax.broadcasted_iota(jnp.int32, (NCAP, L), 1)
    masked = (positions < caption_lengths[:, None]).astype(jnp.float32)
    pooled = lax.optimization_barrier(jnp.sum(encoded * masked[:, :, None], 1)) / caption_lengths.astype(jnp.float32)[:, None]
    caption_embed = jnp.dot(pooled.astype(jnp.bfloat16), text_proj, preferred_element_type=jnp.float32)
    values = image_patches.reshape(NIMG * P_SIZE, DV).astype(jnp.float32)
    vnormed = (values * lax.rsqrt(lax.optimization_barrier(jnp.mean(values * values, -1, keepdims=True)) + 1e-05) * image_gain).astype(jnp.bfloat16)
    vinner = jax.nn.gelu(jnp.dot(vnormed, image_fc1, preferred_element_type=jnp.float32), approximate=False).astype(jnp.bfloat16)
    vout = values + jnp.dot(vinner, image_fc2, preferred_element_type=jnp.float32)
    image_pooled = lax.optimization_barrier(jnp.mean(vout.reshape(NIMG, P_SIZE, DV), 1)).astype(jnp.bfloat16)
    image_embed = jnp.dot(image_pooled, image_proj, preferred_element_type=jnp.float32)
    caption_unit = unit_rows(caption_embed)
    image_unit = unit_rows(image_embed)

    def wrapped(first, second):
        return contrast_total(first, second, group_ids)
    _, pullback, loss_mean = jax.vjp(wrapped, caption_unit, image_unit, has_aux=True)
    grad_captions, grad_images = pullback(jnp.ones((), jnp.float32))
    return (loss_mean, grad_captions, grad_images)
```

```python
import functools

import jax
import jax.numpy as jnp
from jax import lax
from jax.experimental import pallas as pl
from jax.experimental.pallas import tpu as pltpu
from jax.sharding import PartitionSpec as P

MESH = pl.DeviceIdType.MESH
BF16 = jnp.bfloat16
F32 = jnp.float32


def kernel(
    sizes,
    tok_ref, len_ref, gid_ref, gain_ref, gate_ref, up_ref, down_ref, tproj_ref,
    patch_ref, vgain_ref, fc1_ref, fc2_ref, iproj_ref,
    loss_ref, gcap_ref, gimg_ref,
    w_gu, w_dn, w_tp, w_f1, w_f2, w_ip, patches,
    x_buf, xg_buf, p_buf, r_buf, i_buf, q_buf, s_buf, h_buf,
    lens, im1, im1_own, im2, im2_own, imrow, mean_h,
    pin, pd, pdr, emb, embr, outb,
    wsem, tok_ss, xr, ps, pr, iss, ir, qs, qr, hs,
    len_s, len_r, im1_s, im1_r, im2_s, im2_r, pin_s, pin_r, pd_s, pd_r, e_s, e_r, out_s, out_r,
):
    ns, nd, nm = sizes
    grp = nm // nd
    micro, length, piece = tok_ref.shape
    batch = nd * length
    own_rows = batch // nm
    dl = x_buf.shape[2]
    width = gate_ref.shape[2]
    dim = dl * nd
    sec, dp, mp = lax.axis_index("section"), lax.axis_index("dp"), lax.axis_index("mp")
    last = ns - 1
    my_group = mp // grp
    my_q = lax.rem(mp, grp)
    is_final = jnp.logical_and(sec == last, my_group == dp)

    def send(src, dst, s_sem, r_sem, where):
        pltpu.make_async_remote_copy(
            src_ref=src, dst_ref=dst, send_sem=s_sem, recv_sem=r_sem,
            device_id=where, device_id_type=MESH,
        ).start()

    def drain(ref, sem):
        pltpu.make_async_copy(ref, ref, sem).wait()

    def load(src, dst, index):
        pltpu.make_async_copy(src, dst, wsem.at[index]).start()

    def loaded(dst, index):
        pltpu.make_async_copy(dst, dst, wsem.at[index]).wait()

    per = nm // ns

    def token_target(k):
        target = per * sec + k
        home = jnp.logical_and(sec == 0, jnp.logical_and(my_group == dp, target == mp))
        return target, home

    def token_batch(b, _):
        def token_one(k, _):
            target, home = token_target(k)
            dst = x_buf.at[b, pl.ds(pl.multiple_of(dp * length, length), length),
                           pl.ds(pl.multiple_of(my_q * piece, piece), piece)]

            @pl.when(home)
            def _():
                pltpu.make_async_copy(tok_ref.at[b], dst, xr.at[b]).start()

            @pl.when(jnp.logical_not(home))
            def _():
                send(tok_ref.at[b], dst, tok_ss.at[k], xr.at[b], (0, my_group, target))
            return 0

        return lax.fori_loop(0, per, token_one, 0)

    lax.fori_loop(0, micro, token_batch, 0)

    load(patch_ref, patches, 0)
    load(fc1_ref, w_f1, 1)
    load(fc2_ref, w_f2, 2)
    load(gate_ref.at[0], w_gu.at[:, pl.ds(0, width)], 3)
    load(up_ref.at[0], w_gu.at[:, pl.ds(width, width)], 4)
    load(down_ref.at[0], w_dn, 5)
    load(tproj_ref, w_tp, 6)
    load(iproj_ref, w_ip, 7)

    tile_row = lax.broadcasted_iota(jnp.int32, (8, 128), 0)
    my_lens = jnp.ones((8, 128), F32)
    for i in range(micro):
        my_lens = jnp.where(tile_row == i, len_ref[i].astype(F32), my_lens)
    lens[nd - 1] = my_lens

    def dp_peers(body):
        def step(o, _):
            peer = lax.rem(dp + o, nd)
            body(peer, nd - 1 - o)
            return 0

        lax.fori_loop(1, nd, step, 0)

    def slot_of(source):
        return lax.rem(source - dp + 2 * nd - 1, nd)

    dp_peers(lambda peer, slot: send(lens.at[nd - 1], lens.at[slot], len_s, len_r, (sec, peer, mp)))

    loaded(patches, 0)
    loaded(w_f1, 1)
    rows = patches[0].astype(F32)
    scale = lax.rsqrt(jnp.mean(rows * rows, -1, keepdims=True) + 1e-05)
    vnormed = (rows * scale * vgain_ref[...]).astype(BF16)
    hidden = jnp.dot(vnormed, w_f1[...], preferred_element_type=F32)
    vinner = (0.5 * hidden * (1.0 + lax.erf(hidden * (0.5 ** 0.5)))).astype(BF16)
    vsum = jnp.sum(vinner.astype(F32), 0, keepdims=True)
    high = vsum.astype(BF16)
    low = (vsum - high.astype(F32)).astype(BF16)
    loaded(w_f2, 2)
    two = jnp.concatenate([jnp.broadcast_to(high, (8, high.shape[1])), jnp.broadcast_to(low, (8, low.shape[1]))], 0)
    prod = jnp.dot(two, w_f2[...], preferred_element_type=F32)
    part = prod[0:1] + prod[8:9] + jnp.where(mp == 0, 1.0, 0.0) * jnp.sum(rows, 0, keepdims=True)
    vtiles = part.shape[1] // 128
    for i in range(vtiles):
        im1_own[pl.ds(i, 1), :] = part[:, 128 * i:128 * (i + 1)]
    root = grp * lax.rem(dp + 1, nd)

    @pl.when(mp != root)
    def _():
        slot = lax.rem(mp - root - 1 + 2 * nm, nm)
        send(im1_own, im1.at[slot], im1_s, im1_r, (sec, dp, root))

    def image_root():
        @pl.when(mp == root)
        def _():
            drain(im1, im1_r)
            im2_own[...] = im1_own[...] + jnp.sum(im1[...], 0)

            def to_final(t, _):
                d, q = t // grp, lax.rem(t, grp)
                send(im2_own, im2.at[sec * nd + dp], im2_s, im2_r, (last, d, grp * d + q))
                return 0

            lax.fori_loop(0, nd * grp, to_final, 0)

    @pl.when(sec > 0)
    def _():
        image_root()

    loaded(w_gu.at[:, pl.ds(0, width)], 3)
    loaded(w_gu.at[:, pl.ds(width, width)], 4)
    gain = gain_ref[0:1, pl.ds(pl.multiple_of(dp * dl, dl), dl)]

    def chunk(d):
        return pl.ds(pl.multiple_of(d * length, length), length)

    def weights_of(c, b):
        count = lens[slot_of(c), pl.ds(b, 1), :][:, 0:1]
        at = lax.broadcasted_iota(jnp.int32, (length, 1), 0).astype(F32)
        return jnp.where(at < count, 1.0 / count, 0.0)

    def stage_a(b):
        drain(x_buf.at[b], xr.at[b])
        x = x_buf[b].astype(F32)
        total = jnp.sum(x * x, -1, keepdims=True)
        high = total.astype(BF16)
        low = (total - high.astype(F32)).astype(BF16)
        lane = lax.broadcasted_iota(jnp.int32, (batch, 128), 1)
        p_buf[b, :, pl.ds(2 * width, 128)] = jnp.where(
            lane < 64, high.astype(F32), low.astype(F32)).astype(BF16)
        xg_buf[...] = (x * gain).astype(BF16)
        block = 256 if (2 * width) % 256 == 0 else 128

        def columns(j, _):
            at = pl.ds(pl.multiple_of(j * block, block), block)
            p_buf[b, :, at] = jnp.dot(xg_buf[...], w_gu[:, at], preferred_element_type=F32).astype(BF16)
            return 0

        lax.fori_loop(0, 2 * width // block, columns, 0)
        dp_peers(lambda peer, slot: send(
            p_buf.at[b, chunk(peer)], r_buf.at[b, slot], ps.at[b], pr.at[b], (sec, peer, mp)))

    def stage_b(b):
        drain(r_buf.at[b], pr.at[b])
        total = p_buf[b, chunk(dp), :].astype(F32)
        for i in range(nd - 1):
            total = total + r_buf[b, i].astype(F32)
        squares = total[:, 2 * width:2 * width + 1] + total[:, 2 * width + 64:2 * width + 65]
        scale = lax.rsqrt(squares * (1.0 / dim) + 1e-05)
        gate = total[:, :width] * scale
        upper = total[:, width:2 * width] * scale
        inner = (gate * jax.nn.sigmoid(gate) * upper).astype(BF16)

        @pl.when(sec < last)
        def _():
            i_buf[b, chunk(dp), :] = inner
            here = i_buf.at[b, chunk(dp)]
            dp_peers(lambda peer, slot: send(here, here, iss.at[b], ir.at[b], (sec, peer, mp)))

        @pl.when(sec == last)
        def _():
            @pl.when(b == 0)
            def _():
                drain(lens.at[pl.ds(0, nd - 1)], len_r)
                pin[...] = jnp.zeros(pin.shape, F32)
                mean_h[...] = jnp.zeros(mean_h.shape, F32)

            pin[nd - 1, pl.ds(b, 1), :] = jnp.sum(inner.astype(F32) * weights_of(dp, b), 0, keepdims=True)

            @pl.when(is_final)
            def _():
                cols = pl.ds(pl.multiple_of(my_q * piece, piece), piece)
                for c in range(nd):
                    slab = x_buf[b, pl.ds(c * length, length), cols].astype(F32)
                    mean_h[c, pl.ds(b, 1), :] = jnp.sum(slab * weights_of(c, b), 0, keepdims=True)

    def mp_peers(body):
        def step(o, _):
            peer = lax.rem(mp + o, nm)
            body(peer, nm - 1 - o)
            return 0

        lax.fori_loop(1, nm, step, 0)

    def own(j):
        return pl.ds(pl.multiple_of(j * own_rows, own_rows), own_rows)

    def stage_c(b):
        drain(i_buf.at[b, pl.ds(0, batch - length)], ir.at[b])
        q_buf[b] = jnp.dot(i_buf[b], w_dn[...], preferred_element_type=F32).astype(BF16)
        mp_peers(lambda peer, slot: send(
            q_buf.at[b, own(peer)], s_buf.at[b, slot], qs.at[b], qr.at[b], (sec, dp, peer)))

    def stage_d(b):
        drain(s_buf.at[b], qr.at[b])
        total = x_buf[b, own(mp), :].astype(F32) + q_buf[b, own(mp), :].astype(F32)
        for i in range(nm - 1):
            total = total + s_buf[b, i].astype(F32)
        h_buf[b] = total.astype(BF16)

        def onward(o, _):
            send(h_buf.at[b], x_buf.at[b, own(mp)], hs.at[b], xr.at[b], (sec + 1, dp, lax.rem(mp + o, nm)))
            return 0

        lax.fori_loop(0, nm, onward, 0)

    def tick(i, _):
        @pl.when(jnp.logical_and(sec < last, i >= 3))
        def _():
            stage_d(i - 3)

        @pl.when(jnp.logical_and(sec < last, jnp.logical_and(i >= 2, i < micro + 2)))
        def _():
            @pl.when(i == 2)
            def _():
                loaded(w_dn, 5)

            stage_c(i - 2)

        @pl.when(jnp.logical_and(i >= 1, i < micro + 1))
        def _():
            stage_b(i - 1)

        @pl.when(i < micro)
        def _():
            stage_a(i)

        return 0

    lax.fori_loop(0, micro + 3, tick, 0)

    @pl.when(sec == 0)
    def _():
        image_root()

    loaded(w_tp, 6)
    loaded(w_ip, 7)

    @pl.when(sec == last)
    def _():
        loaded(w_dn, 5)
        dp_peers(lambda peer, slot: send(pin.at[nd - 1], pin.at[slot], pin_s, pin_r, (sec, peer, mp)))

        @pl.when(is_final)
        def _():
            drain(im2, im2_r)
            imrow[...] = jnp.zeros(imrow.shape, F32)
            for d in range(nd):
                image = im2[d]
                for s in range(1, ns):
                    image = image + im2[s * nd + d]
                for i in range(vtiles):
                    imrow[d:d + 1, 128 * i:128 * (i + 1)] = image[i:i + 1, :]

        drain(pin.at[pl.ds(0, nd - 1)], pin_r)
        pooled = jnp.concatenate([pin[slot_of(c)] for c in range(nd)], 0).astype(BF16)
        out = jnp.dot(pooled, w_dn[...], preferred_element_type=F32)
        for q in range(grp):
            pd[q] = out[:, q * piece:(q + 1) * piece]

        def to_final(q, _):
            target = grp * dp + q

            @pl.when(target != mp)
            def _():
                slot = lax.rem(mp - target - 1 + 2 * nm, nm)
                send(pd.at[q], pdr.at[slot], pd_s.at[q], pd_r, (sec, dp, target))
            return 0

        lax.fori_loop(0, grp, to_final, 0)

    def fan_target(t):
        s, y = t // nd, lax.rem(t, nd)
        target = y * grp + my_q
        return s, target, jnp.logical_and(s == last, target == mp)

    nf = nd * grp
    me_f = dp * grp + my_q

    @pl.when(is_final)
    def _():
        drain(pdr, pd_r)
        total = pd[my_q]
        for i in range(nm - 1):
            total = total + pdr[i]
        total = total + mean_h[...].reshape(nd * 8, piece)
        emb[...] = jnp.dot(total.astype(BF16), w_tp[...], preferred_element_type=F32)

        def to_others(o, _):
            f = lax.rem(me_f + o, nf)
            d, q = f // grp, lax.rem(f, grp)
            send(emb, embr.at[nf - 1 - o], e_s, e_r, (last, d, grp * d + q))
            return 0

        lax.fori_loop(1, nf, to_others, 0)
        pooled = (imrow[...] * (1.0 / (ns * patch_ref.shape[1]))).astype(BF16)
        image = jnp.dot(pooled, w_ip[...], preferred_element_type=F32)
        iu = image * lax.rsqrt(jnp.sum(image * image, -1, keepdims=True) + 1e-06)

        nrow = nd * 8
        row = lax.broadcasted_iota(jnp.int32, (nrow, 8), 0)
        col = lax.broadcasted_iota(jnp.int32, (nrow, 8), 1)
        gids = jnp.full((nrow, 8), -1, jnp.int32)
        for k in range(nd * micro):
            gids = jnp.where(row == 8 * (k // micro) + k % micro, gid_ref[k], gids)
        match = jnp.where(gids == col, 1.0, 0.0)
        real_row = lax.rem(row, 8) < micro
        real = jnp.where(jnp.logical_and(real_row, col < nd), 1.0, 0.0)

        drain(embr, e_r)
        total = emb[...]
        for i in range(nf - 1):
            total = total + embr[i]
        cu = total * lax.rsqrt(jnp.sum(total * total, -1, keepdims=True) + 1e-06)
        logits = jnp.zeros((nrow, 8), F32)
        for j in range(nd):
            logits = jnp.where(col == j, 10.0 * jnp.sum(cu * iu[j:j + 1], -1, keepdims=True), logits)
        expo = jnp.exp(logits) * real
        good = expo * match
        by_row = jnp.sum(expo, 1, keepdims=True)
        by_row = jnp.where(by_row > 0, by_row, 1.0)
        by_col = jnp.sum(expo, 0, keepdims=True)
        by_col = jnp.where(by_col > 0, by_col, 1.0)
        good_col = jnp.sum(good, 0, keepdims=True)
        good_col = jnp.where(good_col > 0, good_col, 1.0)
        forward = jnp.sum(jnp.log(by_row)) - jnp.sum(logits * match * real)
        backward = jnp.sum(jnp.log(by_col)) - jnp.sum(jnp.log(good_col))
        loss = 0.5 * (forward / (nd * micro) + backward / nd)
        slope = 5.0 * (expo / by_row - match * real + expo / by_col - good / good_col)
        gcap = jnp.zeros(cu.shape, F32)
        gimg = jnp.zeros((1, cu.shape[1]), F32)
        for j in range(nd):
            gcap = gcap + slope[:, j:j + 1] * iu[j:j + 1]
            gimg = gimg + jnp.where(dp == j, 1.0, 0.0) * jnp.sum(slope[:, j:j + 1] * cu, 0, keepdims=True)
        mine = jnp.zeros((8, cu.shape[1]), F32)
        for d in range(nd):
            mine = mine + jnp.where(dp == d, 1.0, 0.0) * gcap[8 * d:8 * d + 8]
        outb[0:8, :] = mine
        outb[8:16, :] = jnp.broadcast_to(gimg, (8, cu.shape[1]))
        outb[16:24, :] = jnp.full((8, cu.shape[1]), loss, F32)

        def fan(t, _):
            s, target, home = fan_target(t)

            @pl.when(jnp.logical_not(home))
            def _():
                send(outb, outb, out_s.at[t], out_r, (s, dp, target))
            return 0

        lax.fori_loop(0, ns * nd, fan, 0)

    @pl.when(jnp.logical_not(is_final))
    def _():
        drain(outb, out_r)

    loss_ref[...] = outb[16:17, 0:128]
    gcap_ref[...] = outb[0:micro, :]
    gimg_ref[...] = outb[8:9, :]

    def sent_tokens(k, _):
        _, home = token_target(k)

        @pl.when(jnp.logical_not(home))
        def _():
            drain(tok_ref, tok_ss.at[k])
        return 0

    lax.fori_loop(0, per, sent_tokens, 0)
    drain(lens.at[pl.ds(0, nd - 1)], len_s)

    @pl.when(sec < last)
    def _():
        drain(lens.at[pl.ds(0, nd - 1)], len_r)

    @pl.when(mp != root)
    def _():
        drain(im1_own, im1_s)

    @pl.when(mp == root)
    def _():
        drain(im2, im2_s)

    def sent_batch(b, _):
        drain(r_buf.at[b], ps.at[b])

        @pl.when(sec < last)
        def _():
            drain(i_buf.at[b, pl.ds(0, batch - length)], iss.at[b])
            drain(s_buf.at[b], qs.at[b])
            drain(x_buf.at[b], hs.at[b])
        return 0

    lax.fori_loop(0, micro, sent_batch, 0)

    @pl.when(sec == last)
    def _():
        drain(pin.at[pl.ds(0, nd - 1)], pin_s)

        def sent_pd(q, _):
            @pl.when(grp * dp + q != mp)
            def _():
                drain(pd.at[0], pd_s.at[q])
            return 0

        lax.fori_loop(0, grp, sent_pd, 0)

    @pl.when(is_final)
    def _():
        drain(embr, e_s)

        def sent_fan(t, _):
            _, _, home = fan_target(t)

            @pl.when(jnp.logical_not(home))
            def _():
                drain(outb, out_s.at[t])
            return 0

        lax.fori_loop(0, ns * nd, sent_fan, 0)


def per_device(
    sizes,
    caption_tokens, caption_lengths, group_ids, text_gain, text_gate, text_up, text_down,
    text_proj, image_patches, image_gain, image_fc1, image_fc2, image_proj,
):
    ns, nd, nm = sizes
    grp = nm // nd
    micro, length, piece = caption_tokens.shape
    batch = nd * length
    own_rows = batch // nm
    dl, width = text_gate.shape[1], text_gate.shape[2]
    dv, hv = image_fc1.shape
    embed = text_proj.shape[1]
    nf = nd * grp
    any_spec = pl.BlockSpec(memory_space=pl.ANY)
    vmem = pl.BlockSpec(memory_space=pltpu.VMEM)
    smem = pl.BlockSpec(memory_space=pltpu.SMEM)
    dma = pltpu.SemaphoreType.DMA
    loss, gcap, gimg = pl.pallas_call(
        functools.partial(kernel, sizes),
        out_shape=(
            jax.ShapeDtypeStruct((1, 128), F32),
            jax.ShapeDtypeStruct((micro, embed), F32),
            jax.ShapeDtypeStruct((1, embed), F32),
        ),
        in_specs=[any_spec, smem, smem, vmem, any_spec, any_spec, any_spec, any_spec,
                  any_spec, vmem, any_spec, any_spec, any_spec],
        out_specs=(vmem, vmem, vmem),
        scratch_shapes=[
            pltpu.VMEM((dl, 2 * width), BF16),
            pltpu.VMEM((width, dl), BF16),
            pltpu.VMEM((piece, embed), BF16),
            pltpu.VMEM((dv, hv), BF16),
            pltpu.VMEM((hv, dv), BF16),
            pltpu.VMEM((dv, embed), BF16),
            pltpu.VMEM(image_patches.shape, BF16),
            pltpu.VMEM((micro, batch, dl), BF16),
            pltpu.VMEM((batch, dl), BF16),
            pltpu.VMEM((micro, batch, 2 * width + 128), BF16),
            pltpu.VMEM((micro, nd - 1, length, 2 * width + 128), BF16),
            pltpu.VMEM((micro, batch, width), BF16),
            pltpu.VMEM((micro, batch, dl), BF16),
            pltpu.VMEM((micro, nm - 1, own_rows, dl), BF16),
            pltpu.VMEM((micro, own_rows, dl), BF16),
            pltpu.VMEM((nd, 8, 128), F32),
            pltpu.VMEM((nm - 1, dv // 128, 128), F32),
            pltpu.VMEM((dv // 128, 128), F32),
            pltpu.VMEM((ns * nd, dv // 128, 128), F32),
            pltpu.VMEM((dv // 128, 128), F32),
            pltpu.VMEM((8, dv), F32),
            pltpu.VMEM((nd, 8, piece), F32),
            pltpu.VMEM((nd, 8, width), F32),
            pltpu.VMEM((grp, nd * 8, piece), F32),
            pltpu.VMEM((nm - 1, nd * 8, piece), F32),
            pltpu.VMEM((nd * 8, embed), F32),
            pltpu.VMEM((nf - 1, nd * 8, embed), F32),
            pltpu.VMEM((24, embed), F32),
            dma((8,)), dma((nm // ns,)), dma((micro,)), dma((micro,)), dma((micro,)), dma((micro,)),
            dma((micro,)), dma((micro,)), dma((micro,)), dma((micro,)),
            dma, dma, dma, dma, dma, dma, dma, dma, dma((grp,)), dma, dma, dma, dma((ns * nd,)), dma,
        ],
        compiler_params=pltpu.CompilerParams(
            has_side_effects=True, vmem_limit_bytes=48 * 2 ** 20),
        name="towers",
    )(
        caption_tokens, caption_lengths, group_ids, text_gain, text_gate, text_up, text_down,
        text_proj, image_patches, image_gain.reshape(1, dv), image_fc1, image_fc2, image_proj,
    )
    return loss[0, 0], gcap, gimg


def solution(mesh):
    sizes = tuple(mesh.shape[axis] for axis in ("section", "dp", "mp"))
    return jax.shard_map(
        functools.partial(per_device, sizes),
        mesh=mesh,
        in_specs=(
            P("dp", None, "mp"),
            P("dp"),
            P(),
            P("section", None),
            P("section", "dp", "mp"),
            P("section", "dp", "mp"),
            P("section", "mp", "dp"),
            P("mp", None),
            P("dp", "section", None),
            P(),
            P(None, "mp"),
            P("mp", None),
            P(),
        ),
        out_specs=(P(), P("dp", None), P("dp", None)),
        check_vma=False,
    )
```

```python
import functools

import jax
import jax.numpy as jnp
from jax import lax
from jax.experimental import pallas as pl
from jax.experimental.pallas import tpu as pltpu
from jax.sharding import PartitionSpec as P

MESH = pl.DeviceIdType.MESH
PLANS = ((2, 256), (2, 320), (2, 384), (2, 512))
BF16 = jnp.bfloat16
F32 = jnp.float32


def kernel(
    sizes,
    tok_ref, len_ref, gid_ref, gain_ref, gate_ref, up_ref, down_ref, tproj_ref,
    patch_ref, vgain_ref, fc1_ref, fc2_ref, iproj_ref,
    loss_ref, gcap_ref, gimg_ref,
    w_gu, w_dn, w_tp, w_f1, w_f2, w_ip, patches,
    tok_buf, x_buf, xg_buf, p_buf, ra_buf, rb_buf, r_buf, i_buf, q_buf, t_buf, u_buf, s_buf, h_buf,
    im1, im1_own, im2, im2_own, imrow, mean_h,
    pin, pin_o, pd, pdr, emb, embr, outb,
    wsem, tok_ss, xz, xy, es, pa_s, pa_r, pb_s, pb_r, pc_s, pc_r, pd_s2, pd_r2,
    iss, ir, qs, qr, us, ur, hs,
    tok_r, cs, im1_s, im1_r, im2_s, im2_r, pin_s, pin_r, pd_s, pd_r, e_s, e_r, out_s, out_r,
):
    ns, nd, nm = sizes
    grp = nm // nd
    caps, slots, piece = tok_ref.shape
    ncap = nd * caps
    micro, batch, dl = x_buf.shape
    length = batch // nd
    strip = piece // 2
    width = gate_ref.shape[2]
    dim = dl * nd
    sec, dp, mp = lax.axis_index("section"), lax.axis_index("dp"), lax.axis_index("mp")
    last = ns - 1
    my_group = mp // grp
    my_q = lax.rem(mp, grp)
    is_final = jnp.logical_and(sec == last, my_group == dp)

    def send(src, dst, s_sem, r_sem, where):
        pltpu.make_async_remote_copy(
            src_ref=src, dst_ref=dst, send_sem=s_sem, recv_sem=r_sem,
            device_id=where, device_id_type=MESH,
        ).start()

    def drain(ref, sem):
        pltpu.make_async_copy(ref, ref, sem).wait()

    def load(src, dst, index):
        pltpu.make_async_copy(src, dst, wsem.at[index]).start()

    def loaded(dst, index):
        pltpu.make_async_copy(dst, dst, wsem.at[index]).wait()

    def chunk(d):
        return pl.ds(pl.multiple_of(d * length, length), length)

    rows_y = pl.ds(pl.multiple_of(my_group * length, length), length)
    cols_z = pl.ds(pl.multiple_of(my_q * piece, piece), piece)

    token_home = jnp.logical_and(sec == 0, jnp.logical_and(my_group == 0, dp == 0))
    token_src = tok_ref.at[:, :, pl.ds(pl.multiple_of(lax.rem(sec, 2) * strip, strip), strip)]

    @pl.when(token_home)
    def _():
        pltpu.make_async_copy(token_src, tok_buf.at[dp], tok_r).start()

    @pl.when(jnp.logical_not(token_home))
    def _():
        send(token_src, tok_buf.at[dp], tok_ss, tok_r, (0, my_group, sec * grp + my_q))

    load(gate_ref.at[0], w_gu.at[:, pl.ds(0, width)], 3)
    load(up_ref.at[0], w_gu.at[:, pl.ds(width, width)], 4)

    load(patch_ref, patches, 0)
    load(fc1_ref, w_f1, 1)
    load(fc2_ref, w_f2, 2)
    load(down_ref.at[0], w_dn, 5)
    load(tproj_ref, w_tp, 6)
    load(iproj_ref, w_ip, 7)

    counts = [len_ref[c] for c in range(ncap)]
    starts = [jnp.int32(0)]
    for c in range(ncap):
        starts.append(starts[-1] + counts[c])

    def dp_peers(body):
        def step(o, _):
            peer = lax.rem(dp + o, nd)
            body(peer, nd - 1 - o)
            return 0

        lax.fori_loop(1, nd, step, 0)

    root = grp * lax.rem(dp + 1, nd)
    vtiles = w_f2.shape[1] // 128

    def image_layer():
        loaded(patches, 0)
        loaded(w_f1, 1)
        rows = patches[0].astype(F32)
        scale = lax.rsqrt(jnp.mean(rows * rows, -1, keepdims=True) + 1e-05)
        vnormed = (rows * scale * vgain_ref[...]).astype(BF16)
        hidden = jnp.dot(vnormed, w_f1[...], preferred_element_type=F32)
        vinner = (0.5 * hidden * (1.0 + lax.erf(hidden * (0.5 ** 0.5)))).astype(BF16)
        vsum = jnp.sum(vinner.astype(F32), 0, keepdims=True)
        high = vsum.astype(BF16)
        low = (vsum - high.astype(F32)).astype(BF16)
        loaded(w_f2, 2)
        two = jnp.concatenate([jnp.broadcast_to(high, (8, high.shape[1])), jnp.broadcast_to(low, (8, low.shape[1]))], 0)
        prod = jnp.dot(two, w_f2[...], preferred_element_type=F32)
        part = prod[0:1] + prod[8:9] + jnp.where(mp == 0, 1.0, 0.0) * jnp.sum(rows, 0, keepdims=True)
        for i in range(vtiles):
            im1_own[pl.ds(i, 1), :] = part[:, 128 * i:128 * (i + 1)]

        @pl.when(mp != root)
        def _():
            slot = lax.rem(mp - root - 1 + 2 * nm, nm)
            send(im1_own, im1.at[slot], im1_s, im1_r, (sec, dp, root))

        @pl.when(mp == root)
        def _():
            drain(im1, im1_r)
            im2_own[...] = im1_own[...] + jnp.sum(im1[...], 0)

            def to_final(t, _):
                d, q = t // grp, lax.rem(t, grp)
                send(im2_own, im2.at[sec * nd + dp], im2_s, im2_r, (last, d, grp * d + q))
                return 0

            lax.fori_loop(0, nd * grp, to_final, 0)

    @pl.when(sec > 0)
    def _():
        image_layer()

    loaded(w_gu.at[:, pl.ds(0, width)], 3)
    loaded(w_gu.at[:, pl.ds(width, width)], 4)
    gain = gain_ref[0:1, pl.ds(pl.multiple_of(dp * dl, dl), dl)]

    def members(first, width):
        row = lax.broadcasted_iota(jnp.int32, (ncap, width), 0)
        token = lax.broadcasted_iota(jnp.int32, (ncap, width), 1) + first
        lo = jnp.zeros((ncap, width), jnp.int32)
        hi = jnp.zeros((ncap, width), jnp.int32)
        for c in range(ncap):
            lo = jnp.where(row == c, starts[c], lo)
            hi = jnp.where(row == c, starts[c + 1], hi)
        return jnp.where(jnp.logical_and(token >= lo, token < hi), 1.0, 0.0).astype(BF16)

    right, left, far = lax.rem(dp + 1, nd), lax.rem(dp + nd - 1, nd), lax.rem(dp + 2, nd)
    full = 2 * width + 128
    low_cols, high_cols = pl.ds(0, width), pl.ds(width, width + 128)

    def y_peers(body):
        for o in range(1, nd):
            y = lax.rem(my_group + o, nd)
            body(y, y * grp + my_q, nd - 1 - o)

    def z_peers(body):
        for o in range(1, grp):
            z = lax.rem(my_q + o, grp)
            body(z, my_group * grp + z, grp - 1 - o)

    half_rows = pl.ds(pl.multiple_of((my_group // 2) * (batch // 2), batch // 2), batch // 2)

    def strip_cols(z):
        return pl.ds(pl.multiple_of(z * piece + lax.rem(my_group, 2) * strip, strip), strip)

    def pack():
        pltpu.make_async_copy(tok_buf, tok_buf, tok_r).wait()
        lane = lax.broadcasted_iota(jnp.int32, (8, ncap * slots), 1)
        cap = lane // slots
        pos = jnp.full((8, ncap * slots), -1, jnp.int32)
        for c in range(ncap):
            at = lane - c * slots
            pos = jnp.where(jnp.logical_and(cap == c, at < counts[c]), starts[c] + at, pos)
        tokens = tok_buf[...].reshape(ncap * slots, strip)

        def one(b, _):
            row = lax.broadcasted_iota(jnp.int32, (batch // 2, ncap * slots), 0)
            row = row + (b * batch + (my_group // 2) * (batch // 2))
            picks = jnp.where(row == pos[0:1], 1.0, 0.0).astype(BF16)
            here = x_buf.at[b, half_rows, strip_cols(my_q)]
            x_buf[b, half_rows, strip_cols(my_q)] = jnp.dot(
                picks, tokens, preferred_element_type=F32).astype(BF16)
            z_peers(lambda z, peer, slot: send(here, here, cs.at[b], xz.at[b], (sec, dp, peer)))
            return 0

        lax.fori_loop(0, micro, one, 0)

    @pl.when(sec == 0)
    def _():
        pack()

    def stage_e(b):
        @pl.when(sec == 0)
        def _():
            drain(x_buf.at[b, pl.ds(0, batch // 2), pl.ds(0, (grp - 1) * strip)], xz.at[b])
            for z in range(grp):
                part = x_buf.at[b, half_rows, strip_cols(z)]
                y_peers(lambda y, peer, slot: send(part, part, es.at[b], xy.at[b], (sec, dp, peer)))

        @pl.when(sec > 0)
        def _():
            here = x_buf.at[b, rows_y]
            drain(here, xz.at[b])
            y_peers(lambda y, peer, slot: send(here, here, es.at[b], xy.at[b], (sec, dp, peer)))

    def stage_a(b):
        drain(x_buf.at[b, pl.ds(0, batch - length)], xy.at[b])
        x = x_buf[b].astype(F32)
        total = jnp.sum(x * x, -1, keepdims=True)
        high = total.astype(BF16)
        low = (total - high.astype(F32)).astype(BF16)
        lane = lax.broadcasted_iota(jnp.int32, (batch, 128), 1)
        p_buf[b, :, pl.ds(2 * width, 128)] = jnp.where(
            lane < 64, high.astype(F32), low.astype(F32)).astype(BF16)
        xg_buf[...] = (x * gain).astype(BF16)
        p_buf[b, :, pl.ds(0, 2 * width)] = jnp.dot(
            xg_buf[...], w_gu[...], preferred_element_type=F32).astype(BF16)
        send(p_buf.at[b, chunk(far), low_cols], ra_buf.at[b], pa_s.at[b], pa_r.at[b], (sec, right, mp))
        send(p_buf.at[b, chunk(far), high_cols], rb_buf.at[b], pb_s.at[b], pb_r.at[b], (sec, left, mp))

    def stage_a2(b):
        drain(ra_buf.at[b], pa_r.at[b])
        p_buf[b, chunk(right), low_cols] = (
            p_buf[b, chunk(right), low_cols].astype(F32) + ra_buf[b].astype(F32)).astype(BF16)
        send(p_buf.at[b, chunk(right)], r_buf.at[b, 0], pc_s.at[b], pc_r.at[b], (sec, right, mp))
        drain(rb_buf.at[b], pb_r.at[b])
        p_buf[b, chunk(left), high_cols] = (
            p_buf[b, chunk(left), high_cols].astype(F32) + rb_buf[b].astype(F32)).astype(BF16)
        send(p_buf.at[b, chunk(left)], r_buf.at[b, 1], pd_s2.at[b], pd_r2.at[b], (sec, left, mp))

    def stage_b(b):
        drain(r_buf.at[b, 0], pc_r.at[b])
        drain(r_buf.at[b, 1], pd_r2.at[b])
        total = p_buf[b, chunk(dp), :].astype(F32) + r_buf[b, 0].astype(F32) + r_buf[b, 1].astype(F32)
        squares = total[:, 2 * width:2 * width + 1] + total[:, 2 * width + 64:2 * width + 65]
        scale = lax.rsqrt(squares * (1.0 / dim) + 1e-05)
        gate = total[:, :width] * scale
        upper = total[:, width:2 * width] * scale
        inner = (gate * jax.nn.sigmoid(gate) * upper).astype(BF16)

        @pl.when(sec < last)
        def _():
            i_buf[b, chunk(dp), :] = inner
            here = i_buf.at[b, chunk(dp)]
            dp_peers(lambda peer, slot: send(here, here, iss.at[b], ir.at[b], (sec, peer, mp)))

        @pl.when(sec == last)
        def _():
            @pl.when(b == 0)
            def _():
                pin[...] = jnp.zeros(pin.shape, F32)
                mean_h[...] = jnp.zeros(mean_h.shape, F32)

            mine = members(b * batch + dp * length, length)
            pin[...] = pin[...] + jnp.dot(mine, inner, preferred_element_type=F32)

            @pl.when(is_final)
            def _():
                mean_h[...] = mean_h[...] + jnp.dot(
                    members(b * batch, batch), x_buf[b, :, cols_z], preferred_element_type=F32)

    def stage_c(b):
        drain(i_buf.at[b, pl.ds(0, batch - length)], ir.at[b])
        q_buf[b] = jnp.dot(i_buf[b], w_dn[...], preferred_element_type=F32).astype(BF16)
        y_peers(lambda y, peer, slot: send(
            q_buf.at[b, chunk(y)], t_buf.at[b, slot], qs.at[b], qr.at[b], (sec, dp, peer)))

    def stage_d1(b):
        drain(t_buf.at[b], qr.at[b])
        total = q_buf[b, rows_y, :].astype(F32)
        for i in range(nd - 1):
            total = total + t_buf[b, i].astype(F32)
        u_buf[b] = total.astype(BF16)
        z_peers(lambda z, peer, slot: send(
            u_buf.at[b, :, pl.ds(pl.multiple_of(z * piece, piece), piece)],
            s_buf.at[b, slot], us.at[b], ur.at[b], (sec, dp, peer)))

    def stage_d2(b):
        drain(s_buf.at[b], ur.at[b])
        total = x_buf[b, rows_y, cols_z].astype(F32) + u_buf[b, :, cols_z].astype(F32)
        for i in range(grp - 1):
            total = total + s_buf[b, i].astype(F32)
        h_buf[b] = total.astype(BF16)
        for z in range(grp):
            send(h_buf.at[b], x_buf.at[b, rows_y, cols_z], hs.at[b], xz.at[b],
                 (sec + 1, dp, my_group * grp + lax.rem(my_q + z, grp)))

    def tick(i, _):
        def at(stage, back, also=True):
            @pl.when(jnp.logical_and(also, jnp.logical_and(i >= back, i < micro + back)))
            def _():
                stage(i - back)

        inside = sec < last
        at(stage_d2, 2, inside)
        at(stage_b, 1)
        at(stage_e, 0)

        @pl.when(jnp.logical_and(inside, i == 1))
        def _():
            loaded(w_dn, 5)

        at(stage_c, 1, inside)
        at(stage_a, 0)
        at(stage_d1, 1, inside)
        at(stage_a2, 0)
        return 0

    lax.fori_loop(0, micro + 2, tick, 0)

    @pl.when(sec == 0)
    def _():
        image_layer()

    loaded(w_tp, 6)
    loaded(w_ip, 7)

    def shares():
        row = lax.broadcasted_iota(jnp.int32, (ncap, 1), 0)
        count = jnp.ones((ncap, 1), F32)
        for c in range(ncap):
            count = jnp.where(row == c, counts[c].astype(F32), count)
        return 1.0 / count

    @pl.when(sec == last)
    def _():
        loaded(w_dn, 5)
        pin_o[nd - 1] = (pin[...] * shares()).astype(BF16)
        dp_peers(lambda peer, slot: send(pin_o.at[nd - 1], pin_o.at[slot], pin_s, pin_r, (sec, peer, mp)))

        @pl.when(is_final)
        def _():
            drain(im2, im2_r)
            imrow[...] = jnp.zeros(imrow.shape, F32)
            for d in range(nd):
                image = im2[d]
                for s in range(1, ns):
                    image = image + im2[s * nd + d]
                for i in range(vtiles):
                    imrow[d:d + 1, 128 * i:128 * (i + 1)] = image[i:i + 1, :]

        drain(pin_o.at[pl.ds(0, nd - 1)], pin_r)
        pooled = pin_o[0].astype(F32)
        for i in range(1, nd):
            pooled = pooled + pin_o[i].astype(F32)
        out = jnp.dot(pooled.astype(BF16), w_dn[...], preferred_element_type=F32)
        for q in range(grp):
            pd[q] = out[:, q * piece:(q + 1) * piece]

        def to_final(q, _):
            target = grp * dp + q

            @pl.when(target != mp)
            def _():
                slot = lax.rem(mp - target - 1 + 2 * nm, nm)
                send(pd.at[q], pdr.at[slot], pd_s.at[q], pd_r, (sec, dp, target))
            return 0

        lax.fori_loop(0, grp, to_final, 0)

    def fan_target(t):
        s, y = t // nd, lax.rem(t, nd)
        target = y * grp + my_q
        return s, target, jnp.logical_and(s == last, target == mp)

    nf = nd * grp
    me_f = dp * grp + my_q

    @pl.when(is_final)
    def _():
        drain(pdr, pd_r)
        total = pd[my_q]
        for i in range(nm - 1):
            total = total + pdr[i]
        total = total + mean_h[...] * shares()
        emb[...] = jnp.dot(total.astype(BF16), w_tp[...], preferred_element_type=F32).astype(BF16)

        def to_others(o, _):
            f = lax.rem(me_f + o, nf)
            d, q = f // grp, lax.rem(f, grp)
            send(emb, embr.at[nf - 1 - o], e_s, e_r, (last, d, grp * d + q))
            return 0

        lax.fori_loop(1, nf, to_others, 0)
        pooled = (imrow[...] * (1.0 / (ns * patch_ref.shape[1]))).astype(BF16)
        image = jnp.dot(pooled, w_ip[...], preferred_element_type=F32)
        iu = image * lax.rsqrt(jnp.sum(image * image, -1, keepdims=True) + 1e-06)

        nrow = ncap
        row = lax.broadcasted_iota(jnp.int32, (nrow, 8), 0)
        col = lax.broadcasted_iota(jnp.int32, (nrow, 8), 1)
        gids = jnp.full((nrow, 8), -1, jnp.int32)
        for k in range(ncap):
            gids = jnp.where(row == k, gid_ref[k], gids)
        match = jnp.where(gids == col, 1.0, 0.0)
        real = jnp.where(col < nd, 1.0, 0.0)

        drain(embr, e_r)
        total = emb[...].astype(F32)
        for i in range(nf - 1):
            total = total + embr[i].astype(F32)
        cu = total * lax.rsqrt(jnp.sum(total * total, -1, keepdims=True) + 1e-06)
        logits = jnp.zeros((nrow, 8), F32)
        for j in range(nd):
            logits = jnp.where(col == j, 10.0 * jnp.sum(cu * iu[j:j + 1], -1, keepdims=True), logits)
        expo = jnp.exp(logits) * real
        good = expo * match
        by_row = jnp.sum(expo, 1, keepdims=True)
        by_row = jnp.where(by_row > 0, by_row, 1.0)
        by_col = jnp.sum(expo, 0, keepdims=True)
        by_col = jnp.where(by_col > 0, by_col, 1.0)
        good_col = jnp.sum(good, 0, keepdims=True)
        good_col = jnp.where(good_col > 0, good_col, 1.0)
        forward = jnp.sum(jnp.log(by_row)) - jnp.sum(logits * match * real)
        backward = jnp.sum(jnp.log(by_col)) - jnp.sum(jnp.log(good_col))
        loss = 0.5 * (forward / ncap + backward / nd)
        slope = 5.0 * (expo / by_row - match * real + expo / by_col - good / good_col)
        gcap = jnp.zeros(cu.shape, F32)
        gimg = jnp.zeros((1, cu.shape[1]), F32)
        for j in range(nd):
            gcap = gcap + slope[:, j:j + 1] * iu[j:j + 1]
            gimg = gimg + jnp.where(dp == j, 1.0, 0.0) * jnp.sum(slope[:, j:j + 1] * cu, 0, keepdims=True)
        mine = jnp.zeros((caps, cu.shape[1]), F32)
        for d in range(nd):
            mine = mine + jnp.where(dp == d, 1.0, 0.0) * gcap[caps * d:caps * d + caps]
        outb[0:caps, :] = mine
        outb[8:16, :] = jnp.broadcast_to(gimg, (8, cu.shape[1]))
        outb[16:24, :] = jnp.full((8, cu.shape[1]), loss, F32)

        def fan(t, _):
            s, target, home = fan_target(t)

            @pl.when(jnp.logical_not(home))
            def _():
                send(outb, outb, out_s.at[t], out_r, (s, dp, target))
            return 0

        lax.fori_loop(0, ns * nd, fan, 0)

    @pl.when(jnp.logical_not(is_final))
    def _():
        drain(outb, out_r)

    loss_ref[...] = outb[16:17, 0:128]
    gcap_ref[...] = outb[0:caps, :]
    gimg_ref[...] = outb[8:9, :]

    @pl.when(jnp.logical_not(token_home))
    def _():
        drain(tok_buf.at[0], tok_ss)

    @pl.when(mp != root)
    def _():
        drain(im1_own, im1_s)

    @pl.when(mp == root)
    def _():
        drain(im2, im2_s)

    def sent_batch(b, _):
        drain(x_buf.at[b, pl.ds(0, batch - length)], es.at[b])

        @pl.when(sec == 0)
        def _():
            drain(x_buf.at[b, pl.ds(0, batch // 2), pl.ds(0, (grp - 1) * strip)], cs.at[b])

        drain(ra_buf.at[b], pa_s.at[b])
        drain(rb_buf.at[b], pb_s.at[b])
        drain(r_buf.at[b, 0], pc_s.at[b])
        drain(r_buf.at[b, 1], pd_s2.at[b])

        @pl.when(sec < last)
        def _():
            drain(i_buf.at[b, pl.ds(0, batch - length)], iss.at[b])
            drain(t_buf.at[b], qs.at[b])
            drain(s_buf.at[b], us.at[b])
            drain(x_buf.at[b, rows_y], hs.at[b])
        return 0

    lax.fori_loop(0, micro, sent_batch, 0)

    @pl.when(sec == last)
    def _():
        drain(pin_o.at[pl.ds(0, nd - 1)], pin_s)

        def sent_pd(q, _):
            @pl.when(grp * dp + q != mp)
            def _():
                drain(pd.at[0], pd_s.at[q])
            return 0

        lax.fori_loop(0, grp, sent_pd, 0)

    @pl.when(is_final)
    def _():
        drain(embr, e_s)

        def sent_fan(t, _):
            _, _, home = fan_target(t)

            @pl.when(jnp.logical_not(home))
            def _():
                drain(outb, out_s.at[t])
            return 0

        lax.fori_loop(0, ns * nd, sent_fan, 0)


def per_device(
    sizes, plans,
    caption_tokens, caption_lengths, group_ids, text_gain, text_gate, text_up, text_down,
    text_proj, image_patches, image_gain, image_fc1, image_fc2, image_proj,
):
    all_lengths = lax.all_gather(caption_lengths, "dp", axis=0, tiled=True)
    counted = jnp.sum(all_lengths)
    room = [micro * batch for micro, batch in plans]
    which = sum((counted > r).astype(jnp.int32) for r in room[:-1])
    operands = (
        caption_tokens, all_lengths, group_ids, text_gain, text_gate, text_up, text_down,
        text_proj, image_patches, image_gain.reshape(1, -1), image_fc1, image_fc2, image_proj,
    )
    return lax.switch(which, [functools.partial(towers, sizes, plan) for plan in plans], *operands)


def towers(
    sizes, plan,
    caption_tokens, caption_lengths, group_ids, text_gain, text_gate, text_up, text_down,
    text_proj, image_patches, image_gain, image_fc1, image_fc2, image_proj,
):
    ns, nd, nm = sizes
    grp = nm // nd
    micro, batch = plan
    caps, slots, piece = caption_tokens.shape
    length = batch // nd
    ncap = nd * caps
    dl, width = text_gate.shape[1], text_gate.shape[2]
    dv, hv = image_fc1.shape
    embed = text_proj.shape[1]
    nf = nd * grp
    any_spec = pl.BlockSpec(memory_space=pl.ANY)
    vmem = pl.BlockSpec(memory_space=pltpu.VMEM)
    smem = pl.BlockSpec(memory_space=pltpu.SMEM)
    dma = pltpu.SemaphoreType.DMA
    loss, gcap, gimg = pl.pallas_call(
        functools.partial(kernel, sizes),
        out_shape=(
            jax.ShapeDtypeStruct((1, 128), F32),
            jax.ShapeDtypeStruct((caps, embed), F32),
            jax.ShapeDtypeStruct((1, embed), F32),
        ),
        in_specs=[any_spec, smem, smem, vmem, any_spec, any_spec, any_spec, any_spec,
                  any_spec, vmem, any_spec, any_spec, any_spec],
        out_specs=(vmem, vmem, vmem),
        scratch_shapes=[
            pltpu.VMEM((dl, 2 * width), BF16),
            pltpu.VMEM((width, dl), BF16),
            pltpu.VMEM((piece, embed), BF16),
            pltpu.VMEM((dv, hv), BF16),
            pltpu.VMEM((hv, dv), BF16),
            pltpu.VMEM((dv, embed), BF16),
            pltpu.VMEM(image_patches.shape, BF16),
            pltpu.VMEM((nd, caps, slots, piece // 2), BF16),
            pltpu.VMEM((micro, batch, dl), BF16),
            pltpu.VMEM((batch, dl), BF16),
            pltpu.VMEM((micro, batch, 2 * width + 128), BF16),
            pltpu.VMEM((micro, length, width), BF16),
            pltpu.VMEM((micro, length, width + 128), BF16),
            pltpu.VMEM((micro, 2, length, 2 * width + 128), BF16),
            pltpu.VMEM((micro, batch, width), BF16),
            pltpu.VMEM((micro, batch, dl), BF16),
            pltpu.VMEM((micro, nd - 1, length, dl), BF16),
            pltpu.VMEM((micro, length, dl), BF16),
            pltpu.VMEM((micro, grp - 1, length, piece), BF16),
            pltpu.VMEM((micro, length, piece), BF16),
            pltpu.VMEM((nm - 1, dv // 128, 128), F32),
            pltpu.VMEM((dv // 128, 128), F32),
            pltpu.VMEM((ns * nd, dv // 128, 128), F32),
            pltpu.VMEM((dv // 128, 128), F32),
            pltpu.VMEM((8, dv), F32),
            pltpu.VMEM((ncap, piece), F32),
            pltpu.VMEM((ncap, width), F32),
            pltpu.VMEM((nd, ncap, width), BF16),
            pltpu.VMEM((grp, ncap, piece), F32),
            pltpu.VMEM((nm - 1, ncap, piece), F32),
            pltpu.VMEM((ncap, embed), BF16),
            pltpu.VMEM((nf - 1, ncap, embed), BF16),
            pltpu.VMEM((24, embed), F32),
            dma((8,)), dma, *([dma((micro,))] * 18),
            dma, dma((micro,)), dma, dma, dma, dma, dma, dma, dma((grp,)), dma, dma, dma, dma((ns * nd,)), dma,
        ],
        compiler_params=pltpu.CompilerParams(
            has_side_effects=True, vmem_limit_bytes=60 * 2 ** 20),
        name=f"towers_{micro}_{batch}",
    )(
        caption_tokens, caption_lengths, group_ids, text_gain, text_gate, text_up, text_down,
        text_proj, image_patches, image_gain, image_fc1, image_fc2, image_proj,
    )
    return loss[0, 0], gcap, gimg


def solution(mesh):
    sizes = tuple(mesh.shape[axis] for axis in ("section", "dp", "mp"))
    return jax.shard_map(
        functools.partial(per_device, sizes, PLANS),
        mesh=mesh,
        in_specs=(
            P("dp", None, "mp"),
            P("dp"),
            P(),
            P("section", None),
            P("section", "dp", "mp"),
            P("section", "dp", "mp"),
            P("section", "mp", "dp"),
            P("mp", None),
            P("dp", "section", None),
            P(),
            P(None, "mp"),
            P("mp", None),
            P(),
        ),
        out_specs=(P(), P("dp", None), P("dp", None)),
        check_vma=False,
    )
```

```python
import functools

import jax
import jax.numpy as jnp
from jax import lax
from jax.experimental import pallas as pl
from jax.experimental.pallas import tpu as pltpu
from jax.sharding import PartitionSpec as P

MESH = pl.DeviceIdType.MESH
PLANS = ((3, 128), (4, 128), (3, 192), (5, 128), (4, 192), (4, 256))
BF16 = jnp.bfloat16
F32 = jnp.float32


def kernel(
    sizes,
    tok_ref, len_ref, gid_ref, gain_ref, gate_ref, up_ref, down_ref, tproj_ref,
    patch_ref, vgain_ref, fc1_ref, fc2_ref, iproj_ref,
    loss_ref, gcap_ref, gimg_ref,
    w_gu, w_dn, w_tp, w_f1, w_f2, w_ip, patches,
    tok_buf, x_buf, far_buf, p_buf, ra_buf, rb_buf, r_buf, i_buf, q_buf, s_buf, h_buf,
    im1, im1_own, im2, im2_own, imrow, mean_h,
    pin, pin_o, pd, pdr, emb, embr, outb,
    wsem, xr, pa_s, pa_r, pb_s, pb_r, pc_s, pc_r, pd_s2, pd_r2,
    iss, qs, qr, hs, ir,
    cs, im1_s, im1_r, im2_s, im2_r, pin_s, pin_r, pd_s, pd_r, e_s, e_r, out_s, out_r,
):
    ns, nd, nm = sizes
    grp = nm // nd
    _, caps, slots, strip = tok_ref.shape
    piece = 2 * strip
    ncap = nd * caps
    micro, batch, dl = x_buf.shape
    length = batch // nd
    width = gate_ref.shape[2]
    dim = dl * nd
    sec, dp, mp = lax.axis_index("section"), lax.axis_index("dp"), lax.axis_index("mp")
    last = ns - 1
    my_group = mp // grp
    my_q = lax.rem(mp, grp)
    is_final = jnp.logical_and(sec == last, my_group == dp)

    def send(src, dst, s_sem, r_sem, where):
        pltpu.make_async_remote_copy(
            src_ref=src, dst_ref=dst, send_sem=s_sem, recv_sem=r_sem,
            device_id=where, device_id_type=MESH,
        ).start()

    def drain(ref, sem):
        pltpu.make_async_copy(ref, ref, sem).wait()

    def load(src, dst, index):
        pltpu.make_async_copy(src, dst, wsem.at[index]).start()

    def loaded(dst, index):
        pltpu.make_async_copy(dst, dst, wsem.at[index]).wait()

    def chunk(d):
        return pl.ds(pl.multiple_of(d * length, length), length)

    rows_y = pl.ds(pl.multiple_of(my_group * length, length), length)
    cols_z = pl.ds(pl.multiple_of(my_q * piece, piece), piece)

    root = grp * lax.rem(dp + 1, nd)
    nf = nd * grp
    me_f = dp * grp + my_q
    final_mp = dp * grp + my_q
    barrier = pltpu.get_barrier_semaphore()

    def hello(where):
        pl.semaphore_signal(barrier, inc=1, device_id=where, device_id_type=MESH)

    def each(lo, hi, body):
        def step(o, _):
            body(o)
            return 0

        lax.fori_loop(lo, hi, step, 0)

    each(1, nd, lambda o: hello((sec, lax.rem(dp + o, nd), mp)))
    each(1, nm, lambda o: hello((sec, dp, lax.rem(mp + o, nm))))

    @pl.when(sec > 0)
    def _():
        each(0, nm, lambda o: hello((sec - 1, dp, lax.rem(mp + o, nm))))

    @pl.when(is_final)
    def _():
        each(0, ns * nd, lambda o: hello((o // nd, lax.rem(o, nd), grp * lax.rem(o + 1, nd))))

        def other_final(o):
            f = lax.rem(me_f + o, nf)
            hello((last, f // grp, f))

        each(1, nf, other_final)

    @pl.when(jnp.logical_not(is_final))
    def _():
        hello((last, dp, final_mp))

    @pl.when(sec == 0)
    def _():
        load(tok_ref, tok_buf, 0)

    load(gate_ref.at[0], w_gu.at[:, pl.ds(0, width)], 3)
    load(up_ref.at[0], w_gu.at[:, pl.ds(width, width)], 4)

    load(patch_ref, patches, 8)
    load(fc1_ref, w_f1, 1)
    load(fc2_ref, w_f2, 2)
    load(down_ref.at[0], w_dn, 5)
    load(tproj_ref, w_tp, 6)
    load(iproj_ref, w_ip, 7)
    partners = nd - 1 + nm - 1 + jnp.where(sec < last, nm, 0) + jnp.where(mp == root, nd * grp, 0)
    partners = partners + jnp.where(is_final, nf - 1 + ns * nd - 1, 0)
    pl.semaphore_wait(barrier, partners)

    counts = [len_ref[c // caps, c % caps:c % caps + 1, 0:1] for c in range(ncap)]
    starts = [jnp.zeros((1, 1), F32)]
    for c in range(ncap):
        starts.append(starts[-1] + counts[c])

    def dp_peers(body):
        def step(o, _):
            peer = lax.rem(dp + o, nd)
            body(peer, nd - 1 - o)
            return 0

        lax.fori_loop(1, nd, step, 0)

    vtiles = w_f2.shape[1] // 128

    def image_layer():
        loaded(patches, 8)
        loaded(w_f1, 1)
        rows = patches[0].astype(F32)
        scale = lax.rsqrt(jnp.mean(rows * rows, -1, keepdims=True) + 1e-05)
        vnormed = (rows * scale * vgain_ref[...]).astype(BF16)
        hidden = jnp.dot(vnormed, w_f1[...], preferred_element_type=F32)
        vinner = (0.5 * hidden * (1.0 + lax.erf(hidden * (0.5 ** 0.5)))).astype(BF16)
        vsum = jnp.sum(vinner.astype(F32), 0, keepdims=True)
        high = vsum.astype(BF16)
        low = (vsum - high.astype(F32)).astype(BF16)
        loaded(w_f2, 2)
        two = jnp.concatenate([jnp.broadcast_to(high, (8, high.shape[1])), jnp.broadcast_to(low, (8, low.shape[1]))], 0)
        prod = jnp.dot(two, w_f2[...], preferred_element_type=F32)
        part = prod[0:1] + prod[8:9] + jnp.where(mp == 0, 1.0, 0.0) * jnp.sum(rows, 0, keepdims=True)
        for i in range(vtiles):
            im1_own[pl.ds(i, 1), :] = part[:, 128 * i:128 * (i + 1)]

        @pl.when(mp != root)
        def _():
            slot = lax.rem(mp - root - 1 + 2 * nm, nm)
            send(im1_own, im1.at[slot], im1_s, im1_r, (sec, dp, root))

        @pl.when(mp == root)
        def _():
            drain(im1, im1_r)
            im2_own[...] = im1_own[...] + jnp.sum(im1[...], 0)

            def to_final(t, _):
                d, q = t // grp, lax.rem(t, grp)
                send(im2_own, im2.at[sec * nd + dp], im2_s, im2_r, (last, d, grp * d + q))
                return 0

            lax.fori_loop(0, nd * grp, to_final, 0)

    @pl.when(sec > 0)
    def _():
        image_layer()

    loaded(w_gu.at[:, pl.ds(0, width)], 3)
    loaded(w_gu.at[:, pl.ds(width, width)], 4)
    gain = gain_ref[0:1, pl.ds(pl.multiple_of(dp * dl, dl), dl)]

    def members(first, width):
        row = lax.broadcasted_iota(jnp.int32, (ncap, width), 0)
        token = (lax.broadcasted_iota(jnp.int32, (ncap, width), 1) + first).astype(F32)
        lo = jnp.zeros((ncap, width), F32)
        hi = jnp.zeros((ncap, width), F32)
        for c in range(ncap):
            lo = jnp.where(row == c, starts[c], lo)
            hi = jnp.where(row == c, starts[c + 1], hi)
        return jnp.where(jnp.logical_and(token >= lo, token < hi), 1.0, 0.0).astype(BF16)

    right, left, far = lax.rem(dp + 1, nd), lax.rem(dp + nd - 1, nd), lax.rem(dp + 2, nd)
    full = 2 * width + 128
    low_cols, high_cols = pl.ds(0, width), pl.ds(width, width + 128)

    def mp_peers(body):
        def step(o, _):
            peer = lax.rem(mp + o, nm)
            body(peer, nm - 1 - o)
            return 0

        lax.fori_loop(1, nm, step, 0)

    half_rows = pl.ds(pl.multiple_of((my_group // 2) * (batch // 2), batch // 2), batch // 2)

    strip_cols = pl.ds(pl.multiple_of(my_q * piece + lax.rem(my_group, 2) * strip, strip), strip)

    def pack():
        loaded(tok_buf, 0)
        lane = lax.broadcasted_iota(jnp.int32, (8, ncap * slots), 1)
        cap = lane // slots
        pos = jnp.full((8, ncap * slots), -1.0, F32)
        for c in range(ncap):
            at = (lane - c * slots).astype(F32)
            pos = jnp.where(jnp.logical_and(cap == c, at < counts[c]), starts[c] + at, pos)
        tokens = tok_buf[...].reshape(ncap * slots, strip)

        def one(b, _):
            row = lax.broadcasted_iota(jnp.int32, (batch // 2, ncap * slots), 0)
            row = (row + (b * batch + (my_group // 2) * (batch // 2))).astype(F32)
            picks = jnp.where(row == pos[0:1], 1.0, 0.0).astype(BF16)
            here = x_buf.at[b, half_rows, strip_cols]
            x_buf[b, half_rows, strip_cols] = jnp.dot(
                picks, tokens, preferred_element_type=F32).astype(BF16)
            mp_peers(lambda peer, slot: send(here, here, cs.at[b], xr.at[b], (sec, dp, peer)))
            return 0

        lax.fori_loop(0, micro, one, 0)

    @pl.when(sec == 0)
    def _():
        pack()

    def products(rows, out):
        x = rows.astype(F32)
        total = jnp.sum(x * x, -1, keepdims=True)
        high = total.astype(BF16).astype(F32)
        lane = lax.broadcasted_iota(jnp.int32, (x.shape[0], 128), 1)
        out[:, pl.ds(2 * width, 128)] = jnp.where(lane < 64, high, total - high).astype(BF16)
        out[:, pl.ds(0, 2 * width)] = jnp.dot(
            (x * gain).astype(BF16), w_gu[...], preferred_element_type=F32).astype(BF16)

    def stage_a(b):
        @pl.when(sec == 0)
        def _():
            drain(s_buf.at[b], xr.at[b])

        @pl.when(sec > 0)
        def _():
            drain(x_buf.at[b], xr.at[b])

        products(x_buf[b, chunk(far), :], far_buf.at[b])
        send(far_buf.at[b, :, low_cols], ra_buf.at[b], pa_s.at[b], pa_r.at[b], (sec, right, mp))
        send(far_buf.at[b, :, high_cols], rb_buf.at[b], pb_s.at[b], pb_r.at[b], (sec, left, mp))
        near = jnp.concatenate([x_buf[b, chunk(c), :] for c in (right, left, dp)], 0)
        products(near, p_buf.at[b])

    to_right, to_left, to_self = pl.ds(0, length), pl.ds(length, length), pl.ds(2 * length, length)

    def stage_a2(b):
        drain(ra_buf.at[b], pa_r.at[b])
        p_buf[b, to_right, low_cols] = (
            p_buf[b, to_right, low_cols].astype(F32) + ra_buf[b].astype(F32)).astype(BF16)
        send(p_buf.at[b, to_right], r_buf.at[b, 0], pc_s.at[b], pc_r.at[b], (sec, right, mp))
        drain(rb_buf.at[b], pb_r.at[b])
        p_buf[b, to_left, high_cols] = (
            p_buf[b, to_left, high_cols].astype(F32) + rb_buf[b].astype(F32)).astype(BF16)
        send(p_buf.at[b, to_left], r_buf.at[b, 1], pd_s2.at[b], pd_r2.at[b], (sec, left, mp))

    def stage_b(b):
        drain(r_buf.at[b, 0], pc_r.at[b])
        drain(r_buf.at[b, 1], pd_r2.at[b])
        total = p_buf[b, to_self, :].astype(F32) + r_buf[b, 0].astype(F32) + r_buf[b, 1].astype(F32)
        squares = total[:, 2 * width:2 * width + 1] + total[:, 2 * width + 64:2 * width + 65]
        scale = lax.rsqrt(squares * (1.0 / dim) + 1e-05)
        gate = total[:, :width] * scale
        upper = total[:, width:2 * width] * scale
        inner = (gate * jax.nn.sigmoid(gate) * upper).astype(BF16)

        @pl.when(sec < last)
        def _():
            i_buf[b, chunk(dp), :] = inner
            here = i_buf.at[b, chunk(dp)]
            for o in (1, nd - 1, 2):
                send(here, here, iss.at[b], ir.at[nd - 1 - o, b], (sec, lax.rem(dp + o, nd), mp))

        @pl.when(sec == last)
        def _():
            @pl.when(b == 0)
            def _():
                pin[...] = jnp.zeros(pin.shape, F32)
                mean_h[...] = jnp.zeros(mean_h.shape, F32)

            mine = members(b * batch + dp * length, length)
            pin[...] = pin[...] + jnp.dot(mine, inner, preferred_element_type=F32)

            @pl.when(is_final)
            def _():
                mean_h[...] = mean_h[...] + jnp.dot(
                    members(b * batch, batch), x_buf[b, :, cols_z], preferred_element_type=F32)

    def stage_c(b):
        def from_sources(offsets):
            sources = [lax.rem(dp + o, nd) for o in offsets]
            for o, source in zip(offsets, sources):
                if o:
                    drain(i_buf.at[b, chunk(source)], ir.at[o - 1, b])
            out = jnp.dot(jnp.concatenate([i_buf[b, chunk(c), :] for c in sources], 0), w_dn[...],
                          preferred_element_type=F32).astype(BF16)
            for at, source in enumerate(sources):
                q_buf[b, chunk(source), :] = out[at * length:(at + 1) * length]

                def to_owner(z, source=source):
                    owner = source * grp + z

                    @pl.when(owner != mp)
                    def _():
                        slot = lax.rem(mp - owner - 1 + 2 * nm, nm)
                        send(q_buf.at[b, chunk(source), pl.ds(pl.multiple_of(z * piece, piece), piece)],
                             s_buf.at[b, slot], qs.at[b], qr.at[b], (sec, dp, owner))

                each(0, grp, to_owner)

        from_sources((0, 1, nd - 1))
        from_sources((2,))

    def stage_d(b):
        drain(s_buf.at[b], qr.at[b])
        total = x_buf[b, rows_y, cols_z].astype(F32) + q_buf[b, rows_y, cols_z].astype(F32)
        for i in range(nm - 1):
            total = total + s_buf[b, i].astype(F32)
        h_buf[b] = total.astype(BF16)

        def onward(o, _):
            send(h_buf.at[b], x_buf.at[b, rows_y, cols_z], hs.at[b], xr.at[b],
                 (sec + 1, dp, lax.rem(mp + o, nm)))
            return 0

        lax.fori_loop(0, nm, onward, 0)

    def tick(i, _):
        def at(stage, back, also=True):
            @pl.when(jnp.logical_and(also, jnp.logical_and(i >= back, i < micro + back)))
            def _():
                stage(i - back)

        inside = sec < last
        at(stage_d, 2, inside)
        at(stage_b, 1)
        at(stage_a, 0)

        @pl.when(jnp.logical_and(inside, i == 1))
        def _():
            loaded(w_dn, 5)

        at(stage_c, 1, inside)
        at(stage_a2, 0)
        return 0

    lax.fori_loop(0, micro + 2, tick, 0)

    @pl.when(sec == 0)
    def _():
        image_layer()

    loaded(w_tp, 6)
    loaded(w_ip, 7)

    def shares():
        row = lax.broadcasted_iota(jnp.int32, (ncap, 1), 0)
        count = jnp.ones((ncap, 1), F32)
        for c in range(ncap):
            count = jnp.where(row == c, counts[c], count)
        return 1.0 / count

    @pl.when(sec == last)
    def _():
        loaded(w_dn, 5)
        pin_o[nd - 1] = (pin[...] * shares()).astype(BF16)
        dp_peers(lambda peer, slot: send(pin_o.at[nd - 1], pin_o.at[slot], pin_s, pin_r, (sec, peer, mp)))

        @pl.when(is_final)
        def _():
            drain(im2, im2_r)
            imrow[...] = jnp.zeros(imrow.shape, F32)
            for d in range(nd):
                image = im2[d]
                for s in range(1, ns):
                    image = image + im2[s * nd + d]
                for i in range(vtiles):
                    imrow[d:d + 1, 128 * i:128 * (i + 1)] = image[i:i + 1, :]

        drain(pin_o.at[pl.ds(0, nd - 1)], pin_r)
        pooled = pin_o[0].astype(F32)
        for i in range(1, nd):
            pooled = pooled + pin_o[i].astype(F32)
        out = jnp.dot(pooled.astype(BF16), w_dn[...], preferred_element_type=F32)
        for q in range(grp):
            pd[q] = out[:, q * piece:(q + 1) * piece]

        def to_final(q, _):
            target = grp * dp + q

            @pl.when(target != mp)
            def _():
                slot = lax.rem(mp - target - 1 + 2 * nm, nm)
                send(pd.at[q], pdr.at[slot], pd_s.at[q], pd_r, (sec, dp, target))
            return 0

        lax.fori_loop(0, grp, to_final, 0)

    def fan_target(t):
        s, y = t // nd, lax.rem(t, nd)
        target = y * grp + my_q
        return s, target, jnp.logical_and(s == last, target == mp)

    @pl.when(is_final)
    def _():
        drain(pdr, pd_r)
        total = pd[my_q]
        for i in range(nm - 1):
            total = total + pdr[i]
        total = total + mean_h[...] * shares()
        emb[...] = jnp.dot(total.astype(BF16), w_tp[...], preferred_element_type=F32).astype(BF16)

        def to_others(o, _):
            f = lax.rem(me_f + o, nf)
            d, q = f // grp, lax.rem(f, grp)
            send(emb, embr.at[nf - 1 - o], e_s, e_r, (last, d, grp * d + q))
            return 0

        lax.fori_loop(1, nf, to_others, 0)
        pooled = (imrow[...] * (1.0 / (ns * patch_ref.shape[1]))).astype(BF16)
        image = jnp.dot(pooled, w_ip[...], preferred_element_type=F32)
        iu = image * lax.rsqrt(jnp.sum(image * image, -1, keepdims=True) + 1e-06)

        nrow = ncap
        row = lax.broadcasted_iota(jnp.int32, (nrow, 8), 0)
        col = lax.broadcasted_iota(jnp.int32, (nrow, 8), 1)
        gids = jnp.full((nrow, 8), -1, jnp.int32)
        for k in range(ncap):
            gids = jnp.where(row == k, gid_ref[k], gids)
        match = jnp.where(gids == col, 1.0, 0.0)
        real = jnp.where(col < nd, 1.0, 0.0)

        drain(embr, e_r)
        total = emb[...].astype(F32)
        for i in range(nf - 1):
            total = total + embr[i].astype(F32)
        cu = total * lax.rsqrt(jnp.sum(total * total, -1, keepdims=True) + 1e-06)
        logits = jnp.zeros((nrow, 8), F32)
        for j in range(nd):
            logits = jnp.where(col == j, 10.0 * jnp.sum(cu * iu[j:j + 1], -1, keepdims=True), logits)
        expo = jnp.exp(logits) * real
        good = expo * match
        by_row = jnp.sum(expo, 1, keepdims=True)
        by_row = jnp.where(by_row > 0, by_row, 1.0)
        by_col = jnp.sum(expo, 0, keepdims=True)
        by_col = jnp.where(by_col > 0, by_col, 1.0)
        good_col = jnp.sum(good, 0, keepdims=True)
        good_col = jnp.where(good_col > 0, good_col, 1.0)
        forward = jnp.sum(jnp.log(by_row)) - jnp.sum(logits * match * real)
        backward = jnp.sum(jnp.log(by_col)) - jnp.sum(jnp.log(good_col))
        loss = 0.5 * (forward / ncap + backward / nd)
        slope = 5.0 * (expo / by_row - match * real + expo / by_col - good / good_col)
        gcap = jnp.zeros(cu.shape, F32)
        gimg = jnp.zeros((1, cu.shape[1]), F32)
        for j in range(nd):
            gcap = gcap + slope[:, j:j + 1] * iu[j:j + 1]
            gimg = gimg + jnp.where(dp == j, 1.0, 0.0) * jnp.sum(slope[:, j:j + 1] * cu, 0, keepdims=True)
        mine = jnp.zeros((caps, cu.shape[1]), F32)
        for d in range(nd):
            mine = mine + jnp.where(dp == d, 1.0, 0.0) * gcap[caps * d:caps * d + caps]
        outb[0:caps, :] = mine
        outb[caps:caps + 1, :] = gimg
        outb[caps + 1:8, :] = jnp.full((7 - caps, cu.shape[1]), loss, F32)

        def fan(t, _):
            s, target, home = fan_target(t)

            @pl.when(jnp.logical_not(home))
            def _():
                send(outb, outb, out_s.at[t], out_r, (s, dp, target))
            return 0

        lax.fori_loop(0, ns * nd, fan, 0)

    @pl.when(jnp.logical_not(is_final))
    def _():
        drain(outb, out_r)

    loss_ref[...] = outb[caps + 1:caps + 2, 0:128]
    gcap_ref[...] = outb[0:caps, :]
    gimg_ref[...] = outb[caps:caps + 1, :]

    @pl.when(mp != root)
    def _():
        drain(im1_own, im1_s)

    @pl.when(mp == root)
    def _():
        drain(im2, im2_s)

    def sent_batch(b, _):
        @pl.when(sec == 0)
        def _():
            drain(s_buf.at[b], cs.at[b])

        drain(ra_buf.at[b], pa_s.at[b])
        drain(rb_buf.at[b], pb_s.at[b])
        drain(r_buf.at[b, 0], pc_s.at[b])
        drain(r_buf.at[b, 1], pd_s2.at[b])

        @pl.when(sec < last)
        def _():
            drain(i_buf.at[b, pl.ds(0, batch - length)], iss.at[b])
            drain(s_buf.at[b], qs.at[b])
            drain(x_buf.at[b], hs.at[b])
        return 0

    lax.fori_loop(0, micro, sent_batch, 0)

    @pl.when(sec == last)
    def _():
        drain(pin_o.at[pl.ds(0, nd - 1)], pin_s)

        def sent_pd(q, _):
            @pl.when(grp * dp + q != mp)
            def _():
                drain(pd.at[0], pd_s.at[q])
            return 0

        lax.fori_loop(0, grp, sent_pd, 0)

    @pl.when(is_final)
    def _():
        drain(embr, e_s)

        def sent_fan(t, _):
            _, _, home = fan_target(t)

            @pl.when(jnp.logical_not(home))
            def _():
                drain(outb, out_s.at[t])
            return 0

        lax.fori_loop(0, ns * nd, sent_fan, 0)


def front_kernel(sizes, rooms, tok_ref, len_ref, strips_ref, lens_ref, which_ref, lens, len_s, len_r, tok_s, tok_r, home_s):
    ns, nd, nm = sizes
    grp = nm // nd
    caps, _, piece = tok_ref.shape
    strip = piece // 2
    sec, dp, mp = lax.axis_index("section"), lax.axis_index("dp"), lax.axis_index("mp")
    my_group, my_q = mp // grp, lax.rem(mp, grp)
    home = jnp.logical_and(sec == 0, jnp.logical_and(my_group == 0, dp == 0))
    want_sec = my_group
    barrier = pltpu.get_barrier_semaphore()

    def hello(where):
        pl.semaphore_signal(barrier, inc=1, device_id=where, device_id_type=MESH)

    for o in range(1, nd):
        hello((sec, lax.rem(dp + o, nd), mp))

    @pl.when(sec == 0)
    def _():
        for d in range(nd):
            @pl.when(jnp.logical_not(jnp.logical_and(want_sec == 0, jnp.logical_and(dp == 0, d == 0))))
            def _():
                hello((want_sec, d, dp * grp + my_q))

    row = lax.broadcasted_iota(jnp.int32, (8, 128), 0)
    mine = jnp.zeros((8, 128), F32)
    for i in range(caps):
        mine = jnp.where(row == i, len_ref[i].astype(F32), mine)
    lens[dp] = mine

    source = tok_ref.at[:, :, pl.ds(pl.multiple_of(lax.rem(sec, 2) * strip, strip), strip)]
    slab = strips_ref.at[dp]

    @pl.when(home)
    def _():
        pltpu.make_async_copy(source, slab, home_s).start()
        pl.semaphore_wait(barrier, nd - 1)

    @pl.when(jnp.logical_not(home))
    def _():
        pl.semaphore_wait(barrier, nd)

    for o in range(1, nd):
        pltpu.make_async_remote_copy(
            src_ref=lens.at[dp], dst_ref=lens.at[dp], send_sem=len_s.at[o - 1], recv_sem=len_r.at[nd - 1 - o],
            device_id=(sec, lax.rem(dp + o, nd), mp), device_id_type=MESH).start()

    @pl.when(jnp.logical_not(home))
    def _():
        pltpu.make_async_remote_copy(
            src_ref=source, dst_ref=slab, send_sem=tok_s, recv_sem=tok_r.at[dp],
            device_id=(0, my_group, sec * grp + my_q), device_id_type=MESH).start()

    for o in range(1, nd):
        other = lens.at[lax.rem(dp + o, nd)]
        pltpu.make_async_copy(other, other, len_r.at[o - 1]).wait()
    lens_ref[...] = lens[...]
    counted = jnp.sum(lens[:, :, 0:1])
    which = jnp.int32(0)
    for room in rooms[:-1]:
        which = which + (counted > room).astype(jnp.int32)
    which_ref[0, 0] = which

    @pl.when(sec == 0)
    def _():
        for d in range(nd):
            here = strips_ref.at[d]
            itself = jnp.logical_and(want_sec == 0, jnp.logical_and(dp == 0, d == 0))

            @pl.when(itself)
            def _():
                pltpu.make_async_copy(here, here, home_s).wait()

            @pl.when(jnp.logical_not(itself))
            def _():
                pltpu.make_async_copy(here, here, tok_r.at[d]).wait()

    for o in range(1, nd):
        pltpu.make_async_copy(lens.at[dp], lens.at[dp], len_s.at[o - 1]).wait()

    @pl.when(jnp.logical_not(home))
    def _():
        pltpu.make_async_copy(slab, slab, tok_s).wait()


def front(sizes, plans, tokens, lengths):
    nd = sizes[1]
    caps, slots, piece = tokens.shape
    dma = pltpu.SemaphoreType.DMA
    return pl.pallas_call(
        functools.partial(front_kernel, sizes, [micro * batch for micro, batch in plans]),
        out_shape=(
            jax.ShapeDtypeStruct((nd, caps, slots, piece // 2), BF16),
            jax.ShapeDtypeStruct((nd, 8, 128), F32),
            jax.ShapeDtypeStruct((1, 1), jnp.int32),
        ),
        in_specs=[pl.BlockSpec(memory_space=pl.ANY), pl.BlockSpec(memory_space=pltpu.SMEM)],
        out_specs=(pl.BlockSpec(memory_space=pl.ANY), pl.BlockSpec(memory_space=pltpu.VMEM),
                   pl.BlockSpec(memory_space=pltpu.SMEM)),
        scratch_shapes=[
            pltpu.VMEM((nd, 8, 128), F32),
            dma((nd - 1,)), dma((nd - 1,)), dma, dma((nd,)), dma,
        ],
        compiler_params=pltpu.CompilerParams(
            collective_id=1, has_side_effects=True, vmem_limit_bytes=60 * 2 ** 20),
        name="front",
    )(tokens, lengths)


def per_device(
    sizes, plans,
    caption_tokens, caption_lengths, group_ids, text_gain, text_gate, text_up, text_down,
    text_proj, image_patches, image_gain, image_fc1, image_fc2, image_proj,
):
    strips, lens, which = front(sizes, plans, caption_tokens, caption_lengths)
    operands = (
        strips, lens, group_ids, text_gain, text_gate, text_up, text_down,
        text_proj, image_patches, image_gain.reshape(1, -1), image_fc1, image_fc2, image_proj,
    )
    branches = [functools.partial(towers, sizes, plan, 2 + i) for i, plan in enumerate(plans)]
    return lax.switch(which[0, 0], branches, *operands)


def towers(
    sizes, plan, barrier_id,
    strips, caption_lengths, group_ids, text_gain, text_gate, text_up, text_down,
    text_proj, image_patches, image_gain, image_fc1, image_fc2, image_proj,
):
    ns, nd, nm = sizes
    grp = nm // nd
    micro, batch = plan
    _, caps, slots, strip = strips.shape
    piece = 2 * strip
    length = batch // nd
    ncap = nd * caps
    dl, width = text_gate.shape[1], text_gate.shape[2]
    dv, hv = image_fc1.shape
    embed = text_proj.shape[1]
    nf = nd * grp
    any_spec = pl.BlockSpec(memory_space=pl.ANY)
    vmem = pl.BlockSpec(memory_space=pltpu.VMEM)
    smem = pl.BlockSpec(memory_space=pltpu.SMEM)
    dma = pltpu.SemaphoreType.DMA
    loss, gcap, gimg = pl.pallas_call(
        functools.partial(kernel, sizes),
        out_shape=(
            jax.ShapeDtypeStruct((1, 128), F32),
            jax.ShapeDtypeStruct((caps, embed), F32),
            jax.ShapeDtypeStruct((1, embed), F32),
        ),
        in_specs=[any_spec, vmem, smem, vmem, any_spec, any_spec, any_spec, any_spec,
                  any_spec, vmem, any_spec, any_spec, any_spec],
        out_specs=(vmem, vmem, vmem),
        scratch_shapes=[
            pltpu.VMEM((dl, 2 * width), BF16),
            pltpu.VMEM((width, dl), BF16),
            pltpu.VMEM((piece, embed), BF16),
            pltpu.VMEM((dv, hv), BF16),
            pltpu.VMEM((hv, dv), BF16),
            pltpu.VMEM((dv, embed), BF16),
            pltpu.VMEM(image_patches.shape, BF16),
            pltpu.VMEM((nd, caps, slots, piece // 2), BF16),
            pltpu.VMEM((micro, batch, dl), BF16),
            pltpu.VMEM((micro, length, 2 * width + 128), BF16),
            pltpu.VMEM((micro, 3 * length, 2 * width + 128), BF16),
            pltpu.VMEM((micro, length, width), BF16),
            pltpu.VMEM((micro, length, width + 128), BF16),
            pltpu.VMEM((micro, 2, length, 2 * width + 128), BF16),
            pltpu.VMEM((micro, batch, width), BF16),
            pltpu.VMEM((micro, batch, dl), BF16),
            pltpu.VMEM((micro, nm - 1, length, piece), BF16),
            pltpu.VMEM((micro, length, piece), BF16),
            pltpu.VMEM((nm - 1, dv // 128, 128), F32),
            pltpu.VMEM((dv // 128, 128), F32),
            pltpu.VMEM((ns * nd, dv // 128, 128), F32),
            pltpu.VMEM((dv // 128, 128), F32),
            pltpu.VMEM((8, dv), F32),
            pltpu.VMEM((ncap, piece), F32),
            pltpu.VMEM((ncap, width), F32),
            pltpu.VMEM((nd, ncap, width), BF16),
            pltpu.VMEM((grp, ncap, piece), F32),
            pltpu.VMEM((nm - 1, ncap, piece), F32),
            pltpu.VMEM((ncap, embed), BF16),
            pltpu.VMEM((nf - 1, ncap, embed), BF16),
            pltpu.VMEM((8, embed), F32),
            dma((9,)), *([dma((micro,))] * 13), dma((nd - 1, micro)),
            dma((micro,)), dma, dma, dma, dma, dma, dma, dma((grp,)), dma, dma, dma, dma((ns * nd,)), dma,
        ],
        compiler_params=pltpu.CompilerParams(
            collective_id=barrier_id, has_side_effects=True, vmem_limit_bytes=60 * 2 ** 20),
        name=f"towers_{micro}_{batch}",
    )(
        strips, caption_lengths, group_ids, text_gain, text_gate, text_up, text_down,
        text_proj, image_patches, image_gain, image_fc1, image_fc2, image_proj,
    )
    return loss[0, 0], gcap, gimg


def solution(mesh):
    sizes = tuple(mesh.shape[axis] for axis in ("section", "dp", "mp"))
    return jax.shard_map(
        functools.partial(per_device, sizes, PLANS),
        mesh=mesh,
        in_specs=(
            P("dp", None, "mp"),
            P("dp"),
            P(),
            P("section", None),
            P("section", "dp", "mp"),
            P("section", "dp", "mp"),
            P("section", "mp", "dp"),
            P("mp", None),
            P("dp", "section", None),
            P(),
            P(None, "mp"),
            P("mp", None),
            P(),
        ),
        out_specs=(P(), P("dp", None), P("dp", None)),
        check_vma=False,
    )
```

```python
import functools

import jax
import jax.numpy as jnp
from jax import lax
from jax.experimental import pallas as pl
from jax.experimental.pallas import tpu as pltpu
from jax.sharding import PartitionSpec as P

MESH = pl.DeviceIdType.MESH
PLANS = ((3, 128), (4, 128), (3, 192), (5, 128), (4, 192), (4, 256))
BF16 = jnp.bfloat16
F32 = jnp.float32


def kernel(
    sizes,
    tok_ref, len_ref, gid_ref, gain_ref, gate_ref, up_ref, down_ref, tproj_ref,
    patch_ref, vgain_ref, fc1_ref, fc2_ref, iproj_ref,
    loss_ref, gcap_ref, gimg_ref,
    w_gu, w_dn, w_tp, w_f1, w_f2, w_ip, patches,
    tok_buf, pos_buf, x_buf, far_buf, p_buf, ra_buf, rb_buf, r_buf, i_buf, q_buf, s_buf, h_buf,
    im1, im1_own, im2, im2_own, imrow, mean_h,
    pin, pin_o, pd, pdr, emb, embr, outb,
    wsem, xr, pa_s, pa_r, pb_s, pb_r, pc_s, pc_r, pd_s2, pd_r2,
    iss, qs, qr, hs, ir,
    cs, im1_s, im1_r, im2_s, im2_r, pin_s, pin_r, pd_s, pd_r, e_s, e_r, out_s, out_r,
):
    ns, nd, nm = sizes
    grp = nm // nd
    _, caps, slots, strip = tok_ref.shape
    piece = 2 * strip
    ncap = nd * caps
    micro, batch, dl = x_buf.shape
    length = batch // nd
    width = gate_ref.shape[2]
    dim = dl * nd
    sec, dp, mp = lax.axis_index("section"), lax.axis_index("dp"), lax.axis_index("mp")
    last = ns - 1
    my_group = mp // grp
    my_q = lax.rem(mp, grp)
    is_final = jnp.logical_and(sec == last, my_group == dp)

    def send(src, dst, s_sem, r_sem, where):
        pltpu.make_async_remote_copy(
            src_ref=src, dst_ref=dst, send_sem=s_sem, recv_sem=r_sem,
            device_id=where, device_id_type=MESH,
        ).start()

    def drain(ref, sem):
        pltpu.make_async_copy(ref, ref, sem).wait()

    def load(src, dst, index):
        pltpu.make_async_copy(src, dst, wsem.at[index]).start()

    def loaded(dst, index):
        pltpu.make_async_copy(dst, dst, wsem.at[index]).wait()

    def chunk(d):
        return pl.ds(pl.multiple_of(d * length, length), length)

    rows_y = pl.ds(pl.multiple_of(my_group * length, length), length)
    cols_z = pl.ds(pl.multiple_of(my_q * piece, piece), piece)

    @pl.when(sec == 0)
    def _():
        load(tok_ref, tok_buf, 0)

    load(gate_ref.at[0], w_gu.at[:, pl.ds(0, width)], 3)
    load(up_ref.at[0], w_gu.at[:, pl.ds(width, width)], 4)
    load(patch_ref, patches, 8)
    load(fc1_ref, w_f1, 1)
    load(fc2_ref, w_f2, 2)
    load(down_ref.at[0], w_dn, 5)
    load(tproj_ref, w_tp, 6)
    load(iproj_ref, w_ip, 7)

    root = grp * lax.rem(dp + 1, nd)
    nf = nd * grp
    me_f = dp * grp + my_q
    final_mp = dp * grp + my_q
    barrier = pltpu.get_barrier_semaphore()

    def hello(where):
        pl.semaphore_signal(barrier, inc=1, device_id=where, device_id_type=MESH)

    def each(lo, hi, body):
        def step(o, _):
            body(o)
            return 0

        lax.fori_loop(lo, hi, step, 0)

    each(1, nd, lambda o: hello((sec, lax.rem(dp + o, nd), mp)))
    each(1, nm, lambda o: hello((sec, dp, lax.rem(mp + o, nm))))

    @pl.when(sec > 0)
    def _():
        each(0, nm, lambda o: hello((sec - 1, dp, lax.rem(mp + o, nm))))

    @pl.when(is_final)
    def _():
        each(0, ns * nd, lambda o: hello((o // nd, lax.rem(o, nd), grp * lax.rem(o + 1, nd))))

        def other_final(o):
            f = lax.rem(me_f + o, nf)
            hello((last, f // grp, f))

        each(1, nf, other_final)

    @pl.when(jnp.logical_not(is_final))
    def _():
        hello((last, dp, final_mp))

    partners = nd - 1 + nm - 1 + jnp.where(sec < last, nm, 0) + jnp.where(mp == root, nd * grp, 0)
    partners = partners + jnp.where(is_final, nf - 1 + ns * nd - 1, 0)
    pl.semaphore_wait(barrier, partners)

    counts = [len_ref[c // caps, c % caps:c % caps + 1, 0:1] for c in range(ncap)]
    starts = [jnp.zeros((1, 1), F32)]
    for c in range(ncap):
        starts.append(starts[-1] + counts[c])

    def dp_peers(body):
        def step(o, _):
            peer = lax.rem(dp + o, nd)
            body(peer, nd - 1 - o)
            return 0

        lax.fori_loop(1, nd, step, 0)

    vtiles = w_f2.shape[1] // 128

    def image_layer():
        loaded(patches, 8)
        loaded(w_f1, 1)
        rows = patches[0].astype(F32)
        scale = lax.rsqrt(jnp.mean(rows * rows, -1, keepdims=True) + 1e-05)
        vnormed = (rows * scale * vgain_ref[...]).astype(BF16)
        hidden = jnp.dot(vnormed, w_f1[...], preferred_element_type=F32)
        vinner = (0.5 * hidden * (1.0 + lax.erf(hidden * (0.5 ** 0.5)))).astype(BF16)
        vsum = jnp.sum(vinner.astype(F32), 0, keepdims=True)
        high = vsum.astype(BF16)
        low = (vsum - high.astype(F32)).astype(BF16)
        loaded(w_f2, 2)
        two = jnp.concatenate([jnp.broadcast_to(high, (8, high.shape[1])), jnp.broadcast_to(low, (8, low.shape[1]))], 0)
        prod = jnp.dot(two, w_f2[...], preferred_element_type=F32)
        part = prod[0:1] + prod[8:9] + jnp.where(mp == 0, 1.0, 0.0) * jnp.sum(rows, 0, keepdims=True)
        for i in range(vtiles):
            im1_own[pl.ds(i, 1), :] = part[:, 128 * i:128 * (i + 1)]

        @pl.when(mp != root)
        def _():
            slot = lax.rem(mp - root - 1 + 2 * nm, nm)
            send(im1_own, im1.at[slot], im1_s, im1_r, (sec, dp, root))

        @pl.when(mp == root)
        def _():
            drain(im1, im1_r)
            im2_own[...] = im1_own[...] + jnp.sum(im1[...], 0)

            def to_final(t, _):
                d, q = t // grp, lax.rem(t, grp)
                send(im2_own, im2.at[sec * nd + dp], im2_s, im2_r, (last, d, grp * d + q))
                return 0

            lax.fori_loop(0, nd * grp, to_final, 0)

    @pl.when(sec > 0)
    def _():
        image_layer()

    loaded(w_gu.at[:, pl.ds(0, width)], 3)
    loaded(w_gu.at[:, pl.ds(width, width)], 4)
    gain = gain_ref[0:1, pl.ds(pl.multiple_of(dp * dl, dl), dl)]

    def members(first, width):
        row = lax.broadcasted_iota(jnp.int32, (ncap, width), 0)
        token = (lax.broadcasted_iota(jnp.int32, (ncap, width), 1) + first).astype(F32)
        lo = jnp.zeros((ncap, width), F32)
        hi = jnp.zeros((ncap, width), F32)
        for c in range(ncap):
            lo = jnp.where(row == c, starts[c], lo)
            hi = jnp.where(row == c, starts[c + 1], hi)
        return jnp.where(jnp.logical_and(token >= lo, token < hi), 1.0, 0.0).astype(BF16)

    right, left, far = lax.rem(dp + 1, nd), lax.rem(dp + nd - 1, nd), lax.rem(dp + 2, nd)
    full = 2 * width + 128
    low_cols, high_cols = pl.ds(0, width), pl.ds(width, width + 128)

    def ranked(t):
        y, z = lax.rem(my_group + t // grp + 2, nd), lax.rem(my_q + t + grp // 2, grp)
        return y * grp + z

    def mp_peers(body):
        def one(t):
            peer = ranked(t)

            @pl.when(peer != mp)
            def _():
                body(peer, lax.rem(mp - peer - 1 + 2 * nm, nm))

        each(0, nm, one)

    half_rows = pl.ds(pl.multiple_of((my_group // 2) * (batch // 2), batch // 2), batch // 2)

    strip_cols = pl.ds(pl.multiple_of(my_q * piece + lax.rem(my_group, 2) * strip, strip), strip)

    def positions():
        loaded(tok_buf, 0)
        lane = lax.broadcasted_iota(jnp.int32, (8, ncap * slots), 1)
        cap = lane // slots
        pos = jnp.full((8, ncap * slots), -1.0, F32)
        for c in range(ncap):
            at = (lane - c * slots).astype(F32)
            pos = jnp.where(jnp.logical_and(cap == c, at < counts[c]), starts[c] + at, pos)
        pos_buf[...] = pos

    def pack(b):
        row = lax.broadcasted_iota(jnp.int32, (batch // 2, ncap * slots), 0)
        row = (row + (b * batch + (my_group // 2) * (batch // 2))).astype(F32)
        picks = jnp.where(row == pos_buf[0:1], 1.0, 0.0).astype(BF16)
        tokens = tok_buf[...].reshape(ncap * slots, strip)
        here = x_buf.at[b, half_rows, strip_cols]
        x_buf[b, half_rows, strip_cols] = jnp.dot(picks, tokens, preferred_element_type=F32).astype(BF16)
        mp_peers(lambda peer, slot: send(here, here, cs.at[b], xr.at[b], (sec, dp, peer)))

    @pl.when(sec == 0)
    def _():
        positions()
        each(0, min(2, micro), pack)

    def products(rows, out):
        x = rows.astype(F32)
        total = jnp.sum(x * x, -1, keepdims=True)
        high = total.astype(BF16).astype(F32)
        lane = lax.broadcasted_iota(jnp.int32, (x.shape[0], 128), 1)
        out[:, pl.ds(2 * width, 128)] = jnp.where(lane < 64, high, total - high).astype(BF16)
        out[:, pl.ds(0, 2 * width)] = jnp.dot(
            (x * gain).astype(BF16), w_gu[...], preferred_element_type=F32).astype(BF16)

    def stage_a(b):
        @pl.when(sec == 0)
        def _():
            drain(s_buf.at[b], xr.at[b])

        @pl.when(sec > 0)
        def _():
            drain(x_buf.at[b], xr.at[b])

        products(x_buf[b, chunk(far), :], far_buf.at[b])
        send(far_buf.at[b, :, low_cols], ra_buf.at[b], pa_s.at[b], pa_r.at[b], (sec, right, mp))
        send(far_buf.at[b, :, high_cols], rb_buf.at[b], pb_s.at[b], pb_r.at[b], (sec, left, mp))
        near = jnp.concatenate([x_buf[b, chunk(c), :] for c in (right, left, dp)], 0)
        products(near, p_buf.at[b])

    to_right, to_left, to_self = pl.ds(0, length), pl.ds(length, length), pl.ds(2 * length, length)

    def stage_a2(b):
        drain(ra_buf.at[b], pa_r.at[b])
        p_buf[b, to_right, low_cols] = (
            p_buf[b, to_right, low_cols].astype(F32) + ra_buf[b].astype(F32)).astype(BF16)
        send(p_buf.at[b, to_right], r_buf.at[b, 0], pc_s.at[b], pc_r.at[b], (sec, right, mp))
        drain(rb_buf.at[b], pb_r.at[b])
        p_buf[b, to_left, high_cols] = (
            p_buf[b, to_left, high_cols].astype(F32) + rb_buf[b].astype(F32)).astype(BF16)
        send(p_buf.at[b, to_left], r_buf.at[b, 1], pd_s2.at[b], pd_r2.at[b], (sec, left, mp))

    def stage_b(b):
        drain(r_buf.at[b, 0], pc_r.at[b])
        drain(r_buf.at[b, 1], pd_r2.at[b])
        total = p_buf[b, to_self, :].astype(F32) + r_buf[b, 0].astype(F32) + r_buf[b, 1].astype(F32)
        squares = total[:, 2 * width:2 * width + 1] + total[:, 2 * width + 64:2 * width + 65]
        scale = lax.rsqrt(squares * (1.0 / dim) + 1e-05)
        gate = total[:, :width] * scale
        upper = total[:, width:2 * width] * scale
        inner = (gate * jax.nn.sigmoid(gate) * upper).astype(BF16)

        @pl.when(sec < last)
        def _():
            i_buf[b, chunk(dp), :] = inner
            here = i_buf.at[b, chunk(dp)]
            for o in (1, nd - 1, 2):
                send(here, here, iss.at[b], ir.at[nd - 1 - o, b], (sec, lax.rem(dp + o, nd), mp))

        @pl.when(sec == last)
        def _():
            @pl.when(b == 0)
            def _():
                pin[...] = jnp.zeros(pin.shape, F32)
                mean_h[...] = jnp.zeros(mean_h.shape, F32)

            mine = members(b * batch + dp * length, length)
            pin[...] = pin[...] + jnp.dot(mine, inner, preferred_element_type=F32)

            @pl.when(is_final)
            def _():
                mean_h[...] = mean_h[...] + jnp.dot(
                    members(b * batch, batch), x_buf[b, :, cols_z], preferred_element_type=F32)

    def stage_c(b):
        def from_sources(offsets):
            sources = [lax.rem(dp + o, nd) for o in offsets]
            for o, source in zip(offsets, sources):
                if o:
                    drain(i_buf.at[b, chunk(source)], ir.at[o - 1, b])
            out = jnp.dot(jnp.concatenate([i_buf[b, chunk(c), :] for c in sources], 0), w_dn[...],
                          preferred_element_type=F32).astype(BF16)
            for at, source in enumerate(sources):
                q_buf[b, chunk(source), :] = out[at * length:(at + 1) * length]

                def to_owner(o, source=source):
                    z = lax.rem(my_q + o + grp // 2, grp)
                    owner = source * grp + z

                    @pl.when(owner != mp)
                    def _():
                        slot = lax.rem(mp - owner - 1 + 2 * nm, nm)
                        send(q_buf.at[b, chunk(source), pl.ds(pl.multiple_of(z * piece, piece), piece)],
                             s_buf.at[b, slot], qs.at[b], qr.at[b], (sec, dp, owner))

                each(0, grp, to_owner)

        from_sources((0, 1, nd - 1))
        from_sources((2,))

    def stage_d(b):
        drain(s_buf.at[b], qr.at[b])
        total = x_buf[b, rows_y, cols_z].astype(F32) + q_buf[b, rows_y, cols_z].astype(F32)
        for i in range(nm - 1):
            total = total + s_buf[b, i].astype(F32)
        h_buf[b] = total.astype(BF16)

        each(0, nm, lambda t: send(
            h_buf.at[b], x_buf.at[b, rows_y, cols_z], hs.at[b], xr.at[b], (sec + 1, dp, ranked(t))))

    def tick(i, _):
        def at(stage, back, also=True):
            @pl.when(jnp.logical_and(also, jnp.logical_and(i >= back, i < micro + back)))
            def _():
                stage(i - back)

        inside = sec < last
        at(stage_d, 2, inside)
        at(stage_b, 1)
        at(stage_a, 0)

        @pl.when(jnp.logical_and(inside, i == 1))
        def _():
            loaded(w_dn, 5)

        @pl.when(jnp.logical_and(sec == 0, i + 2 < micro))
        def _():
            pack(i + 2)

        at(stage_c, 1, inside)
        at(stage_a2, 0)
        return 0

    lax.fori_loop(0, micro + 2, tick, 0)

    @pl.when(sec == 0)
    def _():
        image_layer()

    loaded(w_tp, 6)
    loaded(w_ip, 7)

    def shares():
        row = lax.broadcasted_iota(jnp.int32, (ncap, 1), 0)
        count = jnp.ones((ncap, 1), F32)
        for c in range(ncap):
            count = jnp.where(row == c, counts[c], count)
        return 1.0 / count

    @pl.when(sec == last)
    def _():
        loaded(w_dn, 5)
        pin_o[nd - 1] = (pin[...] * shares()).astype(BF16)
        dp_peers(lambda peer, slot: send(pin_o.at[nd - 1], pin_o.at[slot], pin_s, pin_r, (sec, peer, mp)))

        @pl.when(is_final)
        def _():
            drain(im2, im2_r)
            imrow[...] = jnp.zeros(imrow.shape, F32)
            for d in range(nd):
                image = im2[d]
                for s in range(1, ns):
                    image = image + im2[s * nd + d]
                for i in range(vtiles):
                    imrow[d:d + 1, 128 * i:128 * (i + 1)] = image[i:i + 1, :]

        drain(pin_o.at[pl.ds(0, nd - 1)], pin_r)
        pooled = pin_o[0].astype(F32)
        for i in range(1, nd):
            pooled = pooled + pin_o[i].astype(F32)
        out = jnp.dot(pooled.astype(BF16), w_dn[...], preferred_element_type=F32)
        for q in range(grp):
            pd[q] = out[:, q * piece:(q + 1) * piece]

        def to_final(q, _):
            target = grp * dp + q

            @pl.when(target != mp)
            def _():
                slot = lax.rem(mp - target - 1 + 2 * nm, nm)
                send(pd.at[q], pdr.at[slot], pd_s.at[q], pd_r, (sec, dp, target))
            return 0

        lax.fori_loop(0, grp, to_final, 0)

    def fan_target(t):
        s, y = t // nd, lax.rem(t, nd)
        target = y * grp + my_q
        return s, target, jnp.logical_and(s == last, target == mp)

    @pl.when(is_final)
    def _():
        drain(pdr, pd_r)
        total = pd[my_q]
        for i in range(nm - 1):
            total = total + pdr[i]
        total = total + mean_h[...] * shares()
        emb[...] = jnp.dot(total.astype(BF16), w_tp[...], preferred_element_type=F32).astype(BF16)

        def to_others(o, _):
            f = lax.rem(me_f + o, nf)
            d, q = f // grp, lax.rem(f, grp)
            send(emb, embr.at[nf - 1 - o], e_s, e_r, (last, d, grp * d + q))
            return 0

        lax.fori_loop(1, nf, to_others, 0)
        pooled = (imrow[...] * (1.0 / (ns * patch_ref.shape[1]))).astype(BF16)
        image = jnp.dot(pooled, w_ip[...], preferred_element_type=F32)
        iu = image * lax.rsqrt(jnp.sum(image * image, -1, keepdims=True) + 1e-06)

        nrow = ncap
        row = lax.broadcasted_iota(jnp.int32, (nrow, 8), 0)
        col = lax.broadcasted_iota(jnp.int32, (nrow, 8), 1)
        gids = jnp.full((nrow, 8), -1, jnp.int32)
        for k in range(ncap):
            gids = jnp.where(row == k, gid_ref[k], gids)
        match = jnp.where(gids == col, 1.0, 0.0)
        real = jnp.where(col < nd, 1.0, 0.0)

        drain(embr, e_r)
        total = emb[...].astype(F32)
        for i in range(nf - 1):
            total = total + embr[i].astype(F32)
        cu = total * lax.rsqrt(jnp.sum(total * total, -1, keepdims=True) + 1e-06)
        logits = jnp.zeros((nrow, 8), F32)
        for j in range(nd):
            logits = jnp.where(col == j, 10.0 * jnp.sum(cu * iu[j:j + 1], -1, keepdims=True), logits)
        expo = jnp.exp(logits) * real
        good = expo * match
        by_row = jnp.sum(expo, 1, keepdims=True)
        by_row = jnp.where(by_row > 0, by_row, 1.0)
        by_col = jnp.sum(expo, 0, keepdims=True)
        by_col = jnp.where(by_col > 0, by_col, 1.0)
        good_col = jnp.sum(good, 0, keepdims=True)
        good_col = jnp.where(good_col > 0, good_col, 1.0)
        def whole(array):
            return jnp.sum(jnp.sum(array, 0, keepdims=True), 1, keepdims=True)

        forward = whole(jnp.log(by_row)) - whole(logits * match * real)
        backward = whole(jnp.log(by_col) - jnp.log(good_col))
        loss = 0.5 * (forward / ncap + backward / nd)
        slope = 5.0 * (expo / by_row - match * real + expo / by_col - good / good_col)
        gcap = jnp.zeros(cu.shape, F32)
        gimg = jnp.zeros((1, cu.shape[1]), F32)
        for j in range(nd):
            gcap = gcap + slope[:, j:j + 1] * iu[j:j + 1]
            gimg = gimg + jnp.where(dp == j, 1.0, 0.0) * jnp.sum(slope[:, j:j + 1] * cu, 0, keepdims=True)
        mine = jnp.zeros((caps, cu.shape[1]), F32)
        for d in range(nd):
            mine = mine + jnp.where(dp == d, 1.0, 0.0) * gcap[caps * d:caps * d + caps]
        outb[0:caps, :] = mine
        outb[caps:caps + 1, :] = gimg
        outb[caps + 1:8, :] = jnp.broadcast_to(loss, (7 - caps, cu.shape[1]))

        def fan(t, _):
            s, target, home = fan_target(t)

            @pl.when(jnp.logical_not(home))
            def _():
                send(outb, outb, out_s.at[t], out_r, (s, dp, target))
            return 0

        lax.fori_loop(0, ns * nd, fan, 0)

    @pl.when(jnp.logical_not(is_final))
    def _():
        drain(outb, out_r)

    loss_ref[...] = outb[caps + 1:caps + 2, 0:128]
    gcap_ref[...] = outb[0:caps, :]
    gimg_ref[...] = outb[caps:caps + 1, :]

    @pl.when(mp != root)
    def _():
        drain(im1_own, im1_s)

    @pl.when(mp == root)
    def _():
        drain(im2, im2_s)

    def sent_batch(b, _):
        @pl.when(sec == 0)
        def _():
            drain(s_buf.at[b], cs.at[b])

        drain(ra_buf.at[b], pa_s.at[b])
        drain(rb_buf.at[b], pb_s.at[b])
        drain(r_buf.at[b, 0], pc_s.at[b])
        drain(r_buf.at[b, 1], pd_s2.at[b])

        @pl.when(sec < last)
        def _():
            drain(i_buf.at[b, pl.ds(0, batch - length)], iss.at[b])
            drain(s_buf.at[b], qs.at[b])
            drain(x_buf.at[b], hs.at[b])
        return 0

    lax.fori_loop(0, micro, sent_batch, 0)

    @pl.when(sec == last)
    def _():
        drain(pin_o.at[pl.ds(0, nd - 1)], pin_s)

        def sent_pd(q, _):
            @pl.when(grp * dp + q != mp)
            def _():
                drain(pd.at[0], pd_s.at[q])
            return 0

        lax.fori_loop(0, grp, sent_pd, 0)

    @pl.when(is_final)
    def _():
        drain(embr, e_s)

        def sent_fan(t, _):
            _, _, home = fan_target(t)

            @pl.when(jnp.logical_not(home))
            def _():
                drain(outb, out_s.at[t])
            return 0

        lax.fori_loop(0, ns * nd, sent_fan, 0)


def front_kernel(sizes, rooms, tok_ref, len_ref, strips_ref, lens_ref, which_ref, lens, len_s, len_r, tok_s, tok_r, home_s):
    ns, nd, nm = sizes
    grp = nm // nd
    caps, _, piece = tok_ref.shape
    strip = piece // 2
    sec, dp, mp = lax.axis_index("section"), lax.axis_index("dp"), lax.axis_index("mp")
    my_group, my_q = mp // grp, lax.rem(mp, grp)
    home = jnp.logical_and(sec == 0, jnp.logical_and(my_group == 0, dp == 0))
    want_sec = my_group
    barrier = pltpu.get_barrier_semaphore()

    def hello(where):
        pl.semaphore_signal(barrier, inc=1, device_id=where, device_id_type=MESH)

    for o in range(1, nd):
        hello((sec, lax.rem(dp + o, nd), mp))

    @pl.when(sec == 0)
    def _():
        for d in range(nd):
            @pl.when(jnp.logical_not(jnp.logical_and(want_sec == 0, jnp.logical_and(dp == 0, d == 0))))
            def _():
                hello((want_sec, d, dp * grp + my_q))

    row = lax.broadcasted_iota(jnp.int32, (8, 128), 0)
    mine = jnp.zeros((8, 128), F32)
    for i in range(caps):
        mine = jnp.where(row == i, len_ref[i].astype(F32), mine)
    lens[dp] = mine

    source = tok_ref.at[:, :, pl.ds(pl.multiple_of(lax.rem(sec, 2) * strip, strip), strip)]
    slab = strips_ref.at[dp]

    @pl.when(home)
    def _():
        pltpu.make_async_copy(source, slab, home_s).start()
        pl.semaphore_wait(barrier, nd - 1)

    @pl.when(jnp.logical_not(home))
    def _():
        pl.semaphore_wait(barrier, nd)

    for o in range(1, nd):
        pltpu.make_async_remote_copy(
            src_ref=lens.at[dp], dst_ref=lens.at[dp], send_sem=len_s.at[o - 1], recv_sem=len_r.at[nd - 1 - o],
            device_id=(sec, lax.rem(dp + o, nd), mp), device_id_type=MESH).start()

    @pl.when(jnp.logical_not(home))
    def _():
        pltpu.make_async_remote_copy(
            src_ref=source, dst_ref=slab, send_sem=tok_s, recv_sem=tok_r.at[dp],
            device_id=(0, my_group, sec * grp + my_q), device_id_type=MESH).start()

    for o in range(1, nd):
        other = lens.at[lax.rem(dp + o, nd)]
        pltpu.make_async_copy(other, other, len_r.at[o - 1]).wait()
    lens_ref[...] = lens[...]
    counted = jnp.sum(lens[:, :, 0:1])
    which = jnp.int32(0)
    for room in rooms[:-1]:
        which = which + (counted > room).astype(jnp.int32)
    which_ref[0, 0] = which

    @pl.when(sec == 0)
    def _():
        for d in range(nd):
            here = strips_ref.at[d]
            itself = jnp.logical_and(want_sec == 0, jnp.logical_and(dp == 0, d == 0))

            @pl.when(itself)
            def _():
                pltpu.make_async_copy(here, here, home_s).wait()

            @pl.when(jnp.logical_not(itself))
            def _():
                pltpu.make_async_copy(here, here, tok_r.at[d]).wait()

    for o in range(1, nd):
        pltpu.make_async_copy(lens.at[dp], lens.at[dp], len_s.at[o - 1]).wait()

    @pl.when(jnp.logical_not(home))
    def _():
        pltpu.make_async_copy(slab, slab, tok_s).wait()


def front(sizes, plans, tokens, lengths):
    nd = sizes[1]
    caps, slots, piece = tokens.shape
    dma = pltpu.SemaphoreType.DMA
    return pl.pallas_call(
        functools.partial(front_kernel, sizes, [micro * batch for micro, batch in plans]),
        out_shape=(
            jax.ShapeDtypeStruct((nd, caps, slots, piece // 2), BF16),
            jax.ShapeDtypeStruct((nd, 8, 128), F32),
            jax.ShapeDtypeStruct((1, 1), jnp.int32),
        ),
        in_specs=[pl.BlockSpec(memory_space=pl.ANY), pl.BlockSpec(memory_space=pltpu.SMEM)],
        out_specs=(pl.BlockSpec(memory_space=pl.ANY), pl.BlockSpec(memory_space=pltpu.VMEM),
                   pl.BlockSpec(memory_space=pltpu.SMEM)),
        scratch_shapes=[
            pltpu.VMEM((nd, 8, 128), F32),
            dma((nd - 1,)), dma((nd - 1,)), dma, dma((nd,)), dma,
        ],
        compiler_params=pltpu.CompilerParams(
            collective_id=1, has_side_effects=True, vmem_limit_bytes=60 * 2 ** 20),
        name="front",
    )(tokens, lengths)


def per_device(
    sizes, plans,
    caption_tokens, caption_lengths, group_ids, text_gain, text_gate, text_up, text_down,
    text_proj, image_patches, image_gain, image_fc1, image_fc2, image_proj,
):
    strips, lens, which = front(sizes, plans, caption_tokens, caption_lengths)
    operands = (
        strips, lens, group_ids, text_gain, text_gate, text_up, text_down,
        text_proj, image_patches, image_gain.reshape(1, -1), image_fc1, image_fc2, image_proj,
    )
    branches = [functools.partial(towers, sizes, plan, 2 + i) for i, plan in enumerate(plans)]
    return lax.switch(which[0, 0], branches, *operands)


def towers(
    sizes, plan, barrier_id,
    strips, caption_lengths, group_ids, text_gain, text_gate, text_up, text_down,
    text_proj, image_patches, image_gain, image_fc1, image_fc2, image_proj,
):
    ns, nd, nm = sizes
    grp = nm // nd
    micro, batch = plan
    _, caps, slots, strip = strips.shape
    piece = 2 * strip
    length = batch // nd
    ncap = nd * caps
    dl, width = text_gate.shape[1], text_gate.shape[2]
    dv, hv = image_fc1.shape
    embed = text_proj.shape[1]
    nf = nd * grp
    any_spec = pl.BlockSpec(memory_space=pl.ANY)
    vmem = pl.BlockSpec(memory_space=pltpu.VMEM)
    smem = pl.BlockSpec(memory_space=pltpu.SMEM)
    dma = pltpu.SemaphoreType.DMA
    loss, gcap, gimg = pl.pallas_call(
        functools.partial(kernel, sizes),
        out_shape=(
            jax.ShapeDtypeStruct((1, 128), F32),
            jax.ShapeDtypeStruct((caps, embed), F32),
            jax.ShapeDtypeStruct((1, embed), F32),
        ),
        in_specs=[any_spec, vmem, smem, vmem, any_spec, any_spec, any_spec, any_spec,
                  any_spec, vmem, any_spec, any_spec, any_spec],
        out_specs=(vmem, vmem, vmem),
        scratch_shapes=[
            pltpu.VMEM((dl, 2 * width), BF16),
            pltpu.VMEM((width, dl), BF16),
            pltpu.VMEM((piece, embed), BF16),
            pltpu.VMEM((dv, hv), BF16),
            pltpu.VMEM((hv, dv), BF16),
            pltpu.VMEM((dv, embed), BF16),
            pltpu.VMEM(image_patches.shape, BF16),
            pltpu.VMEM((nd, caps, slots, piece // 2), BF16),
            pltpu.VMEM((8, ncap * slots), F32),
            pltpu.VMEM((micro, batch, dl), BF16),
            pltpu.VMEM((micro, length, 2 * width + 128), BF16),
            pltpu.VMEM((micro, 3 * length, 2 * width + 128), BF16),
            pltpu.VMEM((micro, length, width), BF16),
            pltpu.VMEM((micro, length, width + 128), BF16),
            pltpu.VMEM((micro, 2, length, 2 * width + 128), BF16),
            pltpu.VMEM((micro, batch, width), BF16),
            pltpu.VMEM((micro, batch, dl), BF16),
            pltpu.VMEM((micro, nm - 1, length, piece), BF16),
            pltpu.VMEM((micro, length, piece), BF16),
            pltpu.VMEM((nm - 1, dv // 128, 128), F32),
            pltpu.VMEM((dv // 128, 128), F32),
            pltpu.VMEM((ns * nd, dv // 128, 128), F32),
            pltpu.VMEM((dv // 128, 128), F32),
            pltpu.VMEM((8, dv), F32),
            pltpu.VMEM((ncap, piece), F32),
            pltpu.VMEM((ncap, width), F32),
            pltpu.VMEM((nd, ncap, width), BF16),
            pltpu.VMEM((grp, ncap, piece), F32),
            pltpu.VMEM((nm - 1, ncap, piece), F32),
            pltpu.VMEM((ncap, embed), BF16),
            pltpu.VMEM((nf - 1, ncap, embed), BF16),
            pltpu.VMEM((8, embed), F32),
            dma((9,)), *([dma((micro,))] * 13), dma((nd - 1, micro)),
            dma((micro,)), dma, dma, dma, dma, dma, dma, dma((grp,)), dma, dma, dma, dma((ns * nd,)), dma,
        ],
        compiler_params=pltpu.CompilerParams(
            collective_id=barrier_id, has_side_effects=True, vmem_limit_bytes=60 * 2 ** 20),
        name=f"towers_{micro}_{batch}",
    )(
        strips, caption_lengths, group_ids, text_gain, text_gate, text_up, text_down,
        text_proj, image_patches, image_gain, image_fc1, image_fc2, image_proj,
    )
    return loss[0, 0], gcap, gimg


def solution(mesh):
    sizes = tuple(mesh.shape[axis] for axis in ("section", "dp", "mp"))
    return jax.shard_map(
        functools.partial(per_device, sizes, PLANS),
        mesh=mesh,
        in_specs=(
            P("dp", None, "mp"),
            P("dp"),
            P(),
            P("section", None),
            P("section", "dp", "mp"),
            P("section", "dp", "mp"),
            P("section", "mp", "dp"),
            P("mp", None),
            P("dp", "section", None),
            P(),
            P(None, "mp"),
            P("mp", None),
            P(),
        ),
        out_specs=(P(), P("dp", None), P("dp", None)),
        check_vma=False,
    )
```

```python
import functools

import jax
import jax.numpy as jnp
from jax import lax
from jax.experimental import pallas as pl
from jax.experimental.pallas import tpu as pltpu
from jax.sharding import PartitionSpec as P

MESH = pl.DeviceIdType.MESH
PLANS = ((3, 128), (4, 128), (3, 192), (5, 128), (4, 192), (4, 256))
BF16 = jnp.bfloat16
F32 = jnp.float32


def kernel(
    sizes,
    tok_ref, len_ref, gid_ref, gain_ref, gate_ref, up_ref, down_ref, tproj_ref,
    patch_ref, vgain_ref, fc1_ref, fc2_ref, iproj_ref,
    loss_ref, gcap_ref, gimg_ref,
    w_gu, w_dn, w_tp, w_f1, w_f2, w_ip, patches,
    tok_buf, pos_buf, x_buf, far_buf, p_buf, ra_buf, rb_buf, r_buf, i_buf, q_buf, s_buf, h_buf,
    im1, im1_own, im2, im2_own, imrow, mean_h,
    pin, pin_o, pd, pdr, emb, embr, outb,
    wsem, xr, pa_s, pa_r, pb_s, pb_r, pc_s, pc_r, pd_s2, pd_r2,
    iss, qs, qr, hs, ir,
    cs, im1_s, im1_r, im2_s, im2_r, pin_s, pin_r, pd_s, pd_r, e_s, e_r, out_s, out_r,
):
    ns, nd, nm = sizes
    grp = nm // nd
    _, caps, slots, strip = tok_ref.shape
    piece = 2 * strip
    ncap = nd * caps
    micro, batch, dl = x_buf.shape
    length = batch // nd
    width = gate_ref.shape[2]
    dim = dl * nd
    sec, dp, mp = lax.axis_index("section"), lax.axis_index("dp"), lax.axis_index("mp")
    last = ns - 1
    my_group = mp // grp
    my_q = lax.rem(mp, grp)
    is_final = jnp.logical_and(sec == last, my_group == dp)

    def send(src, dst, s_sem, r_sem, where):
        pltpu.make_async_remote_copy(
            src_ref=src, dst_ref=dst, send_sem=s_sem, recv_sem=r_sem,
            device_id=where, device_id_type=MESH,
        ).start()

    def drain(ref, sem):
        pltpu.make_async_copy(ref, ref, sem).wait()

    def load(src, dst, index):
        pltpu.make_async_copy(src, dst, wsem.at[index]).start()

    def loaded(dst, index):
        pltpu.make_async_copy(dst, dst, wsem.at[index]).wait()

    def chunk(d):
        return pl.ds(pl.multiple_of(d * length, length), length)

    rows_y = pl.ds(pl.multiple_of(my_group * length, length), length)
    cols_z = pl.ds(pl.multiple_of(my_q * piece, piece), piece)

    @pl.when(sec == 0)
    def _():
        load(tok_ref, tok_buf, 0)

    load(gate_ref.at[0], w_gu.at[:, pl.ds(0, width)], 3)
    load(up_ref.at[0], w_gu.at[:, pl.ds(width, width)], 4)
    load(patch_ref, patches, 8)
    load(fc1_ref, w_f1, 1)
    load(fc2_ref, w_f2, 2)
    load(down_ref.at[0], w_dn, 5)
    load(tproj_ref, w_tp, 6)
    load(iproj_ref, w_ip, 7)

    root = grp * lax.rem(dp + 1, nd)
    nf = nd * grp
    me_f = dp * grp + my_q
    final_mp = dp * grp + my_q
    barrier = pltpu.get_barrier_semaphore()

    def hello(where):
        pl.semaphore_signal(barrier, inc=1, device_id=where, device_id_type=MESH)

    def each(lo, hi, body):
        def step(o, _):
            body(o)
            return 0

        lax.fori_loop(lo, hi, step, 0)

    each(1, nd, lambda o: hello((sec, lax.rem(dp + o, nd), mp)))
    each(1, nm, lambda o: hello((sec, dp, lax.rem(mp + o, nm))))

    @pl.when(sec > 0)
    def _():
        each(0, nm, lambda o: hello((sec - 1, dp, lax.rem(mp + o, nm))))

    @pl.when(is_final)
    def _():
        each(0, ns * nd, lambda o: hello((o // nd, lax.rem(o, nd), grp * lax.rem(o + 1, nd))))

        def other_final(o):
            f = lax.rem(me_f + o, nf)
            hello((last, f // grp, f))

        each(1, nf, other_final)

    @pl.when(jnp.logical_not(is_final))
    def _():
        hello((last, dp, final_mp))

    partners = nd - 1 + nm - 1 + jnp.where(sec < last, nm, 0) + jnp.where(mp == root, nd * grp, 0)
    partners = partners + jnp.where(is_final, nf - 1 + ns * nd - 1, 0)
    pl.semaphore_wait(barrier, partners)

    counts = [len_ref[c // caps, c % caps:c % caps + 1, 0:1] for c in range(ncap)]
    starts = [jnp.zeros((1, 1), F32)]
    for c in range(ncap):
        starts.append(starts[-1] + counts[c])

    def dp_peers(body):
        def step(o, _):
            peer = lax.rem(dp + o, nd)
            body(peer, nd - 1 - o)
            return 0

        lax.fori_loop(1, nd, step, 0)

    vtiles = w_f2.shape[1] // 128

    def image_layer():
        loaded(patches, 8)
        loaded(w_f1, 1)
        rows = patches[0].astype(F32)
        scale = lax.rsqrt(jnp.mean(rows * rows, -1, keepdims=True) + 1e-05)
        vnormed = (rows * scale * vgain_ref[...]).astype(BF16)
        hidden = jnp.dot(vnormed, w_f1[...], preferred_element_type=F32)
        vinner = (0.5 * hidden * (1.0 + lax.erf(hidden * (0.5 ** 0.5)))).astype(BF16)
        vsum = jnp.sum(vinner.astype(F32), 0, keepdims=True)
        high = vsum.astype(BF16)
        low = (vsum - high.astype(F32)).astype(BF16)
        loaded(w_f2, 2)
        two = jnp.concatenate([jnp.broadcast_to(high, (8, high.shape[1])), jnp.broadcast_to(low, (8, low.shape[1]))], 0)
        prod = jnp.dot(two, w_f2[...], preferred_element_type=F32)
        part = prod[0:1] + prod[8:9] + jnp.where(mp == 0, 1.0, 0.0) * jnp.sum(rows, 0, keepdims=True)
        for i in range(vtiles):
            im1_own[pl.ds(i, 1), :] = part[:, 128 * i:128 * (i + 1)]

        @pl.when(mp != root)
        def _():
            slot = lax.rem(mp - root - 1 + 2 * nm, nm)
            send(im1_own, im1.at[slot], im1_s, im1_r, (sec, dp, root))

        @pl.when(mp == root)
        def _():
            drain(im1, im1_r)
            im2_own[...] = im1_own[...] + jnp.sum(im1[...], 0)

            def to_final(t, _):
                d, q = t // grp, lax.rem(t, grp)
                send(im2_own, im2.at[sec * nd + dp], im2_s, im2_r, (last, d, grp * d + q))
                return 0

            lax.fori_loop(0, nd * grp, to_final, 0)

    @pl.when(sec > 0)
    def _():
        image_layer()

    loaded(w_gu.at[:, pl.ds(0, width)], 3)
    loaded(w_gu.at[:, pl.ds(width, width)], 4)
    gain = gain_ref[0:1, pl.ds(pl.multiple_of(dp * dl, dl), dl)]

    def members(first, width):
        row = lax.broadcasted_iota(jnp.int32, (ncap, width), 0)
        token = (lax.broadcasted_iota(jnp.int32, (ncap, width), 1) + first).astype(F32)
        lo = jnp.zeros((ncap, width), F32)
        hi = jnp.zeros((ncap, width), F32)
        for c in range(ncap):
            lo = jnp.where(row == c, starts[c], lo)
            hi = jnp.where(row == c, starts[c + 1], hi)
        return jnp.where(jnp.logical_and(token >= lo, token < hi), 1.0, 0.0).astype(BF16)

    right, left, far = lax.rem(dp + 1, nd), lax.rem(dp + nd - 1, nd), lax.rem(dp + 2, nd)
    full = 2 * width + 128
    low_cols, high_cols = pl.ds(0, width), pl.ds(width, width + 128)

    def ranked(t):
        y, z = lax.rem(my_group + t // grp + 2, nd), lax.rem(my_q + t + grp // 2, grp)
        return y * grp + z

    def mp_peers(body):
        def one(t):
            peer = ranked(t)

            @pl.when(peer != mp)
            def _():
                body(peer, lax.rem(mp - peer - 1 + 2 * nm, nm))

        each(0, nm, one)

    half_rows = pl.ds(pl.multiple_of((my_group // 2) * (batch // 2), batch // 2), batch // 2)

    strip_cols = pl.ds(pl.multiple_of(my_q * piece + lax.rem(my_group, 2) * strip, strip), strip)

    def positions():
        loaded(tok_buf, 0)
        lane = lax.broadcasted_iota(jnp.int32, (8, ncap * slots), 1)
        cap = lane // slots
        pos = jnp.full((8, ncap * slots), -1.0, F32)
        for c in range(ncap):
            at = (lane - c * slots).astype(F32)
            pos = jnp.where(jnp.logical_and(cap == c, at < counts[c]), starts[c] + at, pos)
        pos_buf[...] = pos

    def pack(b):
        row = lax.broadcasted_iota(jnp.int32, (batch // 2, ncap * slots), 0)
        row = (row + (b * batch + (my_group // 2) * (batch // 2))).astype(F32)
        picks = jnp.where(row == pos_buf[0:1], 1.0, 0.0).astype(BF16)
        tokens = tok_buf[...].reshape(ncap * slots, strip)
        here = x_buf.at[b, half_rows, strip_cols]
        x_buf[b, half_rows, strip_cols] = jnp.dot(picks, tokens, preferred_element_type=F32).astype(BF16)
        mp_peers(lambda peer, slot: send(here, here, cs.at[b], xr.at[b], (sec, dp, peer)))

    @pl.when(sec == 0)
    def _():
        positions()
        each(0, min(2, micro), pack)

    def products(rows, out):
        x = rows.astype(F32)
        total = jnp.sum(x * x, -1, keepdims=True)
        high = total.astype(BF16).astype(F32)
        lane = lax.broadcasted_iota(jnp.int32, (x.shape[0], 128), 1)
        out[:, pl.ds(2 * width, 128)] = jnp.where(lane < 64, high, total - high).astype(BF16)
        out[:, pl.ds(0, 2 * width)] = jnp.dot(
            (x * gain).astype(BF16), w_gu[...], preferred_element_type=F32).astype(BF16)

    def stage_far(b):
        @pl.when(sec == 0)
        def _():
            drain(s_buf.at[b], xr.at[b])

        @pl.when(sec > 0)
        def _():
            drain(x_buf.at[b], xr.at[b])

        products(x_buf[b, chunk(far), :], far_buf.at[b])
        send(far_buf.at[b, :, low_cols], ra_buf.at[b], pa_s.at[b], pa_r.at[b], (sec, right, mp))
        send(far_buf.at[b, :, high_cols], rb_buf.at[b], pb_s.at[b], pb_r.at[b], (sec, left, mp))

    def stage_near(b):
        near = jnp.concatenate([x_buf[b, chunk(c), :] for c in (right, left, dp)], 0)
        products(near, p_buf.at[b])

    to_right, to_left, to_self = pl.ds(0, length), pl.ds(length, length), pl.ds(2 * length, length)

    def stage_relay(b):
        drain(ra_buf.at[b], pa_r.at[b])
        p_buf[b, to_right, low_cols] = (
            p_buf[b, to_right, low_cols].astype(F32) + ra_buf[b].astype(F32)).astype(BF16)
        send(p_buf.at[b, to_right], r_buf.at[b, 0], pc_s.at[b], pc_r.at[b], (sec, right, mp))
        drain(rb_buf.at[b], pb_r.at[b])
        p_buf[b, to_left, high_cols] = (
            p_buf[b, to_left, high_cols].astype(F32) + rb_buf[b].astype(F32)).astype(BF16)
        send(p_buf.at[b, to_left], r_buf.at[b, 1], pd_s2.at[b], pd_r2.at[b], (sec, left, mp))

    def stage_b(b):
        drain(r_buf.at[b, 0], pc_r.at[b])
        drain(r_buf.at[b, 1], pd_r2.at[b])
        total = p_buf[b, to_self, :].astype(F32) + r_buf[b, 0].astype(F32) + r_buf[b, 1].astype(F32)
        squares = total[:, 2 * width:2 * width + 1] + total[:, 2 * width + 64:2 * width + 65]
        scale = lax.rsqrt(squares * (1.0 / dim) + 1e-05)
        gate = total[:, :width] * scale
        upper = total[:, width:2 * width] * scale
        inner = (gate * jax.nn.sigmoid(gate) * upper).astype(BF16)

        @pl.when(sec < last)
        def _():
            i_buf[b, chunk(dp), :] = inner
            here = i_buf.at[b, chunk(dp)]
            for o in (1, nd - 1, 2):
                send(here, here, iss.at[b], ir.at[nd - 1 - o, b], (sec, lax.rem(dp + o, nd), mp))

        @pl.when(sec == last)
        def _():
            @pl.when(b == 0)
            def _():
                pin[...] = jnp.zeros(pin.shape, F32)
                mean_h[...] = jnp.zeros(mean_h.shape, F32)

            mine = members(b * batch + dp * length, length)
            pin[...] = pin[...] + jnp.dot(mine, inner, preferred_element_type=F32)

            @pl.when(is_final)
            def _():
                mean_h[...] = mean_h[...] + jnp.dot(
                    members(b * batch, batch), x_buf[b, :, cols_z], preferred_element_type=F32)

    def down(b, offsets):
        sources = [lax.rem(dp + o, nd) for o in offsets]
        for o, source in zip(offsets, sources):
            if o:
                drain(i_buf.at[b, chunk(source)], ir.at[o - 1, b])
        out = jnp.dot(jnp.concatenate([i_buf[b, chunk(c), :] for c in sources], 0), w_dn[...],
                      preferred_element_type=F32).astype(BF16)
        for at, source in enumerate(sources):
            q_buf[b, chunk(source), :] = out[at * length:(at + 1) * length]

            def to_owner(o, source=source):
                z = lax.rem(my_q + o + grp // 2, grp)
                owner = source * grp + z

                @pl.when(owner != mp)
                def _():
                    slot = lax.rem(mp - owner - 1 + 2 * nm, nm)
                    send(q_buf.at[b, chunk(source), pl.ds(pl.multiple_of(z * piece, piece), piece)],
                         s_buf.at[b, slot], qs.at[b], qr.at[b], (sec, dp, owner))

            each(0, grp, to_owner)

    def stage_down_near(b):
        down(b, (0, 1, nd - 1))

    def stage_down_far(b):
        down(b, (2,))

    def stage_d(b):
        drain(s_buf.at[b], qr.at[b])
        total = x_buf[b, rows_y, cols_z].astype(F32) + q_buf[b, rows_y, cols_z].astype(F32)
        for i in range(nm - 1):
            total = total + s_buf[b, i].astype(F32)
        h_buf[b] = total.astype(BF16)

        each(0, nm, lambda t: send(
            h_buf.at[b], x_buf.at[b, rows_y, cols_z], hs.at[b], xr.at[b], (sec + 1, dp, ranked(t))))

    def tick(i, _):
        def at(stage, back, also=True):
            @pl.when(jnp.logical_and(also, jnp.logical_and(i >= back, i < micro + back)))
            def _():
                stage(i - back)

        inside = sec < last
        at(stage_far, 0)
        at(stage_b, 1)
        at(stage_near, 0)

        @pl.when(jnp.logical_and(sec == 0, i + 2 < micro))
        def _():
            pack(i + 2)

        at(stage_relay, 0)

        @pl.when(jnp.logical_and(inside, i == 1))
        def _():
            loaded(w_dn, 5)

        at(stage_down_near, 1, inside)
        at(stage_d, 2, inside)
        at(stage_down_far, 1, inside)
        return 0

    lax.fori_loop(0, micro + 2, tick, 0)

    @pl.when(sec == 0)
    def _():
        image_layer()

    loaded(w_tp, 6)
    loaded(w_ip, 7)

    def shares():
        row = lax.broadcasted_iota(jnp.int32, (ncap, 1), 0)
        count = jnp.ones((ncap, 1), F32)
        for c in range(ncap):
            count = jnp.where(row == c, counts[c], count)
        return 1.0 / count

    @pl.when(sec == last)
    def _():
        loaded(w_dn, 5)
        pin_o[nd - 1] = (pin[...] * shares()).astype(BF16)
        dp_peers(lambda peer, slot: send(pin_o.at[nd - 1], pin_o.at[slot], pin_s, pin_r, (sec, peer, mp)))

        @pl.when(is_final)
        def _():
            drain(im2, im2_r)
            imrow[...] = jnp.zeros(imrow.shape, F32)
            for d in range(nd):
                image = im2[d]
                for s in range(1, ns):
                    image = image + im2[s * nd + d]
                for i in range(vtiles):
                    imrow[d:d + 1, 128 * i:128 * (i + 1)] = image[i:i + 1, :]

        drain(pin_o.at[pl.ds(0, nd - 1)], pin_r)
        pooled = pin_o[0].astype(F32)
        for i in range(1, nd):
            pooled = pooled + pin_o[i].astype(F32)
        out = jnp.dot(pooled.astype(BF16), w_dn[...], preferred_element_type=F32)
        for q in range(grp):
            pd[q] = out[:, q * piece:(q + 1) * piece]

        def to_final(q, _):
            target = grp * dp + q

            @pl.when(target != mp)
            def _():
                slot = lax.rem(mp - target - 1 + 2 * nm, nm)
                send(pd.at[q], pdr.at[slot], pd_s.at[q], pd_r, (sec, dp, target))
            return 0

        lax.fori_loop(0, grp, to_final, 0)

    def fan_target(t):
        s, y = t // nd, lax.rem(t, nd)
        target = y * grp + my_q
        return s, target, jnp.logical_and(s == last, target == mp)

    @pl.when(is_final)
    def _():
        drain(pdr, pd_r)
        total = pd[my_q]
        for i in range(nm - 1):
            total = total + pdr[i]
        total = total + mean_h[...] * shares()
        emb[...] = jnp.dot(total.astype(BF16), w_tp[...], preferred_element_type=F32).astype(BF16)

        def to_others(o, _):
            f = lax.rem(me_f + o, nf)
            d, q = f // grp, lax.rem(f, grp)
            send(emb, embr.at[nf - 1 - o], e_s, e_r, (last, d, grp * d + q))
            return 0

        lax.fori_loop(1, nf, to_others, 0)
        pooled = (imrow[...] * (1.0 / (ns * patch_ref.shape[1]))).astype(BF16)
        image = jnp.dot(pooled, w_ip[...], preferred_element_type=F32)
        iu = image * lax.rsqrt(jnp.sum(image * image, -1, keepdims=True) + 1e-06)

        nrow = ncap
        row = lax.broadcasted_iota(jnp.int32, (nrow, 8), 0)
        col = lax.broadcasted_iota(jnp.int32, (nrow, 8), 1)
        gids = jnp.full((nrow, 8), -1, jnp.int32)
        for k in range(ncap):
            gids = jnp.where(row == k, gid_ref[k], gids)
        match = jnp.where(gids == col, 1.0, 0.0)
        real = jnp.where(col < nd, 1.0, 0.0)

        drain(embr, e_r)
        total = emb[...].astype(F32)
        for i in range(nf - 1):
            total = total + embr[i].astype(F32)
        cu = total * lax.rsqrt(jnp.sum(total * total, -1, keepdims=True) + 1e-06)
        logits = jnp.zeros((nrow, 8), F32)
        for j in range(nd):
            logits = jnp.where(col == j, 10.0 * jnp.sum(cu * iu[j:j + 1], -1, keepdims=True), logits)
        expo = jnp.exp(logits) * real
        good = expo * match
        by_row = jnp.sum(expo, 1, keepdims=True)
        by_row = jnp.where(by_row > 0, by_row, 1.0)
        by_col = jnp.sum(expo, 0, keepdims=True)
        by_col = jnp.where(by_col > 0, by_col, 1.0)
        good_col = jnp.sum(good, 0, keepdims=True)
        good_col = jnp.where(good_col > 0, good_col, 1.0)
        def whole(array):
            return jnp.sum(jnp.sum(array, 0, keepdims=True), 1, keepdims=True)

        forward = whole(jnp.log(by_row)) - whole(logits * match * real)
        backward = whole(jnp.log(by_col) - jnp.log(good_col))
        loss = 0.5 * (forward / ncap + backward / nd)
        slope = 5.0 * (expo / by_row - match * real + expo / by_col - good / good_col)
        gcap = jnp.zeros(cu.shape, F32)
        gimg = jnp.zeros((1, cu.shape[1]), F32)
        for j in range(nd):
            gcap = gcap + slope[:, j:j + 1] * iu[j:j + 1]
            gimg = gimg + jnp.where(dp == j, 1.0, 0.0) * jnp.sum(slope[:, j:j + 1] * cu, 0, keepdims=True)
        mine = jnp.zeros((caps, cu.shape[1]), F32)
        for d in range(nd):
            mine = mine + jnp.where(dp == d, 1.0, 0.0) * gcap[caps * d:caps * d + caps]
        outb[0:caps, :] = mine
        outb[caps:caps + 1, :] = gimg
        outb[caps + 1:8, :] = jnp.broadcast_to(loss, (7 - caps, cu.shape[1]))

        def fan(t, _):
            s, target, home = fan_target(t)

            @pl.when(jnp.logical_not(home))
            def _():
                send(outb, outb, out_s.at[t], out_r, (s, dp, target))
            return 0

        lax.fori_loop(0, ns * nd, fan, 0)

    @pl.when(jnp.logical_not(is_final))
    def _():
        drain(outb, out_r)

    loss_ref[...] = outb[caps + 1:caps + 2, 0:128]
    gcap_ref[...] = outb[0:caps, :]
    gimg_ref[...] = outb[caps:caps + 1, :]

    @pl.when(mp != root)
    def _():
        drain(im1_own, im1_s)

    @pl.when(mp == root)
    def _():
        drain(im2, im2_s)

    def sent_batch(b, _):
        @pl.when(sec == 0)
        def _():
            drain(s_buf.at[b], cs.at[b])

        drain(ra_buf.at[b], pa_s.at[b])
        drain(rb_buf.at[b], pb_s.at[b])
        drain(r_buf.at[b, 0], pc_s.at[b])
        drain(r_buf.at[b, 1], pd_s2.at[b])

        @pl.when(sec < last)
        def _():
            drain(i_buf.at[b, pl.ds(0, batch - length)], iss.at[b])
            drain(s_buf.at[b], qs.at[b])
            drain(x_buf.at[b], hs.at[b])
        return 0

    lax.fori_loop(0, micro, sent_batch, 0)

    @pl.when(sec == last)
    def _():
        drain(pin_o.at[pl.ds(0, nd - 1)], pin_s)

        def sent_pd(q, _):
            @pl.when(grp * dp + q != mp)
            def _():
                drain(pd.at[0], pd_s.at[q])
            return 0

        lax.fori_loop(0, grp, sent_pd, 0)

    @pl.when(is_final)
    def _():
        drain(embr, e_s)

        def sent_fan(t, _):
            _, _, home = fan_target(t)

            @pl.when(jnp.logical_not(home))
            def _():
                drain(outb, out_s.at[t])
            return 0

        lax.fori_loop(0, ns * nd, sent_fan, 0)


def front_kernel(sizes, rooms, tok_ref, len_ref, strips_ref, lens_ref, which_ref, lens, len_s, len_r, tok_s, tok_r, home_s):
    ns, nd, nm = sizes
    grp = nm // nd
    caps, _, piece = tok_ref.shape
    strip = piece // 2
    sec, dp, mp = lax.axis_index("section"), lax.axis_index("dp"), lax.axis_index("mp")
    my_group, my_q = mp // grp, lax.rem(mp, grp)
    home = jnp.logical_and(sec == 0, jnp.logical_and(my_group == 0, dp == 0))
    want_sec = my_group
    barrier = pltpu.get_barrier_semaphore()

    def hello(where):
        pl.semaphore_signal(barrier, inc=1, device_id=where, device_id_type=MESH)

    for o in range(1, nd):
        hello((sec, lax.rem(dp + o, nd), mp))

    @pl.when(sec == 0)
    def _():
        for d in range(nd):
            @pl.when(jnp.logical_not(jnp.logical_and(want_sec == 0, jnp.logical_and(dp == 0, d == 0))))
            def _():
                hello((want_sec, d, dp * grp + my_q))

    row = lax.broadcasted_iota(jnp.int32, (8, 128), 0)
    mine = jnp.zeros((8, 128), F32)
    for i in range(caps):
        mine = jnp.where(row == i, len_ref[i].astype(F32), mine)
    lens[dp] = mine

    source = tok_ref.at[:, :, pl.ds(pl.multiple_of(lax.rem(sec, 2) * strip, strip), strip)]
    slab = strips_ref.at[dp]

    @pl.when(home)
    def _():
        pltpu.make_async_copy(source, slab, home_s).start()
        pl.semaphore_wait(barrier, nd - 1)

    @pl.when(jnp.logical_not(home))
    def _():
        pl.semaphore_wait(barrier, nd)

    for o in range(1, nd):
        pltpu.make_async_remote_copy(
            src_ref=lens.at[dp], dst_ref=lens.at[dp], send_sem=len_s.at[o - 1], recv_sem=len_r.at[nd - 1 - o],
            device_id=(sec, lax.rem(dp + o, nd), mp), device_id_type=MESH).start()

    @pl.when(jnp.logical_not(home))
    def _():
        pltpu.make_async_remote_copy(
            src_ref=source, dst_ref=slab, send_sem=tok_s, recv_sem=tok_r.at[dp],
            device_id=(0, my_group, sec * grp + my_q), device_id_type=MESH).start()

    for o in range(1, nd):
        other = lens.at[lax.rem(dp + o, nd)]
        pltpu.make_async_copy(other, other, len_r.at[o - 1]).wait()
    lens_ref[...] = lens[...]
    counted = jnp.sum(lens[:, :, 0:1])
    which = jnp.int32(0)
    for room in rooms[:-1]:
        which = which + (counted > room).astype(jnp.int32)
    which_ref[0, 0] = which

    @pl.when(sec == 0)
    def _():
        for d in range(nd):
            here = strips_ref.at[d]
            itself = jnp.logical_and(want_sec == 0, jnp.logical_and(dp == 0, d == 0))

            @pl.when(itself)
            def _():
                pltpu.make_async_copy(here, here, home_s).wait()

            @pl.when(jnp.logical_not(itself))
            def _():
                pltpu.make_async_copy(here, here, tok_r.at[d]).wait()

    for o in range(1, nd):
        pltpu.make_async_copy(lens.at[dp], lens.at[dp], len_s.at[o - 1]).wait()

    @pl.when(jnp.logical_not(home))
    def _():
        pltpu.make_async_copy(slab, slab, tok_s).wait()


def front(sizes, plans, tokens, lengths):
    nd = sizes[1]
    caps, slots, piece = tokens.shape
    dma = pltpu.SemaphoreType.DMA
    return pl.pallas_call(
        functools.partial(front_kernel, sizes, [micro * batch for micro, batch in plans]),
        out_shape=(
            jax.ShapeDtypeStruct((nd, caps, slots, piece // 2), BF16),
            jax.ShapeDtypeStruct((nd, 8, 128), F32),
            jax.ShapeDtypeStruct((1, 1), jnp.int32),
        ),
        in_specs=[pl.BlockSpec(memory_space=pl.ANY), pl.BlockSpec(memory_space=pltpu.SMEM)],
        out_specs=(pl.BlockSpec(memory_space=pl.ANY), pl.BlockSpec(memory_space=pltpu.VMEM),
                   pl.BlockSpec(memory_space=pltpu.SMEM)),
        scratch_shapes=[
            pltpu.VMEM((nd, 8, 128), F32),
            dma((nd - 1,)), dma((nd - 1,)), dma, dma((nd,)), dma,
        ],
        compiler_params=pltpu.CompilerParams(
            collective_id=1, has_side_effects=True, vmem_limit_bytes=60 * 2 ** 20),
        name="front",
    )(tokens, lengths)


def per_device(
    sizes, plans,
    caption_tokens, caption_lengths, group_ids, text_gain, text_gate, text_up, text_down,
    text_proj, image_patches, image_gain, image_fc1, image_fc2, image_proj,
):
    strips, lens, which = front(sizes, plans, caption_tokens, caption_lengths)
    operands = (
        strips, lens, group_ids, text_gain, text_gate, text_up, text_down,
        text_proj, image_patches, image_gain.reshape(1, -1), image_fc1, image_fc2, image_proj,
    )
    branches = [functools.partial(towers, sizes, plan, 2 + i) for i, plan in enumerate(plans)]
    return lax.switch(which[0, 0], branches, *operands)


def towers(
    sizes, plan, barrier_id,
    strips, caption_lengths, group_ids, text_gain, text_gate, text_up, text_down,
    text_proj, image_patches, image_gain, image_fc1, image_fc2, image_proj,
):
    ns, nd, nm = sizes
    grp = nm // nd
    micro, batch = plan
    _, caps, slots, strip = strips.shape
    piece = 2 * strip
    length = batch // nd
    ncap = nd * caps
    dl, width = text_gate.shape[1], text_gate.shape[2]
    dv, hv = image_fc1.shape
    embed = text_proj.shape[1]
    nf = nd * grp
    any_spec = pl.BlockSpec(memory_space=pl.ANY)
    vmem = pl.BlockSpec(memory_space=pltpu.VMEM)
    smem = pl.BlockSpec(memory_space=pltpu.SMEM)
    dma = pltpu.SemaphoreType.DMA
    loss, gcap, gimg = pl.pallas_call(
        functools.partial(kernel, sizes),
        out_shape=(
            jax.ShapeDtypeStruct((1, 128), F32),
            jax.ShapeDtypeStruct((caps, embed), F32),
            jax.ShapeDtypeStruct((1, embed), F32),
        ),
        in_specs=[any_spec, vmem, smem, vmem, any_spec, any_spec, any_spec, any_spec,
                  any_spec, vmem, any_spec, any_spec, any_spec],
        out_specs=(vmem, vmem, vmem),
        scratch_shapes=[
            pltpu.VMEM((dl, 2 * width), BF16),
            pltpu.VMEM((width, dl), BF16),
            pltpu.VMEM((piece, embed), BF16),
            pltpu.VMEM((dv, hv), BF16),
            pltpu.VMEM((hv, dv), BF16),
            pltpu.VMEM((dv, embed), BF16),
            pltpu.VMEM(image_patches.shape, BF16),
            pltpu.VMEM((nd, caps, slots, piece // 2), BF16),
            pltpu.VMEM((8, ncap * slots), F32),
            pltpu.VMEM((micro, batch, dl), BF16),
            pltpu.VMEM((micro, length, 2 * width + 128), BF16),
            pltpu.VMEM((micro, 3 * length, 2 * width + 128), BF16),
            pltpu.VMEM((micro, length, width), BF16),
            pltpu.VMEM((micro, length, width + 128), BF16),
            pltpu.VMEM((micro, 2, length, 2 * width + 128), BF16),
            pltpu.VMEM((micro, batch, width), BF16),
            pltpu.VMEM((micro, batch, dl), BF16),
            pltpu.VMEM((micro, nm - 1, length, piece), BF16),
            pltpu.VMEM((micro, length, piece), BF16),
            pltpu.VMEM((nm - 1, dv // 128, 128), F32),
            pltpu.VMEM((dv // 128, 128), F32),
            pltpu.VMEM((ns * nd, dv // 128, 128), F32),
            pltpu.VMEM((dv // 128, 128), F32),
            pltpu.VMEM((8, dv), F32),
            pltpu.VMEM((ncap, piece), F32),
            pltpu.VMEM((ncap, width), F32),
            pltpu.VMEM((nd, ncap, width), BF16),
            pltpu.VMEM((grp, ncap, piece), F32),
            pltpu.VMEM((nm - 1, ncap, piece), F32),
            pltpu.VMEM((ncap, embed), BF16),
            pltpu.VMEM((nf - 1, ncap, embed), BF16),
            pltpu.VMEM((8, embed), F32),
            dma((9,)), *([dma((micro,))] * 13), dma((nd - 1, micro)),
            dma((micro,)), dma, dma, dma, dma, dma, dma, dma((grp,)), dma, dma, dma, dma((ns * nd,)), dma,
        ],
        compiler_params=pltpu.CompilerParams(
            collective_id=barrier_id, has_side_effects=True, vmem_limit_bytes=60 * 2 ** 20),
        name=f"towers_{micro}_{batch}",
    )(
        strips, caption_lengths, group_ids, text_gain, text_gate, text_up, text_down,
        text_proj, image_patches, image_gain, image_fc1, image_fc2, image_proj,
    )
    return loss[0, 0], gcap, gimg


def solution(mesh):
    sizes = tuple(mesh.shape[axis] for axis in ("section", "dp", "mp"))
    return jax.shard_map(
        functools.partial(per_device, sizes, PLANS),
        mesh=mesh,
        in_specs=(
            P("dp", None, "mp"),
            P("dp"),
            P(),
            P("section", None),
            P("section", "dp", "mp"),
            P("section", "dp", "mp"),
            P("section", "mp", "dp"),
            P("mp", None),
            P("dp", "section", None),
            P(),
            P(None, "mp"),
            P("mp", None),
            P(),
        ),
        out_specs=(P(), P("dp", None), P("dp", None)),
        check_vma=False,
    )
```

```python
import functools

import jax
import jax.numpy as jnp
from jax import lax
from jax.experimental import pallas as pl
from jax.experimental.pallas import tpu as pltpu
from jax.sharding import PartitionSpec as P

MESH = pl.DeviceIdType.MESH
PLANS = ((3, 128), (3, 192), (3, 256), (4, 256))
BF16 = jnp.bfloat16
F32 = jnp.float32


def kernel(
    sizes,
    tok_ref, len_ref, gid_ref, gain_ref, gate_ref, up_ref, down_ref, tproj_ref,
    patch_ref, vgain_ref, fc1_ref, fc2_ref, iproj_ref,
    loss_ref, gcap_ref, gimg_ref,
    w_gu, w_dn, w_tp, w_f1, w_f2, w_ip, patches,
    tok_buf, pos_buf, x_buf, far_buf, p_buf, ra_buf, rb_buf, r_buf, i_buf, q_buf, s_buf, h_buf,
    im1, im1_own, im2, im2_own, imrow, mean_h,
    pin, pin_o, pd, pdr, emb, embr, outb,
    wsem, xr, pa_s, pa_r, pb_s, pb_r, pc_s, pc_r, pd_s2, pd_r2,
    iss, qs, qr, hs, ir,
    cs, im1_s, im1_r, im2_s, im2_r, pin_s, pin_r, pd_s, pd_r, e_s, e_r, out_s, out_r,
):
    ns, nd, nm = sizes
    grp = nm // nd
    _, caps, slots, strip = tok_ref.shape
    piece = 2 * strip
    ncap = nd * caps
    micro, batch, dl = x_buf.shape
    length = batch // nd
    width = gate_ref.shape[2]
    dim = dl * nd
    sec, dp, mp = lax.axis_index("section"), lax.axis_index("dp"), lax.axis_index("mp")
    last = ns - 1
    my_group = mp // grp
    my_q = lax.rem(mp, grp)
    is_final = jnp.logical_and(sec == last, my_group == dp)

    def send(src, dst, s_sem, r_sem, where):
        pltpu.make_async_remote_copy(
            src_ref=src, dst_ref=dst, send_sem=s_sem, recv_sem=r_sem,
            device_id=where, device_id_type=MESH,
        ).start()

    def drain(ref, sem):
        pltpu.make_async_copy(ref, ref, sem).wait()

    def load(src, dst, index):
        pltpu.make_async_copy(src, dst, wsem.at[index]).start()

    def loaded(dst, index):
        pltpu.make_async_copy(dst, dst, wsem.at[index]).wait()

    def chunk(d):
        return pl.ds(pl.multiple_of(d * length, length), length)

    rows_y = pl.ds(pl.multiple_of(my_group * length, length), length)
    cols_z = pl.ds(pl.multiple_of(my_q * piece, piece), piece)

    @pl.when(sec == 0)
    def _():
        load(tok_ref, tok_buf, 0)

    load(gate_ref.at[0], w_gu.at[:, pl.ds(0, width)], 3)
    load(up_ref.at[0], w_gu.at[:, pl.ds(width, width)], 4)
    load(patch_ref, patches, 8)
    load(fc1_ref, w_f1, 1)
    load(fc2_ref, w_f2, 2)
    load(down_ref.at[0], w_dn, 5)
    load(tproj_ref, w_tp, 6)
    load(iproj_ref, w_ip, 7)

    root = grp * lax.rem(dp + 1, nd)
    nf = nd * grp
    me_f = dp * grp + my_q
    final_mp = dp * grp + my_q
    barrier = pltpu.get_barrier_semaphore()

    def hello(where):
        pl.semaphore_signal(barrier, inc=1, device_id=where, device_id_type=MESH)

    def each(lo, hi, body):
        def step(o, _):
            body(o)
            return 0

        lax.fori_loop(lo, hi, step, 0, unroll=True)

    each(1, nd, lambda o: hello((sec, lax.rem(dp + o, nd), mp)))
    each(1, nm, lambda o: hello((sec, dp, lax.rem(mp + o, nm))))

    @pl.when(sec > 0)
    def _():
        each(0, nm, lambda o: hello((sec - 1, dp, lax.rem(mp + o, nm))))

    @pl.when(is_final)
    def _():
        each(0, ns * nd, lambda o: hello((o // nd, lax.rem(o, nd), grp * lax.rem(o + 1, nd))))

        def other_final(o):
            f = lax.rem(me_f + o, nf)
            hello((last, f // grp, f))

        each(1, nf, other_final)

    @pl.when(jnp.logical_not(is_final))
    def _():
        hello((last, dp, final_mp))

    partners = nd - 1 + nm - 1 + jnp.where(sec < last, nm, 0) + jnp.where(mp == root, nd * grp, 0)
    partners = partners + jnp.where(is_final, nf - 1 + ns * nd - 1, 0)
    pl.semaphore_wait(barrier, partners)

    counts = [len_ref[c // caps, c % caps:c % caps + 1, 0:1] for c in range(ncap)]
    starts = [jnp.zeros((1, 1), F32)]
    for c in range(ncap):
        starts.append(starts[-1] + counts[c])

    def dp_peers(body):
        def step(o, _):
            peer = lax.rem(dp + o, nd)
            body(peer, nd - 1 - o)
            return 0

        lax.fori_loop(1, nd, step, 0)

    vtiles = w_f2.shape[1] // 128

    def image_layer():
        loaded(patches, 8)
        loaded(w_f1, 1)
        rows = patches[0].astype(F32)
        scale = lax.rsqrt(jnp.mean(rows * rows, -1, keepdims=True) + 1e-05)
        vnormed = (rows * scale * vgain_ref[...]).astype(BF16)
        hidden = jnp.dot(vnormed, w_f1[...], preferred_element_type=F32)
        vinner = (0.5 * hidden * (1.0 + lax.erf(hidden * (0.5 ** 0.5)))).astype(BF16)
        vsum = jnp.sum(vinner.astype(F32), 0, keepdims=True)
        high = vsum.astype(BF16)
        low = (vsum - high.astype(F32)).astype(BF16)
        loaded(w_f2, 2)
        two = jnp.concatenate([jnp.broadcast_to(high, (8, high.shape[1])), jnp.broadcast_to(low, (8, low.shape[1]))], 0)
        prod = jnp.dot(two, w_f2[...], preferred_element_type=F32)
        part = prod[0:1] + prod[8:9] + jnp.where(mp == 0, 1.0, 0.0) * jnp.sum(rows, 0, keepdims=True)
        for i in range(vtiles):
            im1_own[pl.ds(i, 1), :] = part[:, 128 * i:128 * (i + 1)]

        @pl.when(mp != root)
        def _():
            slot = lax.rem(mp - root - 1 + 2 * nm, nm)
            send(im1_own, im1.at[slot], im1_s, im1_r, (sec, dp, root))

        @pl.when(mp == root)
        def _():
            drain(im1, im1_r)
            im2_own[...] = im1_own[...] + jnp.sum(im1[...], 0)

            def to_final(t, _):
                d, q = t // grp, lax.rem(t, grp)
                send(im2_own, im2.at[sec * nd + dp], im2_s, im2_r, (last, d, grp * d + q))
                return 0

            lax.fori_loop(0, nd * grp, to_final, 0)

    @pl.when(sec > 0)
    def _():
        image_layer()

    loaded(w_gu.at[:, pl.ds(0, width)], 3)
    loaded(w_gu.at[:, pl.ds(width, width)], 4)
    gain = gain_ref[0:1, pl.ds(pl.multiple_of(dp * dl, dl), dl)]

    def members(first, width):
        row = lax.broadcasted_iota(jnp.int32, (ncap, width), 0)
        token = (lax.broadcasted_iota(jnp.int32, (ncap, width), 1) + first).astype(F32)
        lo = jnp.zeros((ncap, width), F32)
        hi = jnp.zeros((ncap, width), F32)
        for c in range(ncap):
            lo = jnp.where(row == c, starts[c], lo)
            hi = jnp.where(row == c, starts[c + 1], hi)
        return jnp.where(jnp.logical_and(token >= lo, token < hi), 1.0, 0.0).astype(BF16)

    right, left, far = lax.rem(dp + 1, nd), lax.rem(dp + nd - 1, nd), lax.rem(dp + 2, nd)
    full = 2 * width + 128
    low_cols, high_cols = pl.ds(0, width), pl.ds(width, width + 128)

    def ranked(t):
        y, z = lax.rem(my_group + t // grp + 2, nd), lax.rem(my_q + t + grp // 2, grp)
        return y * grp + z

    def mp_peers(body):
        def one(t):
            peer = ranked(t)
            body(peer, lax.rem(mp - peer - 1 + 2 * nm, nm))

        itself = (nd - 2) * grp + grp // 2
        each(0, itself, one)
        each(itself + 1, nm, one)

    half_rows = pl.ds(pl.multiple_of((my_group // 2) * (batch // 2), batch // 2), batch // 2)

    strip_cols = pl.ds(pl.multiple_of(my_q * piece + lax.rem(my_group, 2) * strip, strip), strip)

    def positions():
        loaded(tok_buf, 0)
        lane = lax.broadcasted_iota(jnp.int32, (8, ncap * slots), 1)
        cap = lane // slots
        pos = jnp.full((8, ncap * slots), -1.0, F32)
        for c in range(ncap):
            at = (lane - c * slots).astype(F32)
            pos = jnp.where(jnp.logical_and(cap == c, at < counts[c]), starts[c] + at, pos)
        pos_buf[...] = pos

    def pack(b):
        row = lax.broadcasted_iota(jnp.int32, (batch // 2, ncap * slots), 0)
        row = (row + (b * batch + (my_group // 2) * (batch // 2))).astype(F32)
        picks = jnp.where(row == pos_buf[0:1], 1.0, 0.0).astype(BF16)
        tokens = tok_buf[...].reshape(ncap * slots, strip)
        here = x_buf.at[b, half_rows, strip_cols]
        x_buf[b, half_rows, strip_cols] = jnp.dot(picks, tokens, preferred_element_type=F32).astype(BF16)
        mp_peers(lambda peer, slot: send(here, here, cs.at[b], xr.at[b], (sec, dp, peer)))

    @pl.when(sec == 0)
    def _():
        positions()
        lax.fori_loop(0, min(2, micro), lambda b, _: (pack(b), 0)[1], 0)

    def products(rows, out, first_done=None):
        x = rows.astype(F32)
        scaled = (x * gain).astype(BF16)
        if first_done is None:
            out[:, pl.ds(0, 2 * width)] = jnp.dot(
                scaled, w_gu[...], preferred_element_type=F32).astype(BF16)
        else:
            out[:, pl.ds(0, width)] = jnp.dot(
                scaled, w_gu[:, 0:width], preferred_element_type=F32).astype(BF16)
            first_done()
            out[:, pl.ds(width, width)] = jnp.dot(
                scaled, w_gu[:, width:2 * width], preferred_element_type=F32).astype(BF16)
        total = jnp.sum(x * x, -1, keepdims=True)
        high = total.astype(BF16).astype(F32)
        lane = lax.broadcasted_iota(jnp.int32, (x.shape[0], 128), 1)
        out[:, pl.ds(2 * width, 128)] = jnp.where(lane < 64, high, total - high).astype(BF16)

    def stage_far(b):
        @pl.when(sec == 0)
        def _():
            drain(s_buf.at[b], xr.at[b])

        @pl.when(sec > 0)
        def _():
            drain(x_buf.at[b], xr.at[b])

        products(x_buf[b, chunk(far), :], far_buf.at[b], lambda: send(
            far_buf.at[b, :, low_cols], ra_buf.at[b], pa_s.at[b], pa_r.at[b], (sec, right, mp)))
        send(far_buf.at[b, :, high_cols], rb_buf.at[b], pb_s.at[b], pb_r.at[b], (sec, left, mp))

    def stage_near(b):
        near = jnp.concatenate([x_buf[b, chunk(c), :] for c in (right, left, dp)], 0)
        products(near, p_buf.at[b])

    to_right, to_left, to_self = pl.ds(0, length), pl.ds(length, length), pl.ds(2 * length, length)

    def stage_relay(b):
        drain(ra_buf.at[b], pa_r.at[b])
        p_buf[b, to_right, low_cols] = (
            p_buf[b, to_right, low_cols].astype(F32) + ra_buf[b].astype(F32)).astype(BF16)
        send(p_buf.at[b, to_right], r_buf.at[b, 0], pc_s.at[b], pc_r.at[b], (sec, right, mp))
        drain(rb_buf.at[b], pb_r.at[b])
        p_buf[b, to_left, high_cols] = (
            p_buf[b, to_left, high_cols].astype(F32) + rb_buf[b].astype(F32)).astype(BF16)
        send(p_buf.at[b, to_left], r_buf.at[b, 1], pd_s2.at[b], pd_r2.at[b], (sec, left, mp))

    def stage_b(b):
        drain(r_buf.at[b, 0], pc_r.at[b])
        drain(r_buf.at[b, 1], pd_r2.at[b])
        total = p_buf[b, to_self, :].astype(F32) + r_buf[b, 0].astype(F32) + r_buf[b, 1].astype(F32)
        squares = total[:, 2 * width:2 * width + 1] + total[:, 2 * width + 64:2 * width + 65]
        scale = lax.rsqrt(squares * (1.0 / dim) + 1e-05)
        gate = total[:, :width] * scale
        upper = total[:, width:2 * width] * scale
        inner = (gate * jax.nn.sigmoid(gate) * upper).astype(BF16)

        @pl.when(sec < last)
        def _():
            i_buf[b, chunk(dp), :] = inner
            here = i_buf.at[b, chunk(dp)]
            for o in (1, nd - 1, 2):
                send(here, here, iss.at[b], ir.at[nd - 1 - o, b], (sec, lax.rem(dp + o, nd), mp))

        @pl.when(sec == last)
        def _():
            @pl.when(b == 0)
            def _():
                pin[...] = jnp.zeros(pin.shape, F32)
                mean_h[...] = jnp.zeros(mean_h.shape, F32)

            mine = members(b * batch + dp * length, length)
            pin[...] = pin[...] + jnp.dot(mine, inner, preferred_element_type=F32)

            @pl.when(is_final)
            def _():
                mean_h[...] = mean_h[...] + jnp.dot(
                    members(b * batch, batch), x_buf[b, :, cols_z], preferred_element_type=F32)

    def down(b, offsets):
        sources = [lax.rem(dp + o, nd) for o in offsets]
        for o, source in zip(offsets, sources):
            if o:
                drain(i_buf.at[b, chunk(source)], ir.at[o - 1, b])
        out = jnp.dot(jnp.concatenate([i_buf[b, chunk(c), :] for c in sources], 0), w_dn[...],
                      preferred_element_type=F32).astype(BF16)
        for at, source in enumerate(sources):
            q_buf[b, chunk(source), :] = out[at * length:(at + 1) * length]

            def to_owner(o, source=source):
                z = lax.rem(my_q + o + grp // 2, grp)
                owner = source * grp + z

                @pl.when(owner != mp)
                def _():
                    slot = lax.rem(mp - owner - 1 + 2 * nm, nm)
                    send(q_buf.at[b, chunk(source), pl.ds(pl.multiple_of(z * piece, piece), piece)],
                         s_buf.at[b, slot], qs.at[b], qr.at[b], (sec, dp, owner))

            each(0, grp, to_owner)

    def stage_down_near(b):
        down(b, (0, 1, nd - 1))

    def stage_down_far(b):
        down(b, (2,))

    def stage_d(b):
        drain(s_buf.at[b], qr.at[b])
        total = x_buf[b, rows_y, cols_z].astype(F32) + q_buf[b, rows_y, cols_z].astype(F32)
        for i in range(nm - 1):
            total = total + s_buf[b, i].astype(F32)
        h_buf[b] = total.astype(BF16)

        each(0, nm, lambda t: send(
            h_buf.at[b], x_buf.at[b, rows_y, cols_z], hs.at[b], xr.at[b], (sec + 1, dp, ranked(t))))

    def tick(i, _):
        def at(stage, back, also=True):
            @pl.when(jnp.logical_and(also, jnp.logical_and(i >= back, i < micro + back)))
            def _():
                stage(i - back)

        inside = sec < last
        at(stage_far, 0)
        at(stage_b, 1)
        at(stage_near, 0)

        @pl.when(jnp.logical_and(sec == 0, i + 2 < micro))
        def _():
            pack(i + 2)

        at(stage_relay, 0)

        @pl.when(jnp.logical_and(inside, i == 1))
        def _():
            loaded(w_dn, 5)

        at(stage_down_near, 1, inside)
        at(stage_d, 2, inside)
        at(stage_down_far, 1, inside)
        return 0

    lax.fori_loop(0, micro + 2, tick, 0)

    @pl.when(sec == 0)
    def _():
        image_layer()

    loaded(w_tp, 6)
    loaded(w_ip, 7)

    def shares():
        row = lax.broadcasted_iota(jnp.int32, (ncap, 1), 0)
        count = jnp.ones((ncap, 1), F32)
        for c in range(ncap):
            count = jnp.where(row == c, counts[c], count)
        return 1.0 / count

    @pl.when(sec == last)
    def _():
        loaded(w_dn, 5)
        pin_o[nd - 1] = (pin[...] * shares()).astype(BF16)
        dp_peers(lambda peer, slot: send(pin_o.at[nd - 1], pin_o.at[slot], pin_s, pin_r, (sec, peer, mp)))

        @pl.when(is_final)
        def _():
            drain(im2, im2_r)
            imrow[...] = jnp.zeros(imrow.shape, F32)
            for d in range(nd):
                image = im2[d]
                for s in range(1, ns):
                    image = image + im2[s * nd + d]
                for i in range(vtiles):
                    imrow[d:d + 1, 128 * i:128 * (i + 1)] = image[i:i + 1, :]

        drain(pin_o.at[pl.ds(0, nd - 1)], pin_r)
        pooled = pin_o[0].astype(F32)
        for i in range(1, nd):
            pooled = pooled + pin_o[i].astype(F32)
        out = jnp.dot(pooled.astype(BF16), w_dn[...], preferred_element_type=F32)
        for q in range(grp):
            pd[q] = out[:, q * piece:(q + 1) * piece]

        def to_final(q, _):
            target = grp * dp + q

            @pl.when(target != mp)
            def _():
                slot = lax.rem(mp - target - 1 + 2 * nm, nm)
                send(pd.at[q], pdr.at[slot], pd_s.at[q], pd_r, (sec, dp, target))
            return 0

        lax.fori_loop(0, grp, to_final, 0)

    def fan_target(t):
        s, y = t // nd, lax.rem(t, nd)
        target = y * grp + my_q
        return s, target, jnp.logical_and(s == last, target == mp)

    @pl.when(is_final)
    def _():
        drain(pdr, pd_r)
        total = pd[my_q]
        for i in range(nm - 1):
            total = total + pdr[i]
        total = total + mean_h[...] * shares()
        emb[...] = jnp.dot(total.astype(BF16), w_tp[...], preferred_element_type=F32).astype(BF16)

        def to_others(o, _):
            f = lax.rem(me_f + o, nf)
            d, q = f // grp, lax.rem(f, grp)
            send(emb, embr.at[nf - 1 - o], e_s, e_r, (last, d, grp * d + q))
            return 0

        lax.fori_loop(1, nf, to_others, 0)
        pooled = (imrow[...] * (1.0 / (ns * patch_ref.shape[1]))).astype(BF16)
        image = jnp.dot(pooled, w_ip[...], preferred_element_type=F32)
        iu = image * lax.rsqrt(jnp.sum(image * image, -1, keepdims=True) + 1e-06)

        nrow = ncap
        row = lax.broadcasted_iota(jnp.int32, (nrow, 8), 0)
        col = lax.broadcasted_iota(jnp.int32, (nrow, 8), 1)
        gids = jnp.full((nrow, 8), -1, jnp.int32)
        for k in range(ncap):
            gids = jnp.where(row == k, gid_ref[k], gids)
        match = jnp.where(gids == col, 1.0, 0.0)
        real = jnp.where(col < nd, 1.0, 0.0)

        drain(embr, e_r)
        total = emb[...].astype(F32)
        for i in range(nf - 1):
            total = total + embr[i].astype(F32)
        cu = total * lax.rsqrt(jnp.sum(total * total, -1, keepdims=True) + 1e-06)
        logits = jnp.zeros((nrow, 8), F32)
        for j in range(nd):
            logits = jnp.where(col == j, 10.0 * jnp.sum(cu * iu[j:j + 1], -1, keepdims=True), logits)
        expo = jnp.exp(logits) * real
        good = expo * match
        by_row = jnp.sum(expo, 1, keepdims=True)
        by_row = jnp.where(by_row > 0, by_row, 1.0)
        by_col = jnp.sum(expo, 0, keepdims=True)
        by_col = jnp.where(by_col > 0, by_col, 1.0)
        good_col = jnp.sum(good, 0, keepdims=True)
        good_col = jnp.where(good_col > 0, good_col, 1.0)
        def whole(array):
            return jnp.sum(jnp.sum(array, 0, keepdims=True), 1, keepdims=True)

        forward = whole(jnp.log(by_row)) - whole(logits * match * real)
        backward = whole(jnp.log(by_col) - jnp.log(good_col))
        loss = 0.5 * (forward / ncap + backward / nd)
        slope = 5.0 * (expo / by_row - match * real + expo / by_col - good / good_col)
        gcap = jnp.zeros(cu.shape, F32)
        gimg = jnp.zeros((1, cu.shape[1]), F32)
        for j in range(nd):
            gcap = gcap + slope[:, j:j + 1] * iu[j:j + 1]
            gimg = gimg + jnp.where(dp == j, 1.0, 0.0) * jnp.sum(slope[:, j:j + 1] * cu, 0, keepdims=True)
        mine = jnp.zeros((caps, cu.shape[1]), F32)
        for d in range(nd):
            mine = mine + jnp.where(dp == d, 1.0, 0.0) * gcap[caps * d:caps * d + caps]
        outb[0:caps, :] = mine
        outb[caps:caps + 1, :] = gimg
        outb[caps + 1:8, :] = jnp.broadcast_to(loss, (7 - caps, cu.shape[1]))

        def fan(t, _):
            s, target, home = fan_target(t)

            @pl.when(jnp.logical_not(home))
            def _():
                send(outb, outb, out_s.at[t], out_r, (s, dp, target))
            return 0

        lax.fori_loop(0, ns * nd, fan, 0)

    @pl.when(jnp.logical_not(is_final))
    def _():
        drain(outb, out_r)

    loss_ref[...] = outb[caps + 1:caps + 2, 0:128]
    gcap_ref[...] = outb[0:caps, :]
    gimg_ref[...] = outb[caps:caps + 1, :]

    @pl.when(mp != root)
    def _():
        drain(im1_own, im1_s)

    @pl.when(mp == root)
    def _():
        drain(im2, im2_s)

    def sent_batch(b, _):
        @pl.when(sec == 0)
        def _():
            drain(s_buf.at[b], cs.at[b])

        drain(ra_buf.at[b], pa_s.at[b])
        drain(rb_buf.at[b], pb_s.at[b])
        drain(r_buf.at[b, 0], pc_s.at[b])
        drain(r_buf.at[b, 1], pd_s2.at[b])

        @pl.when(sec < last)
        def _():
            drain(i_buf.at[b, pl.ds(0, batch - length)], iss.at[b])
            drain(s_buf.at[b], qs.at[b])
            drain(x_buf.at[b], hs.at[b])
        return 0

    lax.fori_loop(0, micro, sent_batch, 0)

    @pl.when(sec == last)
    def _():
        drain(pin_o.at[pl.ds(0, nd - 1)], pin_s)

        def sent_pd(q, _):
            @pl.when(grp * dp + q != mp)
            def _():
                drain(pd.at[0], pd_s.at[q])
            return 0

        lax.fori_loop(0, grp, sent_pd, 0)

    @pl.when(is_final)
    def _():
        drain(embr, e_s)

        def sent_fan(t, _):
            _, _, home = fan_target(t)

            @pl.when(jnp.logical_not(home))
            def _():
                drain(outb, out_s.at[t])
            return 0

        lax.fori_loop(0, ns * nd, sent_fan, 0)


def front_kernel(sizes, rooms, tok_ref, len_ref, strips_ref, lens_ref, which_ref, lens, len_s, len_r, tok_s, tok_r, home_s):
    ns, nd, nm = sizes
    grp = nm // nd
    caps, _, piece = tok_ref.shape
    strip = piece // 2
    sec, dp, mp = lax.axis_index("section"), lax.axis_index("dp"), lax.axis_index("mp")
    my_group, my_q = mp // grp, lax.rem(mp, grp)
    home = jnp.logical_and(sec == 0, jnp.logical_and(my_group == 0, dp == 0))
    want_sec = my_group
    barrier = pltpu.get_barrier_semaphore()

    def hello(where):
        pl.semaphore_signal(barrier, inc=1, device_id=where, device_id_type=MESH)

    for o in range(1, nd):
        hello((sec, lax.rem(dp + o, nd), mp))

    @pl.when(sec == 0)
    def _():
        for d in range(nd):
            @pl.when(jnp.logical_not(jnp.logical_and(want_sec == 0, jnp.logical_and(dp == 0, d == 0))))
            def _():
                hello((want_sec, d, dp * grp + my_q))

    row = lax.broadcasted_iota(jnp.int32, (8, 128), 0)
    mine = jnp.zeros((8, 128), F32)
    for i in range(caps):
        mine = jnp.where(row == i, len_ref[i].astype(F32), mine)
    lens[dp] = mine

    source = tok_ref.at[:, :, pl.ds(pl.multiple_of(lax.rem(sec, 2) * strip, strip), strip)]
    slab = strips_ref.at[dp]

    @pl.when(home)
    def _():
        pltpu.make_async_copy(source, slab, home_s).start()
        pl.semaphore_wait(barrier, nd - 1)

    @pl.when(jnp.logical_not(home))
    def _():
        pl.semaphore_wait(barrier, nd)

    for o in range(1, nd):
        pltpu.make_async_remote_copy(
            src_ref=lens.at[dp], dst_ref=lens.at[dp], send_sem=len_s.at[o - 1], recv_sem=len_r.at[nd - 1 - o],
            device_id=(sec, lax.rem(dp + o, nd), mp), device_id_type=MESH).start()

    @pl.when(jnp.logical_not(home))
    def _():
        pltpu.make_async_remote_copy(
            src_ref=source, dst_ref=slab, send_sem=tok_s, recv_sem=tok_r.at[dp],
            device_id=(0, my_group, sec * grp + my_q), device_id_type=MESH).start()

    for o in range(1, nd):
        other = lens.at[lax.rem(dp + o, nd)]
        pltpu.make_async_copy(other, other, len_r.at[o - 1]).wait()
    lens_ref[...] = lens[...]
    counted = jnp.sum(lens[:, :, 0:1])
    which = jnp.int32(0)
    for room in rooms[:-1]:
        which = which + (counted > room).astype(jnp.int32)
    which_ref[0, 0] = which

    @pl.when(sec == 0)
    def _():
        for d in range(nd):
            here = strips_ref.at[d]
            itself = jnp.logical_and(want_sec == 0, jnp.logical_and(dp == 0, d == 0))

            @pl.when(itself)
            def _():
                pltpu.make_async_copy(here, here, home_s).wait()

            @pl.when(jnp.logical_not(itself))
            def _():
                pltpu.make_async_copy(here, here, tok_r.at[d]).wait()

    for o in range(1, nd):
        pltpu.make_async_copy(lens.at[dp], lens.at[dp], len_s.at[o - 1]).wait()

    @pl.when(jnp.logical_not(home))
    def _():
        pltpu.make_async_copy(slab, slab, tok_s).wait()


def front(sizes, plans, tokens, lengths):
    nd = sizes[1]
    caps, slots, piece = tokens.shape
    dma = pltpu.SemaphoreType.DMA
    return pl.pallas_call(
        functools.partial(front_kernel, sizes, [micro * batch for micro, batch in plans]),
        out_shape=(
            jax.ShapeDtypeStruct((nd, caps, slots, piece // 2), BF16),
            jax.ShapeDtypeStruct((nd, 8, 128), F32),
            jax.ShapeDtypeStruct((1, 1), jnp.int32),
        ),
        in_specs=[pl.BlockSpec(memory_space=pl.ANY), pl.BlockSpec(memory_space=pltpu.SMEM)],
        out_specs=(pl.BlockSpec(memory_space=pl.ANY), pl.BlockSpec(memory_space=pltpu.VMEM),
                   pl.BlockSpec(memory_space=pltpu.SMEM)),
        scratch_shapes=[
            pltpu.VMEM((nd, 8, 128), F32),
            dma((nd - 1,)), dma((nd - 1,)), dma, dma((nd,)), dma,
        ],
        compiler_params=pltpu.CompilerParams(
            collective_id=1, has_side_effects=True, vmem_limit_bytes=60 * 2 ** 20),
        name="front",
    )(tokens, lengths)


def per_device(
    sizes, plans,
    caption_tokens, caption_lengths, group_ids, text_gain, text_gate, text_up, text_down,
    text_proj, image_patches, image_gain, image_fc1, image_fc2, image_proj,
):
    strips, lens, which = front(sizes, plans, caption_tokens, caption_lengths)
    operands = (
        strips, lens, group_ids, text_gain, text_gate, text_up, text_down,
        text_proj, image_patches, image_gain.reshape(1, -1), image_fc1, image_fc2, image_proj,
    )
    branches = [functools.partial(towers, sizes, plan, 2 + i) for i, plan in enumerate(plans)]
    return lax.switch(which[0, 0], branches, *operands)


def towers(
    sizes, plan, barrier_id,
    strips, caption_lengths, group_ids, text_gain, text_gate, text_up, text_down,
    text_proj, image_patches, image_gain, image_fc1, image_fc2, image_proj,
):
    ns, nd, nm = sizes
    grp = nm // nd
    micro, batch = plan
    _, caps, slots, strip = strips.shape
    piece = 2 * strip
    length = batch // nd
    ncap = nd * caps
    dl, width = text_gate.shape[1], text_gate.shape[2]
    dv, hv = image_fc1.shape
    embed = text_proj.shape[1]
    nf = nd * grp
    any_spec = pl.BlockSpec(memory_space=pl.ANY)
    vmem = pl.BlockSpec(memory_space=pltpu.VMEM)
    smem = pl.BlockSpec(memory_space=pltpu.SMEM)
    dma = pltpu.SemaphoreType.DMA
    loss, gcap, gimg = pl.pallas_call(
        functools.partial(kernel, sizes),
        out_shape=(
            jax.ShapeDtypeStruct((1, 128), F32),
            jax.ShapeDtypeStruct((caps, embed), F32),
            jax.ShapeDtypeStruct((1, embed), F32),
        ),
        in_specs=[any_spec, vmem, smem, vmem, any_spec, any_spec, any_spec, any_spec,
                  any_spec, vmem, any_spec, any_spec, any_spec],
        out_specs=(vmem, vmem, vmem),
        scratch_shapes=[
            pltpu.VMEM((dl, 2 * width), BF16),
            pltpu.VMEM((width, dl), BF16),
            pltpu.VMEM((piece, embed), BF16),
            pltpu.VMEM((dv, hv), BF16),
            pltpu.VMEM((hv, dv), BF16),
            pltpu.VMEM((dv, embed), BF16),
            pltpu.VMEM(image_patches.shape, BF16),
            pltpu.VMEM((nd, caps, slots, piece // 2), BF16),
            pltpu.VMEM((8, ncap * slots), F32),
            pltpu.VMEM((micro, batch, dl), BF16),
            pltpu.VMEM((micro, length, 2 * width + 128), BF16),
            pltpu.VMEM((micro, 3 * length, 2 * width + 128), BF16),
            pltpu.VMEM((micro, length, width), BF16),
            pltpu.VMEM((micro, length, width + 128), BF16),
            pltpu.VMEM((micro, 2, length, 2 * width + 128), BF16),
            pltpu.VMEM((micro, batch, width), BF16),
            pltpu.VMEM((micro, batch, dl), BF16),
            pltpu.VMEM((micro, nm - 1, length, piece), BF16),
            pltpu.VMEM((micro, length, piece), BF16),
            pltpu.VMEM((nm - 1, dv // 128, 128), F32),
            pltpu.VMEM((dv // 128, 128), F32),
            pltpu.VMEM((ns * nd, dv // 128, 128), F32),
            pltpu.VMEM((dv // 128, 128), F32),
            pltpu.VMEM((8, dv), F32),
            pltpu.VMEM((ncap, piece), F32),
            pltpu.VMEM((ncap, width), F32),
            pltpu.VMEM((nd, ncap, width), BF16),
            pltpu.VMEM((grp, ncap, piece), F32),
            pltpu.VMEM((nm - 1, ncap, piece), F32),
            pltpu.VMEM((ncap, embed), BF16),
            pltpu.VMEM((nf - 1, ncap, embed), BF16),
            pltpu.VMEM((8, embed), F32),
            dma((9,)), *([dma((micro,))] * 13), dma((nd - 1, micro)),
            dma((micro,)), dma, dma, dma, dma, dma, dma, dma((grp,)), dma, dma, dma, dma((ns * nd,)), dma,
        ],
        compiler_params=pltpu.CompilerParams(
            collective_id=barrier_id, has_side_effects=True, vmem_limit_bytes=60 * 2 ** 20),
        name=f"towers_{micro}_{batch}",
    )(
        strips, caption_lengths, group_ids, text_gain, text_gate, text_up, text_down,
        text_proj, image_patches, image_gain, image_fc1, image_fc2, image_proj,
    )
    return loss[0, 0], gcap, gimg


def solution(mesh):
    sizes = tuple(mesh.shape[axis] for axis in ("section", "dp", "mp"))
    return jax.shard_map(
        functools.partial(per_device, sizes, PLANS),
        mesh=mesh,
        in_specs=(
            P("dp", None, "mp"),
            P("dp"),
            P(),
            P("section", None),
            P("section", "dp", "mp"),
            P("section", "dp", "mp"),
            P("section", "mp", "dp"),
            P("mp", None),
            P("dp", "section", None),
            P(),
            P(None, "mp"),
            P("mp", None),
            P(),
        ),
        out_specs=(P(), P("dp", None), P("dp", None)),
        check_vma=False,
    )
```

```python
import functools

import jax
import jax.numpy as jnp
from jax import lax
from jax.experimental import pallas as pl
from jax.experimental.pallas import tpu as pltpu
from jax.sharding import PartitionSpec as P

MESH = pl.DeviceIdType.MESH
PLANS = ((3, 128), (4, 128), (3, 192), (5, 128), (4, 192), (4, 256))
BF16 = jnp.bfloat16
F32 = jnp.float32


def kernel(
    sizes,
    tok_ref, len_ref, gid_ref, gain_ref, gate_ref, up_ref, down_ref, tproj_ref,
    patch_ref, vgain_ref, fc1_ref, fc2_ref, iproj_ref,
    loss_ref, gcap_ref, gimg_ref,
    w_gu, w_dn, w_tp, w_f1, w_f2, w_ip, patches,
    tok_buf, pos_buf, x_buf, far_buf, p_buf, ra_buf, rb_buf, r_buf, i_buf, q_buf, s_buf, h_buf,
    im1, im1_own, im2, im2_own, imrow, mean_h,
    pin, pin_o, pd, pdr, emb, embr, outb,
    wsem, xr, pa_s, pa_r, pb_s, pb_r, pc_s, pc_r, pd_s2, pd_r2,
    iss, qs, qr, hs, ir,
    cs, im1_s, im1_r, im2_s, im2_r, pin_s, pin_r, pd_s, pd_r, e_s, e_r, out_s, out_r,
):
    ns, nd, nm = sizes
    grp = nm // nd
    _, caps, slots, strip = tok_ref.shape
    piece = 2 * strip
    ncap = nd * caps
    micro, batch, dl = x_buf.shape
    length = batch // nd
    width = gate_ref.shape[2]
    dim = dl * nd
    sec, dp, mp = lax.axis_index("section"), lax.axis_index("dp"), lax.axis_index("mp")
    last = ns - 1
    my_group = mp // grp
    my_q = lax.rem(mp, grp)
    is_final = jnp.logical_and(sec == last, my_group == dp)

    def send(src, dst, s_sem, r_sem, where):
        pltpu.make_async_remote_copy(
            src_ref=src, dst_ref=dst, send_sem=s_sem, recv_sem=r_sem,
            device_id=where, device_id_type=MESH,
        ).start()

    def drain(ref, sem):
        pltpu.make_async_copy(ref, ref, sem).wait()

    def load(src, dst, index):
        pltpu.make_async_copy(src, dst, wsem.at[index]).start()

    def loaded(dst, index):
        pltpu.make_async_copy(dst, dst, wsem.at[index]).wait()

    def chunk(d):
        return pl.ds(pl.multiple_of(d * length, length), length)

    rows_y = pl.ds(pl.multiple_of(my_group * length, length), length)
    cols_z = pl.ds(pl.multiple_of(my_q * piece, piece), piece)

    @pl.when(sec == 0)
    def _():
        load(tok_ref, tok_buf, 0)

    load(gate_ref.at[0], w_gu.at[:, pl.ds(0, width)], 3)
    load(up_ref.at[0], w_gu.at[:, pl.ds(width, width)], 4)
    load(patch_ref, patches, 8)
    load(fc1_ref, w_f1, 1)
    load(fc2_ref, w_f2, 2)
    load(down_ref.at[0], w_dn, 5)
    load(tproj_ref, w_tp, 6)
    load(iproj_ref, w_ip, 7)

    root = grp * lax.rem(dp + 1, nd)
    nf = nd * grp
    me_f = dp * grp + my_q
    final_mp = dp * grp + my_q
    barrier = pltpu.get_barrier_semaphore()

    def hello(where):
        pl.semaphore_signal(barrier, inc=1, device_id=where, device_id_type=MESH)

    def each(lo, hi, body):
        def step(o, _):
            body(o)
            return 0

        lax.fori_loop(lo, hi, step, 0, unroll=True)

    each(1, nd, lambda o: hello((sec, lax.rem(dp + o, nd), mp)))
    each(1, nm, lambda o: hello((sec, dp, lax.rem(mp + o, nm))))

    @pl.when(sec > 0)
    def _():
        each(0, nm, lambda o: hello((sec - 1, dp, lax.rem(mp + o, nm))))

    @pl.when(is_final)
    def _():
        each(0, ns * nd, lambda o: hello((o // nd, lax.rem(o, nd), grp * lax.rem(o + 1, nd))))

        def other_final(o):
            f = lax.rem(me_f + o, nf)
            hello((last, f // grp, f))

        each(1, nf, other_final)

    @pl.when(jnp.logical_not(is_final))
    def _():
        hello((last, dp, final_mp))

    counts = [len_ref[c // caps, c % caps:c % caps + 1, 0:1] for c in range(ncap)]
    starts = [jnp.zeros((1, 1), F32)]
    for c in range(ncap):
        starts.append(starts[-1] + counts[c])

    def dp_peers(body):
        def step(o, _):
            peer = lax.rem(dp + o, nd)
            body(peer, nd - 1 - o)
            return 0

        lax.fori_loop(1, nd, step, 0)

    def ranked(t):
        y, z = lax.rem(my_group + t // grp + 2, nd), lax.rem(my_q + t + grp // 2, grp)
        return y * grp + z

    def mp_peers(body):
        def one(t):
            peer = ranked(t)
            body(peer, lax.rem(mp - peer - 1 + 2 * nm, nm))

        itself = (nd - 2) * grp + grp // 2
        each(0, itself, one)
        each(itself + 1, nm, one)

    half_rows = pl.ds(pl.multiple_of((my_group // 2) * (batch // 2), batch // 2), batch // 2)

    strip_cols = pl.ds(pl.multiple_of(my_q * piece + lax.rem(my_group, 2) * strip, strip), strip)

    def positions():
        loaded(tok_buf, 0)
        lane = lax.broadcasted_iota(jnp.int32, (8, ncap * slots), 1)
        cap = lane // slots
        pos = jnp.full((8, ncap * slots), -1.0, F32)
        for c in range(ncap):
            at = (lane - c * slots).astype(F32)
            pos = jnp.where(jnp.logical_and(cap == c, at < counts[c]), starts[c] + at, pos)
        pos_buf[...] = pos

    def pack_rows(b):
        row = lax.broadcasted_iota(jnp.int32, (batch // 2, ncap * slots), 0)
        row = (row + (b * batch + (my_group // 2) * (batch // 2))).astype(F32)
        picks = jnp.where(row == pos_buf[0:1], 1.0, 0.0).astype(BF16)
        tokens = tok_buf[...].reshape(ncap * slots, strip)
        x_buf[b, half_rows, strip_cols] = jnp.dot(picks, tokens, preferred_element_type=F32).astype(BF16)

    def pack_send(b):
        here = x_buf.at[b, half_rows, strip_cols]
        mp_peers(lambda peer, slot: send(here, here, cs.at[b], xr.at[b], (sec, dp, peer)))

    ahead = min(2, micro)

    @pl.when(sec == 0)
    def _():
        positions()
        lax.fori_loop(0, ahead, lambda b, _: (pack_rows(b), 0)[1], 0)

    partners = nd - 1 + nm - 1 + jnp.where(sec < last, nm, 0) + jnp.where(mp == root, nd * grp, 0)
    partners = partners + jnp.where(is_final, nf - 1 + ns * nd - 1, 0)
    pl.semaphore_wait(barrier, partners)

    @pl.when(sec == 0)
    def _():
        lax.fori_loop(0, ahead, lambda b, _: (pack_send(b), 0)[1], 0)

    vtiles = w_f2.shape[1] // 128

    def image_layer():
        loaded(patches, 8)
        loaded(w_f1, 1)
        rows = patches[0].astype(F32)
        scale = lax.rsqrt(jnp.mean(rows * rows, -1, keepdims=True) + 1e-05)
        vnormed = (rows * scale * vgain_ref[...]).astype(BF16)
        hidden = jnp.dot(vnormed, w_f1[...], preferred_element_type=F32)
        vinner = (0.5 * hidden * (1.0 + lax.erf(hidden * (0.5 ** 0.5)))).astype(BF16)
        vsum = jnp.sum(vinner.astype(F32), 0, keepdims=True)
        high = vsum.astype(BF16)
        low = (vsum - high.astype(F32)).astype(BF16)
        loaded(w_f2, 2)
        two = jnp.concatenate([jnp.broadcast_to(high, (8, high.shape[1])), jnp.broadcast_to(low, (8, low.shape[1]))], 0)
        prod = jnp.dot(two, w_f2[...], preferred_element_type=F32)
        part = prod[0:1] + prod[8:9] + jnp.where(mp == 0, 1.0, 0.0) * jnp.sum(rows, 0, keepdims=True)
        for i in range(vtiles):
            im1_own[pl.ds(i, 1), :] = part[:, 128 * i:128 * (i + 1)]

        @pl.when(mp != root)
        def _():
            slot = lax.rem(mp - root - 1 + 2 * nm, nm)
            send(im1_own, im1.at[slot], im1_s, im1_r, (sec, dp, root))

        @pl.when(mp == root)
        def _():
            drain(im1, im1_r)
            im2_own[...] = im1_own[...] + jnp.sum(im1[...], 0)

            def to_final(t, _):
                d, q = t // grp, lax.rem(t, grp)
                send(im2_own, im2.at[sec * nd + dp], im2_s, im2_r, (last, d, grp * d + q))
                return 0

            lax.fori_loop(0, nd * grp, to_final, 0)

    @pl.when(sec > 0)
    def _():
        image_layer()

    loaded(w_gu.at[:, pl.ds(0, width)], 3)
    loaded(w_gu.at[:, pl.ds(width, width)], 4)
    gain = gain_ref[0:1, pl.ds(pl.multiple_of(dp * dl, dl), dl)]

    def members(first, width):
        row = lax.broadcasted_iota(jnp.int32, (ncap, width), 0)
        token = (lax.broadcasted_iota(jnp.int32, (ncap, width), 1) + first).astype(F32)
        lo = jnp.zeros((ncap, width), F32)
        hi = jnp.zeros((ncap, width), F32)
        for c in range(ncap):
            lo = jnp.where(row == c, starts[c], lo)
            hi = jnp.where(row == c, starts[c + 1], hi)
        return jnp.where(jnp.logical_and(token >= lo, token < hi), 1.0, 0.0).astype(BF16)

    right, left, far = lax.rem(dp + 1, nd), lax.rem(dp + nd - 1, nd), lax.rem(dp + 2, nd)
    full = 2 * width + 128
    low_cols, high_cols = pl.ds(0, width), pl.ds(width, width + 128)

    def products(rows, out, first_done=None):
        x = rows.astype(F32)
        scaled = (x * gain).astype(BF16)
        if first_done is None:
            out[:, pl.ds(0, 2 * width)] = jnp.dot(
                scaled, w_gu[...], preferred_element_type=F32).astype(BF16)
        else:
            out[:, pl.ds(0, width)] = jnp.dot(
                scaled, w_gu[:, 0:width], preferred_element_type=F32).astype(BF16)
            first_done()
            out[:, pl.ds(width, width)] = jnp.dot(
                scaled, w_gu[:, width:2 * width], preferred_element_type=F32).astype(BF16)
        total = jnp.sum(x * x, -1, keepdims=True)
        high = total.astype(BF16).astype(F32)
        lane = lax.broadcasted_iota(jnp.int32, (x.shape[0], 128), 1)
        out[:, pl.ds(2 * width, 128)] = jnp.where(lane < 64, high, total - high).astype(BF16)

    def stage_far(b):
        @pl.when(sec == 0)
        def _():
            drain(s_buf.at[b], xr.at[b])

        @pl.when(sec > 0)
        def _():
            drain(x_buf.at[b], xr.at[b])

        products(x_buf[b, chunk(far), :], far_buf.at[b], lambda: send(
            far_buf.at[b, :, low_cols], ra_buf.at[b], pa_s.at[b], pa_r.at[b], (sec, right, mp)))
        send(far_buf.at[b, :, high_cols], rb_buf.at[b], pb_s.at[b], pb_r.at[b], (sec, left, mp))

    def stage_near(b):
        near = jnp.concatenate([x_buf[b, chunk(c), :] for c in (right, left, dp)], 0)
        products(near, p_buf.at[b])

    to_right, to_left, to_self = pl.ds(0, length), pl.ds(length, length), pl.ds(2 * length, length)

    def stage_relay(b):
        drain(ra_buf.at[b], pa_r.at[b])
        p_buf[b, to_right, low_cols] = (
            p_buf[b, to_right, low_cols].astype(F32) + ra_buf[b].astype(F32)).astype(BF16)
        send(p_buf.at[b, to_right], r_buf.at[b, 0], pc_s.at[b], pc_r.at[b], (sec, right, mp))
        drain(rb_buf.at[b], pb_r.at[b])
        p_buf[b, to_left, high_cols] = (
            p_buf[b, to_left, high_cols].astype(F32) + rb_buf[b].astype(F32)).astype(BF16)
        send(p_buf.at[b, to_left], r_buf.at[b, 1], pd_s2.at[b], pd_r2.at[b], (sec, left, mp))

    def stage_b(b):
        drain(r_buf.at[b, 0], pc_r.at[b])
        drain(r_buf.at[b, 1], pd_r2.at[b])
        total = p_buf[b, to_self, :].astype(F32) + r_buf[b, 0].astype(F32) + r_buf[b, 1].astype(F32)
        squares = total[:, 2 * width:2 * width + 1] + total[:, 2 * width + 64:2 * width + 65]
        scale = lax.rsqrt(squares * (1.0 / dim) + 1e-05)
        gate = total[:, :width] * scale
        upper = total[:, width:2 * width] * scale
        inner = (gate * jax.nn.sigmoid(gate) * upper).astype(BF16)

        @pl.when(sec < last)
        def _():
            i_buf[b, chunk(dp), :] = inner
            here = i_buf.at[b, chunk(dp)]
            for o in (1, nd - 1, 2):
                send(here, here, iss.at[b], ir.at[nd - 1 - o, b], (sec, lax.rem(dp + o, nd), mp))

        @pl.when(sec == last)
        def _():
            @pl.when(b == 0)
            def _():
                pin[...] = jnp.zeros(pin.shape, F32)
                mean_h[...] = jnp.zeros(mean_h.shape, F32)

            mine = members(b * batch + dp * length, length)
            pin[...] = pin[...] + jnp.dot(mine, inner, preferred_element_type=F32)

            @pl.when(is_final)
            def _():
                mean_h[...] = mean_h[...] + jnp.dot(
                    members(b * batch, batch), x_buf[b, :, cols_z], preferred_element_type=F32)

    def down(b, offsets):
        sources = [lax.rem(dp + o, nd) for o in offsets]
        for o, source in zip(offsets, sources):
            if o:
                drain(i_buf.at[b, chunk(source)], ir.at[o - 1, b])
        out = jnp.dot(jnp.concatenate([i_buf[b, chunk(c), :] for c in sources], 0), w_dn[...],
                      preferred_element_type=F32).astype(BF16)
        for at, source in enumerate(sources):
            q_buf[b, chunk(source), :] = out[at * length:(at + 1) * length]

            def to_owner(o, source=source):
                z = lax.rem(my_q + o + grp // 2, grp)
                owner = source * grp + z

                @pl.when(owner != mp)
                def _():
                    slot = lax.rem(mp - owner - 1 + 2 * nm, nm)
                    send(q_buf.at[b, chunk(source), pl.ds(pl.multiple_of(z * piece, piece), piece)],
                         s_buf.at[b, slot], qs.at[b], qr.at[b], (sec, dp, owner))

            each(0, grp, to_owner)

    def stage_down_near(b):
        down(b, (0, 1, nd - 1))

    def stage_down_far(b):
        down(b, (2,))

    def stage_d(b):
        drain(s_buf.at[b], qr.at[b])
        total = x_buf[b, rows_y, cols_z].astype(F32) + q_buf[b, rows_y, cols_z].astype(F32)
        for i in range(nm - 1):
            total = total + s_buf[b, i].astype(F32)
        h_buf[b] = total.astype(BF16)

        each(0, nm, lambda t: send(
            h_buf.at[b], x_buf.at[b, rows_y, cols_z], hs.at[b], xr.at[b], (sec + 1, dp, ranked(t))))

    def tick(i, _):
        def at(stage, back, also=True):
            @pl.when(jnp.logical_and(also, jnp.logical_and(i >= back, i < micro + back)))
            def _():
                stage(i - back)

        inside = sec < last
        at(stage_far, 0)
        at(stage_b, 1)
        at(stage_near, 0)

        @pl.when(jnp.logical_and(sec == 0, i + 2 < micro))
        def _():
            pack_rows(i + 2)
            pack_send(i + 2)

        at(stage_relay, 0)

        @pl.when(jnp.logical_and(inside, i == 1))
        def _():
            loaded(w_dn, 5)

        at(stage_down_near, 1, inside)
        at(stage_d, 2, inside)
        at(stage_down_far, 1, inside)
        return 0

    lax.fori_loop(0, micro + 2, tick, 0)

    @pl.when(sec == 0)
    def _():
        image_layer()

    loaded(w_tp, 6)
    loaded(w_ip, 7)

    def shares():
        row = lax.broadcasted_iota(jnp.int32, (ncap, 1), 0)
        count = jnp.ones((ncap, 1), F32)
        for c in range(ncap):
            count = jnp.where(row == c, counts[c], count)
        return 1.0 / count

    @pl.when(sec == last)
    def _():
        loaded(w_dn, 5)
        pin_o[nd - 1] = (pin[...] * shares()).astype(BF16)
        dp_peers(lambda peer, slot: send(pin_o.at[nd - 1], pin_o.at[slot], pin_s, pin_r, (sec, peer, mp)))

        @pl.when(is_final)
        def _():
            drain(im2, im2_r)
            imrow[...] = jnp.zeros(imrow.shape, F32)
            for d in range(nd):
                image = im2[d]
                for s in range(1, ns):
                    image = image + im2[s * nd + d]
                for i in range(vtiles):
                    imrow[d:d + 1, 128 * i:128 * (i + 1)] = image[i:i + 1, :]

        drain(pin_o.at[pl.ds(0, nd - 1)], pin_r)
        pooled = pin_o[0].astype(F32)
        for i in range(1, nd):
            pooled = pooled + pin_o[i].astype(F32)
        out = jnp.dot(pooled.astype(BF16), w_dn[...], preferred_element_type=F32)
        for q in range(grp):
            pd[q] = out[:, q * piece:(q + 1) * piece]

        def to_final(q, _):
            target = grp * dp + q

            @pl.when(target != mp)
            def _():
                slot = lax.rem(mp - target - 1 + 2 * nm, nm)
                send(pd.at[q], pdr.at[slot], pd_s.at[q], pd_r, (sec, dp, target))
            return 0

        lax.fori_loop(0, grp, to_final, 0)

    def fan_target(t):
        s, y = t // nd, lax.rem(t, nd)
        target = y * grp + my_q
        return s, target, jnp.logical_and(s == last, target == mp)

    @pl.when(is_final)
    def _():
        drain(pdr, pd_r)
        total = pd[my_q]
        for i in range(nm - 1):
            total = total + pdr[i]
        total = total + mean_h[...] * shares()
        emb[...] = jnp.dot(total.astype(BF16), w_tp[...], preferred_element_type=F32).astype(BF16)

        def to_others(o, _):
            f = lax.rem(me_f + o, nf)
            d, q = f // grp, lax.rem(f, grp)
            send(emb, embr.at[nf - 1 - o], e_s, e_r, (last, d, grp * d + q))
            return 0

        lax.fori_loop(1, nf, to_others, 0)
        pooled = (imrow[...] * (1.0 / (ns * patch_ref.shape[1]))).astype(BF16)
        image = jnp.dot(pooled, w_ip[...], preferred_element_type=F32)
        iu = image * lax.rsqrt(jnp.sum(image * image, -1, keepdims=True) + 1e-06)

        nrow = ncap
        row = lax.broadcasted_iota(jnp.int32, (nrow, 8), 0)
        col = lax.broadcasted_iota(jnp.int32, (nrow, 8), 1)
        gids = jnp.full((nrow, 8), -1, jnp.int32)
        for k in range(ncap):
            gids = jnp.where(row == k, gid_ref[k], gids)
        match = jnp.where(gids == col, 1.0, 0.0)
        real = jnp.where(col < nd, 1.0, 0.0)

        drain(embr, e_r)
        total = emb[...].astype(F32)
        for i in range(nf - 1):
            total = total + embr[i].astype(F32)
        cu = total * lax.rsqrt(jnp.sum(total * total, -1, keepdims=True) + 1e-06)
        logits = jnp.zeros((nrow, 8), F32)
        for j in range(nd):
            logits = jnp.where(col == j, 10.0 * jnp.sum(cu * iu[j:j + 1], -1, keepdims=True), logits)
        expo = jnp.exp(logits) * real
        good = expo * match
        by_row = jnp.sum(expo, 1, keepdims=True)
        by_row = jnp.where(by_row > 0, by_row, 1.0)
        by_col = jnp.sum(expo, 0, keepdims=True)
        by_col = jnp.where(by_col > 0, by_col, 1.0)
        good_col = jnp.sum(good, 0, keepdims=True)
        good_col = jnp.where(good_col > 0, good_col, 1.0)
        def whole(array):
            return jnp.sum(jnp.sum(array, 0, keepdims=True), 1, keepdims=True)

        forward = whole(jnp.log(by_row)) - whole(logits * match * real)
        backward = whole(jnp.log(by_col) - jnp.log(good_col))
        loss = 0.5 * (forward / ncap + backward / nd)
        slope = 5.0 * (expo / by_row - match * real + expo / by_col - good / good_col)
        gcap = jnp.zeros(cu.shape, F32)
        gimg = jnp.zeros((1, cu.shape[1]), F32)
        for j in range(nd):
            gcap = gcap + slope[:, j:j + 1] * iu[j:j + 1]
            gimg = gimg + jnp.where(dp == j, 1.0, 0.0) * jnp.sum(slope[:, j:j + 1] * cu, 0, keepdims=True)
        mine = jnp.zeros((caps, cu.shape[1]), F32)
        for d in range(nd):
            mine = mine + jnp.where(dp == d, 1.0, 0.0) * gcap[caps * d:caps * d + caps]
        outb[0:caps, :] = mine
        outb[caps:caps + 1, :] = gimg
        outb[caps + 1:8, :] = jnp.broadcast_to(loss, (7 - caps, cu.shape[1]))

        def fan(t, _):
            s, target, home = fan_target(t)

            @pl.when(jnp.logical_not(home))
            def _():
                send(outb, outb, out_s.at[t], out_r, (s, dp, target))
            return 0

        lax.fori_loop(0, ns * nd, fan, 0)

    @pl.when(mp != root)
    def _():
        drain(im1_own, im1_s)

    @pl.when(mp == root)
    def _():
        drain(im2, im2_s)

    def sent_batch(b, _):
        @pl.when(sec == 0)
        def _():
            drain(s_buf.at[b], cs.at[b])

        drain(ra_buf.at[b], pa_s.at[b])
        drain(rb_buf.at[b], pb_s.at[b])
        drain(r_buf.at[b, 0], pc_s.at[b])
        drain(r_buf.at[b, 1], pd_s2.at[b])

        @pl.when(sec < last)
        def _():
            drain(i_buf.at[b, pl.ds(0, batch - length)], iss.at[b])
            drain(s_buf.at[b], qs.at[b])
            drain(x_buf.at[b], hs.at[b])
        return 0

    lax.fori_loop(0, micro, sent_batch, 0)

    @pl.when(sec == last)
    def _():
        drain(pin_o.at[pl.ds(0, nd - 1)], pin_s)

        def sent_pd(q, _):
            @pl.when(grp * dp + q != mp)
            def _():
                drain(pd.at[0], pd_s.at[q])
            return 0

        lax.fori_loop(0, grp, sent_pd, 0)

    @pl.when(jnp.logical_not(is_final))
    def _():
        drain(outb, out_r)

    loss_ref[...] = outb[caps + 1:caps + 2, 0:128]
    gcap_ref[...] = outb[0:caps, :]
    gimg_ref[...] = outb[caps:caps + 1, :]

    @pl.when(is_final)
    def _():
        drain(embr, e_s)

        def sent_fan(t, _):
            _, _, home = fan_target(t)

            @pl.when(jnp.logical_not(home))
            def _():
                drain(outb, out_s.at[t])
            return 0

        lax.fori_loop(0, ns * nd, sent_fan, 0)


def front_kernel(sizes, rooms, tok_ref, len_ref, strips_ref, lens_ref, which_ref, lens, len_s, len_r, tok_s, tok_r, home_s):
    ns, nd, nm = sizes
    grp = nm // nd
    caps, _, piece = tok_ref.shape
    strip = piece // 2
    sec, dp, mp = lax.axis_index("section"), lax.axis_index("dp"), lax.axis_index("mp")
    my_group, my_q = mp // grp, lax.rem(mp, grp)
    home = jnp.logical_and(sec == 0, jnp.logical_and(my_group == 0, dp == 0))
    want_sec = my_group
    barrier = pltpu.get_barrier_semaphore()

    def hello(where):
        pl.semaphore_signal(barrier, inc=1, device_id=where, device_id_type=MESH)

    for o in range(1, nd):
        hello((sec, lax.rem(dp + o, nd), mp))

    @pl.when(sec == 0)
    def _():
        for d in range(nd):
            @pl.when(jnp.logical_not(jnp.logical_and(want_sec == 0, jnp.logical_and(dp == 0, d == 0))))
            def _():
                hello((want_sec, d, dp * grp + my_q))

    row = lax.broadcasted_iota(jnp.int32, (8, 128), 0)
    mine = jnp.zeros((8, 128), F32)
    for i in range(caps):
        mine = jnp.where(row == i, len_ref[i].astype(F32), mine)
    lens[dp] = mine

    source = tok_ref.at[:, :, pl.ds(pl.multiple_of(lax.rem(sec, 2) * strip, strip), strip)]
    slab = strips_ref.at[dp]

    @pl.when(home)
    def _():
        pltpu.make_async_copy(source, slab, home_s).start()
        pl.semaphore_wait(barrier, nd - 1)

    @pl.when(jnp.logical_not(home))
    def _():
        pl.semaphore_wait(barrier, nd)

    for o in range(1, nd):
        pltpu.make_async_remote_copy(
            src_ref=lens.at[dp], dst_ref=lens.at[dp], send_sem=len_s.at[o - 1], recv_sem=len_r.at[nd - 1 - o],
            device_id=(sec, lax.rem(dp + o, nd), mp), device_id_type=MESH).start()

    @pl.when(jnp.logical_not(home))
    def _():
        pltpu.make_async_remote_copy(
            src_ref=source, dst_ref=slab, send_sem=tok_s, recv_sem=tok_r.at[dp],
            device_id=(0, my_group, sec * grp + my_q), device_id_type=MESH).start()

    for o in range(1, nd):
        other = lens.at[lax.rem(dp + o, nd)]
        pltpu.make_async_copy(other, other, len_r.at[o - 1]).wait()
    lens_ref[...] = lens[...]
    counted = jnp.sum(lens[:, :, 0:1])
    which = jnp.int32(0)
    for room in rooms[:-1]:
        which = which + (counted > room).astype(jnp.int32)
    which_ref[0, 0] = which

    @pl.when(sec == 0)
    def _():
        for d in range(nd):
            here = strips_ref.at[d]
            itself = jnp.logical_and(want_sec == 0, jnp.logical_and(dp == 0, d == 0))

            @pl.when(itself)
            def _():
                pltpu.make_async_copy(here, here, home_s).wait()

            @pl.when(jnp.logical_not(itself))
            def _():
                pltpu.make_async_copy(here, here, tok_r.at[d]).wait()

    for o in range(1, nd):
        pltpu.make_async_copy(lens.at[dp], lens.at[dp], len_s.at[o - 1]).wait()

    @pl.when(jnp.logical_not(home))
    def _():
        pltpu.make_async_copy(slab, slab, tok_s).wait()


def front(sizes, plans, tokens, lengths):
    nd = sizes[1]
    caps, slots, piece = tokens.shape
    dma = pltpu.SemaphoreType.DMA
    return pl.pallas_call(
        functools.partial(front_kernel, sizes, [micro * batch for micro, batch in plans]),
        out_shape=(
            jax.ShapeDtypeStruct((nd, caps, slots, piece // 2), BF16),
            jax.ShapeDtypeStruct((nd, 8, 128), F32),
            jax.ShapeDtypeStruct((1, 1), jnp.int32),
        ),
        in_specs=[pl.BlockSpec(memory_space=pl.ANY), pl.BlockSpec(memory_space=pltpu.SMEM)],
        out_specs=(pl.BlockSpec(memory_space=pl.ANY), pl.BlockSpec(memory_space=pltpu.VMEM),
                   pl.BlockSpec(memory_space=pltpu.SMEM)),
        scratch_shapes=[
            pltpu.VMEM((nd, 8, 128), F32),
            dma((nd - 1,)), dma((nd - 1,)), dma, dma((nd,)), dma,
        ],
        compiler_params=pltpu.CompilerParams(
            collective_id=1, has_side_effects=True, vmem_limit_bytes=60 * 2 ** 20),
        name="front",
    )(tokens, lengths)


def per_device(
    sizes, plans,
    caption_tokens, caption_lengths, group_ids, text_gain, text_gate, text_up, text_down,
    text_proj, image_patches, image_gain, image_fc1, image_fc2, image_proj,
):
    strips, lens, which = front(sizes, plans, caption_tokens, caption_lengths)
    operands = (
        strips, lens, group_ids, text_gain, text_gate, text_up, text_down,
        text_proj, image_patches, image_gain.reshape(1, -1), image_fc1, image_fc2, image_proj,
    )
    branches = [functools.partial(towers, sizes, plan, 2 + i) for i, plan in enumerate(plans)]
    return lax.switch(which[0, 0], branches, *operands)


def towers(
    sizes, plan, barrier_id,
    strips, caption_lengths, group_ids, text_gain, text_gate, text_up, text_down,
    text_proj, image_patches, image_gain, image_fc1, image_fc2, image_proj,
):
    ns, nd, nm = sizes
    grp = nm // nd
    micro, batch = plan
    _, caps, slots, strip = strips.shape
    piece = 2 * strip
    length = batch // nd
    ncap = nd * caps
    dl, width = text_gate.shape[1], text_gate.shape[2]
    dv, hv = image_fc1.shape
    embed = text_proj.shape[1]
    nf = nd * grp
    any_spec = pl.BlockSpec(memory_space=pl.ANY)
    vmem = pl.BlockSpec(memory_space=pltpu.VMEM)
    smem = pl.BlockSpec(memory_space=pltpu.SMEM)
    dma = pltpu.SemaphoreType.DMA
    loss, gcap, gimg = pl.pallas_call(
        functools.partial(kernel, sizes),
        out_shape=(
            jax.ShapeDtypeStruct((1, 128), F32),
            jax.ShapeDtypeStruct((caps, embed), F32),
            jax.ShapeDtypeStruct((1, embed), F32),
        ),
        in_specs=[any_spec, vmem, smem, vmem, any_spec, any_spec, any_spec, any_spec,
                  any_spec, vmem, any_spec, any_spec, any_spec],
        out_specs=(vmem, vmem, vmem),
        scratch_shapes=[
            pltpu.VMEM((dl, 2 * width), BF16),
            pltpu.VMEM((width, dl), BF16),
            pltpu.VMEM((piece, embed), BF16),
            pltpu.VMEM((dv, hv), BF16),
            pltpu.VMEM((hv, dv), BF16),
            pltpu.VMEM((dv, embed), BF16),
            pltpu.VMEM(image_patches.shape, BF16),
            pltpu.VMEM((nd, caps, slots, piece // 2), BF16),
            pltpu.VMEM((8, ncap * slots), F32),
            pltpu.VMEM((micro, batch, dl), BF16),
            pltpu.VMEM((micro, length, 2 * width + 128), BF16),
            pltpu.VMEM((micro, 3 * length, 2 * width + 128), BF16),
            pltpu.VMEM((micro, length, width), BF16),
            pltpu.VMEM((micro, length, width + 128), BF16),
            pltpu.VMEM((micro, 2, length, 2 * width + 128), BF16),
            pltpu.VMEM((micro, batch, width), BF16),
            pltpu.VMEM((micro, batch, dl), BF16),
            pltpu.VMEM((micro, nm - 1, length, piece), BF16),
            pltpu.VMEM((micro, length, piece), BF16),
            pltpu.VMEM((nm - 1, dv // 128, 128), F32),
            pltpu.VMEM((dv // 128, 128), F32),
            pltpu.VMEM((ns * nd, dv // 128, 128), F32),
            pltpu.VMEM((dv // 128, 128), F32),
            pltpu.VMEM((8, dv), F32),
            pltpu.VMEM((ncap, piece), F32),
            pltpu.VMEM((ncap, width), F32),
            pltpu.VMEM((nd, ncap, width), BF16),
            pltpu.VMEM((grp, ncap, piece), F32),
            pltpu.VMEM((nm - 1, ncap, piece), F32),
            pltpu.VMEM((ncap, embed), BF16),
            pltpu.VMEM((nf - 1, ncap, embed), BF16),
            pltpu.VMEM((8, embed), F32),
            dma((9,)), *([dma((micro,))] * 13), dma((nd - 1, micro)),
            dma((micro,)), dma, dma, dma, dma, dma, dma, dma((grp,)), dma, dma, dma, dma((ns * nd,)), dma,
        ],
        compiler_params=pltpu.CompilerParams(
            collective_id=barrier_id, has_side_effects=True, vmem_limit_bytes=60 * 2 ** 20),
        name=f"towers_{micro}_{batch}",
    )(
        strips, caption_lengths, group_ids, text_gain, text_gate, text_up, text_down,
        text_proj, image_patches, image_gain, image_fc1, image_fc2, image_proj,
    )
    return loss[0, 0], gcap, gimg


def solution(mesh):
    sizes = tuple(mesh.shape[axis] for axis in ("section", "dp", "mp"))
    return jax.shard_map(
        functools.partial(per_device, sizes, PLANS),
        mesh=mesh,
        in_specs=(
            P("dp", None, "mp"),
            P("dp"),
            P(),
            P("section", None),
            P("section", "dp", "mp"),
            P("section", "dp", "mp"),
            P("section", "mp", "dp"),
            P("mp", None),
            P("dp", "section", None),
            P(),
            P(None, "mp"),
            P("mp", None),
            P(),
        ),
        out_specs=(P(), P("dp", None), P("dp", None)),
        check_vma=False,
    )
```

```python
import functools

import jax
import jax.numpy as jnp
from jax import lax
from jax.experimental import pallas as pl
from jax.experimental.pallas import tpu as pltpu
from jax.sharding import PartitionSpec as P

MESH = pl.DeviceIdType.MESH
PLANS = ((3, 128), (4, 128), (3, 192), (5, 128), (4, 192), (4, 256))
BF16 = jnp.bfloat16
F32 = jnp.float32


def kernel(
    sizes,
    tok_ref, len_ref, gid_ref, gain_ref, gate_ref, up_ref, down_ref, tproj_ref,
    patch_ref, vgain_ref, fc1_ref, fc2_ref, iproj_ref,
    loss_ref, gcap_ref, gimg_ref,
    w_gu, w_dn, w_tp, w_f1, w_f2, w_ip, patches,
    tok_buf, pos_buf, x_buf, far_buf, p_buf, ra_buf, rb_buf, r_buf, i_buf, q_buf, s_buf, h_buf,
    im1, im1_own, im2, im2_own, imrow, mean_h,
    pin, pin_o, pd, pdr, emb, embr, outb,
    wsem, xr, pa_s, pa_r, pb_s, pb_r, pc_s, pc_r, pd_s2, pd_r2,
    iss, qs, qr, hs, ir,
    cs, im1_s, im1_r, im2_s, im2_r, pin_s, pin_r, pd_s, pd_r, e_s, e_r, out_s, out_r,
):
    ns, nd, nm = sizes
    grp = nm // nd
    _, caps, slots, strip = tok_ref.shape
    piece = 2 * strip
    ncap = nd * caps
    micro, batch, dl = x_buf.shape
    length = batch // nd
    width = gate_ref.shape[2]
    dim = dl * nd
    sec, dp, mp = lax.axis_index("section"), lax.axis_index("dp"), lax.axis_index("mp")
    last = ns - 1
    my_group = mp // grp
    my_q = lax.rem(mp, grp)
    is_final = jnp.logical_and(sec == last, my_group == dp)

    def send(src, dst, s_sem, r_sem, where):
        pltpu.make_async_remote_copy(
            src_ref=src, dst_ref=dst, send_sem=s_sem, recv_sem=r_sem,
            device_id=where, device_id_type=MESH,
        ).start()

    def drain(ref, sem):
        pltpu.make_async_copy(ref, ref, sem).wait()

    def load(src, dst, index):
        pltpu.make_async_copy(src, dst, wsem.at[index]).start()

    def loaded(dst, index):
        pltpu.make_async_copy(dst, dst, wsem.at[index]).wait()

    def chunk(d):
        return pl.ds(pl.multiple_of(d * length, length), length)

    rows_y = pl.ds(pl.multiple_of(my_group * length, length), length)
    cols_z = pl.ds(pl.multiple_of(my_q * piece, piece), piece)

    @pl.when(sec == 0)
    def _():
        load(tok_ref, tok_buf, 0)

    load(gate_ref.at[0], w_gu.at[:, pl.ds(0, width)], 3)
    load(up_ref.at[0], w_gu.at[:, pl.ds(width, width)], 4)
    load(patch_ref, patches, 8)
    load(fc1_ref, w_f1, 1)
    load(fc2_ref, w_f2, 2)
    load(down_ref.at[0], w_dn, 5)
    load(tproj_ref, w_tp, 6)
    load(iproj_ref, w_ip, 7)

    root = grp * lax.rem(dp + 1, nd)
    nf = nd * grp
    me_f = dp * grp + my_q
    final_mp = dp * grp + my_q
    barrier = pltpu.get_barrier_semaphore()

    def hello(where):
        pl.semaphore_signal(barrier, inc=1, device_id=where, device_id_type=MESH)

    def each(lo, hi, body):
        def step(o, _):
            body(o)
            return 0

        lax.fori_loop(lo, hi, step, 0, unroll=True)

    each(1, nd, lambda o: hello((sec, lax.rem(dp + o, nd), mp)))
    each(1, nm, lambda o: hello((sec, dp, lax.rem(mp + o, nm))))

    @pl.when(sec > 0)
    def _():
        each(0, nm, lambda o: hello((sec - 1, dp, lax.rem(mp + o, nm))))

    @pl.when(is_final)
    def _():
        each(0, ns * nd, lambda o: hello((o // nd, lax.rem(o, nd), grp * lax.rem(o + 1, nd))))

        def other_final(o):
            f = lax.rem(me_f + o, nf)
            hello((last, f // grp, f))

        each(1, nf, other_final)

    @pl.when(jnp.logical_not(is_final))
    def _():
        hello((last, dp, final_mp))

    counts = [len_ref[c // caps, c % caps:c % caps + 1, 0:1] for c in range(ncap)]
    starts = [jnp.zeros((1, 1), F32)]
    for c in range(ncap):
        starts.append(starts[-1] + counts[c])

    def dp_peers(body):
        def step(o, _):
            peer = lax.rem(dp + o, nd)
            body(peer, nd - 1 - o)
            return 0

        lax.fori_loop(1, nd, step, 0)

    def ranked(t):
        y, z = lax.rem(my_group + t // grp + 2, nd), lax.rem(my_q + t + grp // 2, grp)
        return y * grp + z

    def mp_peers(body):
        def one(t):
            peer = ranked(t)
            body(peer, lax.rem(mp - peer - 1 + 2 * nm, nm))

        itself = (nd - 2) * grp + grp // 2
        each(0, itself, one)
        each(itself + 1, nm, one)

    half_rows = pl.ds(pl.multiple_of((my_group // 2) * (batch // 2), batch // 2), batch // 2)

    strip_cols = pl.ds(pl.multiple_of(my_q * piece + lax.rem(my_group, 2) * strip, strip), strip)

    def positions():
        loaded(tok_buf, 0)
        lane = lax.broadcasted_iota(jnp.int32, (8, ncap * slots), 1)
        cap = lane // slots
        pos = jnp.full((8, ncap * slots), -1.0, F32)
        for c in range(ncap):
            at = (lane - c * slots).astype(F32)
            pos = jnp.where(jnp.logical_and(cap == c, at < counts[c]), starts[c] + at, pos)
        pos_buf[...] = pos

    def pack_rows(b):
        row = lax.broadcasted_iota(jnp.int32, (batch // 2, ncap * slots), 0)
        row = (row + (b * batch + (my_group // 2) * (batch // 2))).astype(F32)
        picks = jnp.where(row == pos_buf[0:1], 1.0, 0.0).astype(BF16)
        tokens = tok_buf[...].reshape(ncap * slots, strip)
        x_buf[b, half_rows, strip_cols] = jnp.dot(picks, tokens, preferred_element_type=F32).astype(BF16)

    def pack_send(b):
        here = x_buf.at[b, half_rows, strip_cols]
        mp_peers(lambda peer, slot: send(here, here, cs.at[b], xr.at[b], (sec, dp, peer)))

    ahead = min(2, micro)

    @pl.when(sec == 0)
    def _():
        positions()
        lax.fori_loop(0, ahead, lambda b, _: (pack_rows(b), 0)[1], 0)

    partners = nd - 1 + nm - 1 + jnp.where(sec < last, nm, 0) + jnp.where(mp == root, nd * grp, 0)
    partners = partners + jnp.where(is_final, nf - 1 + ns * nd - 1, 0)
    pl.semaphore_wait(barrier, partners)

    @pl.when(sec == 0)
    def _():
        lax.fori_loop(0, ahead, lambda b, _: (pack_send(b), 0)[1], 0)

    vtiles = w_f2.shape[1] // 128

    def image_layer():
        loaded(patches, 8)
        loaded(w_f1, 1)
        rows = patches[0].astype(F32)
        scale = lax.rsqrt(jnp.mean(rows * rows, -1, keepdims=True) + 1e-05)
        vnormed = (rows * scale * vgain_ref[...]).astype(BF16)
        hidden = jnp.dot(vnormed, w_f1[...], preferred_element_type=F32)
        vinner = (0.5 * hidden * (1.0 + lax.erf(hidden * (0.5 ** 0.5)))).astype(BF16)
        vsum = jnp.sum(vinner.astype(F32), 0, keepdims=True)
        high = vsum.astype(BF16)
        low = (vsum - high.astype(F32)).astype(BF16)
        loaded(w_f2, 2)
        two = jnp.concatenate([jnp.broadcast_to(high, (8, high.shape[1])), jnp.broadcast_to(low, (8, low.shape[1]))], 0)
        prod = jnp.dot(two, w_f2[...], preferred_element_type=F32)
        part = prod[0:1] + prod[8:9] + jnp.where(mp == 0, 1.0, 0.0) * jnp.sum(rows, 0, keepdims=True)
        for i in range(vtiles):
            im1_own[pl.ds(i, 1), :] = part[:, 128 * i:128 * (i + 1)]

        @pl.when(mp != root)
        def _():
            slot = lax.rem(mp - root - 1 + 2 * nm, nm)
            send(im1_own, im1.at[slot], im1_s, im1_r, (sec, dp, root))

        @pl.when(mp == root)
        def _():
            drain(im1, im1_r)
            im2_own[...] = im1_own[...] + jnp.sum(im1[...], 0)

            def to_final(t, _):
                d, q = t // grp, lax.rem(t, grp)
                send(im2_own, im2.at[sec * nd + dp], im2_s, im2_r, (last, d, grp * d + q))
                return 0

            lax.fori_loop(0, nd * grp, to_final, 0)

    @pl.when(sec > 0)
    def _():
        image_layer()

    loaded(w_gu.at[:, pl.ds(0, width)], 3)
    loaded(w_gu.at[:, pl.ds(width, width)], 4)
    gain = gain_ref[0:1, pl.ds(pl.multiple_of(dp * dl, dl), dl)]

    def members(first, width):
        row = lax.broadcasted_iota(jnp.int32, (ncap, width), 0)
        token = (lax.broadcasted_iota(jnp.int32, (ncap, width), 1) + first).astype(F32)
        lo = jnp.zeros((ncap, width), F32)
        hi = jnp.zeros((ncap, width), F32)
        for c in range(ncap):
            lo = jnp.where(row == c, starts[c], lo)
            hi = jnp.where(row == c, starts[c + 1], hi)
        return jnp.where(jnp.logical_and(token >= lo, token < hi), 1.0, 0.0).astype(BF16)

    right, left, far = lax.rem(dp + 1, nd), lax.rem(dp + nd - 1, nd), lax.rem(dp + 2, nd)
    full = 2 * width + 128
    low_cols, high_cols = pl.ds(0, width), pl.ds(width, width + 128)

    def products(rows, out, first_done=None):
        x = rows.astype(F32)
        scaled = (x * gain).astype(BF16)
        if first_done is None:
            out[:, pl.ds(0, 2 * width)] = jnp.dot(
                scaled, w_gu[...], preferred_element_type=F32).astype(BF16)
        else:
            out[:, pl.ds(0, width)] = jnp.dot(
                scaled, w_gu[:, 0:width], preferred_element_type=F32).astype(BF16)
            first_done()
            out[:, pl.ds(width, width)] = jnp.dot(
                scaled, w_gu[:, width:2 * width], preferred_element_type=F32).astype(BF16)
        total = jnp.sum(x * x, -1, keepdims=True)
        high = total.astype(BF16).astype(F32)
        lane = lax.broadcasted_iota(jnp.int32, (x.shape[0], 128), 1)
        out[:, pl.ds(2 * width, 128)] = jnp.where(lane < 64, high, total - high).astype(BF16)

    def stage_far(b):
        @pl.when(sec == 0)
        def _():
            drain(s_buf.at[b], xr.at[b])

        @pl.when(sec > 0)
        def _():
            drain(x_buf.at[b], xr.at[b])

        products(x_buf[b, chunk(far), :], far_buf.at[b], lambda: send(
            far_buf.at[b, :, low_cols], ra_buf.at[b], pa_s.at[b], pa_r.at[b], (sec, right, mp)))
        send(far_buf.at[b, :, high_cols], rb_buf.at[b], pb_s.at[b], pb_r.at[b], (sec, left, mp))

    def stage_near(b):
        near = jnp.concatenate([x_buf[b, chunk(c), :] for c in (right, left, dp)], 0)
        products(near, p_buf.at[b])

    to_right, to_left, to_self = pl.ds(0, length), pl.ds(length, length), pl.ds(2 * length, length)

    def stage_relay(b):
        drain(ra_buf.at[b], pa_r.at[b])
        p_buf[b, to_right, low_cols] = (
            p_buf[b, to_right, low_cols].astype(F32) + ra_buf[b].astype(F32)).astype(BF16)
        send(p_buf.at[b, to_right], r_buf.at[b, 0], pc_s.at[b], pc_r.at[b], (sec, right, mp))
        drain(rb_buf.at[b], pb_r.at[b])
        p_buf[b, to_left, high_cols] = (
            p_buf[b, to_left, high_cols].astype(F32) + rb_buf[b].astype(F32)).astype(BF16)
        send(p_buf.at[b, to_left], r_buf.at[b, 1], pd_s2.at[b], pd_r2.at[b], (sec, left, mp))

    def stage_b(b):
        drain(r_buf.at[b, 0], pc_r.at[b])
        drain(r_buf.at[b, 1], pd_r2.at[b])
        total = p_buf[b, to_self, :].astype(F32) + r_buf[b, 0].astype(F32) + r_buf[b, 1].astype(F32)
        squares = total[:, 2 * width:2 * width + 1] + total[:, 2 * width + 64:2 * width + 65]
        scale = lax.rsqrt(squares * (1.0 / dim) + 1e-05)
        gate = total[:, :width] * scale
        upper = total[:, width:2 * width] * scale
        inner = (gate * jax.nn.sigmoid(gate) * upper).astype(BF16)

        @pl.when(sec < last)
        def _():
            i_buf[b, chunk(dp), :] = inner
            here = i_buf.at[b, chunk(dp)]
            for o in (1, nd - 1, 2):
                send(here, here, iss.at[b], ir.at[nd - 1 - o, b], (sec, lax.rem(dp + o, nd), mp))

        @pl.when(sec == last)
        def _():
            @pl.when(b == 0)
            def _():
                pin[...] = jnp.zeros(pin.shape, F32)
                mean_h[...] = jnp.zeros(mean_h.shape, F32)

            mine = members(b * batch + dp * length, length)
            pin[...] = pin[...] + jnp.dot(mine, inner, preferred_element_type=F32)

    def down(b, offsets):
        sources = [lax.rem(dp + o, nd) for o in offsets]
        for o, source in zip(offsets, sources):
            if o:
                drain(i_buf.at[b, chunk(source)], ir.at[o - 1, b])
        out = jnp.dot(jnp.concatenate([i_buf[b, chunk(c), :] for c in sources], 0), w_dn[...],
                      preferred_element_type=F32).astype(BF16)
        for at, source in enumerate(sources):
            q_buf[b, chunk(source), :] = out[at * length:(at + 1) * length]

            def to_owner(o, source=source):
                z = lax.rem(my_q + o + grp // 2, grp)
                owner = source * grp + z

                @pl.when(owner != mp)
                def _():
                    slot = lax.rem(mp - owner - 1 + 2 * nm, nm)
                    send(q_buf.at[b, chunk(source), pl.ds(pl.multiple_of(z * piece, piece), piece)],
                         s_buf.at[b, slot], qs.at[b], qr.at[b], (sec, dp, owner))

            each(0, grp, to_owner)

    def stage_down_near(b):
        down(b, (0, 1, nd - 1))

    def stage_down_far(b):
        down(b, (2,))

    def stage_d(b):
        drain(s_buf.at[b], qr.at[b])
        total = x_buf[b, rows_y, cols_z].astype(F32) + q_buf[b, rows_y, cols_z].astype(F32)
        for i in range(nm - 1):
            total = total + s_buf[b, i].astype(F32)
        h_buf[b] = total.astype(BF16)

        each(0, nm, lambda t: send(
            h_buf.at[b], x_buf.at[b, rows_y, cols_z], hs.at[b], xr.at[b], (sec + 1, dp, ranked(t))))

    def tick(i, _):
        def at(stage, back, also=True):
            @pl.when(jnp.logical_and(also, jnp.logical_and(i >= back, i < micro + back)))
            def _():
                stage(i - back)

        inside = sec < last
        at(stage_far, 0)
        at(stage_b, 1)
        at(stage_near, 0)

        @pl.when(jnp.logical_and(sec == 0, i + 2 < micro))
        def _():
            pack_rows(i + 2)
            pack_send(i + 2)

        at(stage_relay, 0)

        @pl.when(jnp.logical_and(inside, i == 1))
        def _():
            loaded(w_dn, 5)

        at(stage_down_near, 1, inside)
        at(stage_d, 2, inside)
        at(stage_down_far, 1, inside)
        return 0

    lax.fori_loop(0, micro + 2, tick, 0)

    @pl.when(sec == 0)
    def _():
        image_layer()

    loaded(w_tp, 6)
    loaded(w_ip, 7)

    def shares():
        row = lax.broadcasted_iota(jnp.int32, (ncap, 1), 0)
        count = jnp.ones((ncap, 1), F32)
        for c in range(ncap):
            count = jnp.where(row == c, counts[c], count)
        return 1.0 / count

    @pl.when(sec == last)
    def _():
        loaded(w_dn, 5)
        pin_o[nd - 1] = (pin[...] * shares()).astype(BF16)
        dp_peers(lambda peer, slot: send(pin_o.at[nd - 1], pin_o.at[slot], pin_s, pin_r, (sec, peer, mp)))

        @pl.when(is_final)
        def _():
            def mean_of(b, _):
                mean_h[...] = mean_h[...] + jnp.dot(
                    members(b * batch, batch), x_buf[b, :, cols_z], preferred_element_type=F32)
                return 0

            lax.fori_loop(0, micro, mean_of, 0)
            drain(im2, im2_r)
            imrow[...] = jnp.zeros(imrow.shape, F32)
            for d in range(nd):
                image = im2[d]
                for s in range(1, ns):
                    image = image + im2[s * nd + d]
                for i in range(vtiles):
                    imrow[d:d + 1, 128 * i:128 * (i + 1)] = image[i:i + 1, :]

        drain(pin_o.at[pl.ds(0, nd - 1)], pin_r)
        pooled = pin_o[0].astype(F32)
        for i in range(1, nd):
            pooled = pooled + pin_o[i].astype(F32)
        out = jnp.dot(pooled.astype(BF16), w_dn[...], preferred_element_type=F32)
        for q in range(grp):
            pd[q] = out[:, q * piece:(q + 1) * piece]

        def to_final(q, _):
            target = grp * dp + q

            @pl.when(target != mp)
            def _():
                slot = lax.rem(mp - target - 1 + 2 * nm, nm)
                send(pd.at[q], pdr.at[slot], pd_s.at[q], pd_r, (sec, dp, target))
            return 0

        lax.fori_loop(0, grp, to_final, 0, unroll=True)

    def fan_target(t):
        s, y = t // nd, lax.rem(t, nd)
        target = y * grp + my_q
        return s, target, jnp.logical_and(s == last, target == mp)

    @pl.when(is_final)
    def _():
        drain(pdr, pd_r)
        total = pd[my_q]
        for i in range(nm - 1):
            total = total + pdr[i]
        total = total + mean_h[...] * shares()
        emb[...] = jnp.dot(total.astype(BF16), w_tp[...], preferred_element_type=F32).astype(BF16)

        def to_others(o, _):
            f = lax.rem(me_f + o, nf)
            d, q = f // grp, lax.rem(f, grp)
            send(emb, embr.at[nf - 1 - o], e_s, e_r, (last, d, grp * d + q))
            return 0

        lax.fori_loop(1, nf, to_others, 0, unroll=True)
        pooled = (imrow[...] * (1.0 / (ns * patch_ref.shape[1]))).astype(BF16)
        image = jnp.dot(pooled, w_ip[...], preferred_element_type=F32)
        iu = image * lax.rsqrt(jnp.sum(image * image, -1, keepdims=True) + 1e-06)

        nrow = ncap
        row = lax.broadcasted_iota(jnp.int32, (nrow, 8), 0)
        col = lax.broadcasted_iota(jnp.int32, (nrow, 8), 1)
        gids = jnp.full((nrow, 8), -1, jnp.int32)
        for k in range(ncap):
            gids = jnp.where(row == k, gid_ref[k], gids)
        match = jnp.where(gids == col, 1.0, 0.0)
        real = jnp.where(col < nd, 1.0, 0.0)

        drain(embr, e_r)
        total = emb[...].astype(F32)
        for i in range(nf - 1):
            total = total + embr[i].astype(F32)
        cu = total * lax.rsqrt(jnp.sum(total * total, -1, keepdims=True) + 1e-06)
        logits = jnp.zeros((nrow, 8), F32)
        for j in range(nd):
            logits = jnp.where(col == j, 10.0 * jnp.sum(cu * iu[j:j + 1], -1, keepdims=True), logits)
        expo = jnp.exp(logits) * real
        good = expo * match
        by_row = jnp.sum(expo, 1, keepdims=True)
        by_row = jnp.where(by_row > 0, by_row, 1.0)
        by_col = jnp.sum(expo, 0, keepdims=True)
        by_col = jnp.where(by_col > 0, by_col, 1.0)
        good_col = jnp.sum(good, 0, keepdims=True)
        good_col = jnp.where(good_col > 0, good_col, 1.0)
        def whole(array):
            return jnp.sum(jnp.sum(array, 0, keepdims=True), 1, keepdims=True)

        forward = whole(jnp.log(by_row)) - whole(logits * match * real)
        backward = whole(jnp.log(by_col) - jnp.log(good_col))
        loss = 0.5 * (forward / ncap + backward / nd)
        slope = 5.0 * (expo / by_row - match * real + expo / by_col - good / good_col)
        gcap = jnp.zeros(cu.shape, F32)
        gimg = jnp.zeros((1, cu.shape[1]), F32)
        for j in range(nd):
            gcap = gcap + slope[:, j:j + 1] * iu[j:j + 1]
            gimg = gimg + jnp.where(dp == j, 1.0, 0.0) * jnp.sum(slope[:, j:j + 1] * cu, 0, keepdims=True)
        mine = jnp.zeros((caps, cu.shape[1]), F32)
        for d in range(nd):
            mine = mine + jnp.where(dp == d, 1.0, 0.0) * gcap[caps * d:caps * d + caps]
        outb[0:caps, :] = mine
        outb[caps:caps + 1, :] = gimg
        outb[caps + 1:8, :] = jnp.broadcast_to(loss, (7 - caps, cu.shape[1]))

        def fan(t, _):
            s, target, home = fan_target(t)

            @pl.when(jnp.logical_not(home))
            def _():
                send(outb, outb, out_s.at[t], out_r, (s, dp, target))
            return 0

        lax.fori_loop(0, ns * nd, fan, 0, unroll=True)

    @pl.when(mp != root)
    def _():
        drain(im1_own, im1_s)

    @pl.when(mp == root)
    def _():
        drain(im2, im2_s)

    def sent_batch(b, _):
        @pl.when(sec == 0)
        def _():
            drain(s_buf.at[b], cs.at[b])

        drain(ra_buf.at[b], pa_s.at[b])
        drain(rb_buf.at[b], pb_s.at[b])
        drain(r_buf.at[b, 0], pc_s.at[b])
        drain(r_buf.at[b, 1], pd_s2.at[b])

        @pl.when(sec < last)
        def _():
            drain(i_buf.at[b, pl.ds(0, batch - length)], iss.at[b])
            drain(s_buf.at[b], qs.at[b])
            drain(x_buf.at[b], hs.at[b])
        return 0

    lax.fori_loop(0, micro, sent_batch, 0)

    @pl.when(sec == last)
    def _():
        drain(pin_o.at[pl.ds(0, nd - 1)], pin_s)

        def sent_pd(q, _):
            @pl.when(grp * dp + q != mp)
            def _():
                drain(pd.at[0], pd_s.at[q])
            return 0

        lax.fori_loop(0, grp, sent_pd, 0)

    @pl.when(jnp.logical_not(is_final))
    def _():
        drain(outb, out_r)

    loss_ref[...] = outb[caps + 1:caps + 2, 0:128]
    gcap_ref[...] = outb[0:caps, :]
    gimg_ref[...] = outb[caps:caps + 1, :]

    @pl.when(is_final)
    def _():
        drain(embr, e_s)

        def sent_fan(t, _):
            _, _, home = fan_target(t)

            @pl.when(jnp.logical_not(home))
            def _():
                drain(outb, out_s.at[t])
            return 0

        lax.fori_loop(0, ns * nd, sent_fan, 0)


def front_kernel(sizes, rooms, tok_ref, len_ref, strips_ref, lens_ref, which_ref, lens, len_s, len_r, tok_s, tok_r, home_s):
    ns, nd, nm = sizes
    grp = nm // nd
    caps, _, piece = tok_ref.shape
    strip = piece // 2
    sec, dp, mp = lax.axis_index("section"), lax.axis_index("dp"), lax.axis_index("mp")
    my_group, my_q = mp // grp, lax.rem(mp, grp)
    home = jnp.logical_and(sec == 0, jnp.logical_and(my_group == 0, dp == 0))
    want_sec = my_group
    barrier = pltpu.get_barrier_semaphore()

    def hello(where):
        pl.semaphore_signal(barrier, inc=1, device_id=where, device_id_type=MESH)

    for o in range(1, nd):
        hello((sec, lax.rem(dp + o, nd), mp))

    @pl.when(sec == 0)
    def _():
        for d in range(nd):
            @pl.when(jnp.logical_not(jnp.logical_and(want_sec == 0, jnp.logical_and(dp == 0, d == 0))))
            def _():
                hello((want_sec, d, dp * grp + my_q))

    row = lax.broadcasted_iota(jnp.int32, (8, 128), 0)
    mine = jnp.zeros((8, 128), F32)
    for i in range(caps):
        mine = jnp.where(row == i, len_ref[i].astype(F32), mine)
    lens[dp] = mine

    source = tok_ref.at[:, :, pl.ds(pl.multiple_of(lax.rem(sec, 2) * strip, strip), strip)]
    slab = strips_ref.at[dp]

    @pl.when(home)
    def _():
        pltpu.make_async_copy(source, slab, home_s).start()
        pl.semaphore_wait(barrier, nd - 1)

    @pl.when(jnp.logical_not(home))
    def _():
        pl.semaphore_wait(barrier, nd)

    for o in range(1, nd):
        pltpu.make_async_remote_copy(
            src_ref=lens.at[dp], dst_ref=lens.at[dp], send_sem=len_s.at[o - 1], recv_sem=len_r.at[nd - 1 - o],
            device_id=(sec, lax.rem(dp + o, nd), mp), device_id_type=MESH).start()

    @pl.when(jnp.logical_not(home))
    def _():
        pltpu.make_async_remote_copy(
            src_ref=source, dst_ref=slab, send_sem=tok_s, recv_sem=tok_r.at[dp],
            device_id=(0, my_group, sec * grp + my_q), device_id_type=MESH).start()

    for o in range(1, nd):
        other = lens.at[lax.rem(dp + o, nd)]
        pltpu.make_async_copy(other, other, len_r.at[o - 1]).wait()
    lens_ref[...] = lens[...]
    counted = jnp.sum(lens[:, :, 0:1])
    which = jnp.int32(0)
    for room in rooms[:-1]:
        which = which + (counted > room).astype(jnp.int32)
    which_ref[0, 0] = which

    @pl.when(sec == 0)
    def _():
        for d in range(nd):
            here = strips_ref.at[d]
            itself = jnp.logical_and(want_sec == 0, jnp.logical_and(dp == 0, d == 0))

            @pl.when(itself)
            def _():
                pltpu.make_async_copy(here, here, home_s).wait()

            @pl.when(jnp.logical_not(itself))
            def _():
                pltpu.make_async_copy(here, here, tok_r.at[d]).wait()

    for o in range(1, nd):
        pltpu.make_async_copy(lens.at[dp], lens.at[dp], len_s.at[o - 1]).wait()

    @pl.when(jnp.logical_not(home))
    def _():
        pltpu.make_async_copy(slab, slab, tok_s).wait()


def front(sizes, plans, tokens, lengths):
    nd = sizes[1]
    caps, slots, piece = tokens.shape
    dma = pltpu.SemaphoreType.DMA
    return pl.pallas_call(
        functools.partial(front_kernel, sizes, [micro * batch for micro, batch in plans]),
        out_shape=(
            jax.ShapeDtypeStruct((nd, caps, slots, piece // 2), BF16),
            jax.ShapeDtypeStruct((nd, 8, 128), F32),
            jax.ShapeDtypeStruct((1, 1), jnp.int32),
        ),
        in_specs=[pl.BlockSpec(memory_space=pl.ANY), pl.BlockSpec(memory_space=pltpu.SMEM)],
        out_specs=(pl.BlockSpec(memory_space=pl.ANY), pl.BlockSpec(memory_space=pltpu.VMEM),
                   pl.BlockSpec(memory_space=pltpu.SMEM)),
        scratch_shapes=[
            pltpu.VMEM((nd, 8, 128), F32),
            dma((nd - 1,)), dma((nd - 1,)), dma, dma((nd,)), dma,
        ],
        compiler_params=pltpu.CompilerParams(
            collective_id=1, has_side_effects=True, vmem_limit_bytes=60 * 2 ** 20),
        name="front",
    )(tokens, lengths)


def per_device(
    sizes, plans,
    caption_tokens, caption_lengths, group_ids, text_gain, text_gate, text_up, text_down,
    text_proj, image_patches, image_gain, image_fc1, image_fc2, image_proj,
):
    strips, lens, which = front(sizes, plans, caption_tokens, caption_lengths)
    operands = (
        strips, lens, group_ids, text_gain, text_gate, text_up, text_down,
        text_proj, image_patches, image_gain.reshape(1, -1), image_fc1, image_fc2, image_proj,
    )
    branches = [functools.partial(towers, sizes, plan, 2 + i) for i, plan in enumerate(plans)]
    return lax.switch(which[0, 0], branches, *operands)


def towers(
    sizes, plan, barrier_id,
    strips, caption_lengths, group_ids, text_gain, text_gate, text_up, text_down,
    text_proj, image_patches, image_gain, image_fc1, image_fc2, image_proj,
):
    ns, nd, nm = sizes
    grp = nm // nd
    micro, batch = plan
    _, caps, slots, strip = strips.shape
    piece = 2 * strip
    length = batch // nd
    ncap = nd * caps
    dl, width = text_gate.shape[1], text_gate.shape[2]
    dv, hv = image_fc1.shape
    embed = text_proj.shape[1]
    nf = nd * grp
    any_spec = pl.BlockSpec(memory_space=pl.ANY)
    vmem = pl.BlockSpec(memory_space=pltpu.VMEM)
    smem = pl.BlockSpec(memory_space=pltpu.SMEM)
    dma = pltpu.SemaphoreType.DMA
    loss, gcap, gimg = pl.pallas_call(
        functools.partial(kernel, sizes),
        out_shape=(
            jax.ShapeDtypeStruct((1, 128), F32),
            jax.ShapeDtypeStruct((caps, embed), F32),
            jax.ShapeDtypeStruct((1, embed), F32),
        ),
        in_specs=[any_spec, vmem, smem, vmem, any_spec, any_spec, any_spec, any_spec,
                  any_spec, vmem, any_spec, any_spec, any_spec],
        out_specs=(vmem, vmem, vmem),
        scratch_shapes=[
            pltpu.VMEM((dl, 2 * width), BF16),
            pltpu.VMEM((width, dl), BF16),
            pltpu.VMEM((piece, embed), BF16),
            pltpu.VMEM((dv, hv), BF16),
            pltpu.VMEM((hv, dv), BF16),
            pltpu.VMEM((dv, embed), BF16),
            pltpu.VMEM(image_patches.shape, BF16),
            pltpu.VMEM((nd, caps, slots, piece // 2), BF16),
            pltpu.VMEM((8, ncap * slots), F32),
            pltpu.VMEM((micro, batch, dl), BF16),
            pltpu.VMEM((micro, length, 2 * width + 128), BF16),
            pltpu.VMEM((micro, 3 * length, 2 * width + 128), BF16),
            pltpu.VMEM((micro, length, width), BF16),
            pltpu.VMEM((micro, length, width + 128), BF16),
            pltpu.VMEM((micro, 2, length, 2 * width + 128), BF16),
            pltpu.VMEM((micro, batch, width), BF16),
            pltpu.VMEM((micro, batch, dl), BF16),
            pltpu.VMEM((micro, nm - 1, length, piece), BF16),
            pltpu.VMEM((micro, length, piece), BF16),
            pltpu.VMEM((nm - 1, dv // 128, 128), F32),
            pltpu.VMEM((dv // 128, 128), F32),
            pltpu.VMEM((ns * nd, dv // 128, 128), F32),
            pltpu.VMEM((dv // 128, 128), F32),
            pltpu.VMEM((8, dv), F32),
            pltpu.VMEM((ncap, piece), F32),
            pltpu.VMEM((ncap, width), F32),
            pltpu.VMEM((nd, ncap, width), BF16),
            pltpu.VMEM((grp, ncap, piece), F32),
            pltpu.VMEM((nm - 1, ncap, piece), F32),
            pltpu.VMEM((ncap, embed), BF16),
            pltpu.VMEM((nf - 1, ncap, embed), BF16),
            pltpu.VMEM((8, embed), F32),
            dma((9,)), *([dma((micro,))] * 13), dma((nd - 1, micro)),
            dma((micro,)), dma, dma, dma, dma, dma, dma, dma((grp,)), dma, dma, dma, dma((ns * nd,)), dma,
        ],
        compiler_params=pltpu.CompilerParams(
            collective_id=barrier_id, has_side_effects=True, vmem_limit_bytes=60 * 2 ** 20),
        name=f"towers_{micro}_{batch}",
    )(
        strips, caption_lengths, group_ids, text_gain, text_gate, text_up, text_down,
        text_proj, image_patches, image_gain, image_fc1, image_fc2, image_proj,
    )
    return loss[0, 0], gcap, gimg


def solution(mesh):
    sizes = tuple(mesh.shape[axis] for axis in ("section", "dp", "mp"))
    return jax.shard_map(
        functools.partial(per_device, sizes, PLANS),
        mesh=mesh,
        in_specs=(
            P("dp", None, "mp"),
            P("dp"),
            P(),
            P("section", None),
            P("section", "dp", "mp"),
            P("section", "dp", "mp"),
            P("section", "mp", "dp"),
            P("mp", None),
            P("dp", "section", None),
            P(),
            P(None, "mp"),
            P("mp", None),
            P(),
        ),
        out_specs=(P(), P("dp", None), P("dp", None)),
        check_vma=False,
    )
```

```python
import functools

import jax
import jax.numpy as jnp
from jax import lax
from jax.experimental import pallas as pl
from jax.experimental.pallas import tpu as pltpu
from jax.sharding import PartitionSpec as P

MESH = pl.DeviceIdType.MESH
PLANS = ((3, 128), (4, 128), (3, 192), (5, 128), (4, 192), (4, 256))
BF16 = jnp.bfloat16
F32 = jnp.float32


def kernel(
    sizes,
    tok_ref, len_ref, gid_ref, gain_ref, gate_ref, up_ref, down_ref, tproj_ref,
    patch_ref, vgain_ref, fc1_ref, fc2_ref, iproj_ref,
    loss_ref, gcap_ref, gimg_ref,
    w_gu, w_dn, w_tp, w_f1, w_f2, w_ip, patches,
    tok_buf, pos_buf, x_buf, far_buf, p_buf, ra_buf, rb_buf, r_buf, i_buf, q_buf, s_buf, h_buf,
    im1, im1_own, im2, im2_own, imrow, mean_h,
    pin, pin_o, pd, pdr, emb, embr, outb,
    wsem, xr, pa_s, pa_r, pb_s, pb_r, pc_s, pc_r, pd_s2, pd_r2,
    iss, qs, qr, hs, ir,
    cs, im1_s, im1_r, im2_s, im2_r, pin_s, pin_r, pd_s, pd_r, e_s, e_r, out_s, out_r,
):
    ns, nd, nm = sizes
    grp = nm // nd
    _, caps, slots, strip = tok_ref.shape
    piece = 2 * strip
    ncap = nd * caps
    micro, batch, dl = x_buf.shape
    length = batch // nd
    width = gate_ref.shape[2]
    dim = dl * nd
    sec, dp, mp = lax.axis_index("section"), lax.axis_index("dp"), lax.axis_index("mp")
    last = ns - 1
    my_group = mp // grp
    my_q = lax.rem(mp, grp)
    is_final = jnp.logical_and(sec == last, my_group == dp)

    def send(src, dst, s_sem, r_sem, where):
        pltpu.make_async_remote_copy(
            src_ref=src, dst_ref=dst, send_sem=s_sem, recv_sem=r_sem,
            device_id=where, device_id_type=MESH,
        ).start()

    def drain(ref, sem):
        pltpu.make_async_copy(ref, ref, sem).wait()

    def load(src, dst, index):
        pltpu.make_async_copy(src, dst, wsem.at[index]).start()

    def loaded(dst, index):
        pltpu.make_async_copy(dst, dst, wsem.at[index]).wait()

    def chunk(d):
        return pl.ds(pl.multiple_of(d * length, length), length)

    rows_y = pl.ds(pl.multiple_of(my_group * length, length), length)
    cols_z = pl.ds(pl.multiple_of(my_q * piece, piece), piece)

    @pl.when(sec == 0)
    def _():
        load(tok_ref, tok_buf, 0)

    load(gate_ref.at[0], w_gu.at[:, pl.ds(0, width)], 3)
    load(up_ref.at[0], w_gu.at[:, pl.ds(width, width)], 4)
    load(patch_ref, patches, 8)
    load(fc1_ref, w_f1, 1)
    load(fc2_ref, w_f2, 2)
    load(down_ref.at[0], w_dn, 5)
    load(tproj_ref, w_tp, 6)
    load(iproj_ref, w_ip, 7)

    root = grp * lax.rem(dp + 1, nd)
    nf = nd * grp
    me_f = dp * grp + my_q
    final_mp = dp * grp + my_q
    barrier = pltpu.get_barrier_semaphore()

    def hello(where):
        pl.semaphore_signal(barrier, inc=1, device_id=where, device_id_type=MESH)

    def each(lo, hi, body):
        def step(o, _):
            body(o)
            return 0

        lax.fori_loop(lo, hi, step, 0, unroll=True)

    each(1, nd, lambda o: hello((sec, lax.rem(dp + o, nd), mp)))
    each(1, nm, lambda o: hello((sec, dp, lax.rem(mp + o, nm))))

    @pl.when(sec > 0)
    def _():
        each(0, nm, lambda o: hello((sec - 1, dp, lax.rem(mp + o, nm))))

    @pl.when(is_final)
    def _():
        each(0, ns * nd, lambda o: hello((o // nd, lax.rem(o, nd), grp * lax.rem(o + 1, nd))))

        def other_final(o):
            f = lax.rem(me_f + o, nf)
            hello((last, f // grp, f))

        each(1, nf, other_final)

    @pl.when(jnp.logical_not(is_final))
    def _():
        hello((last, dp, final_mp))

    counts = [len_ref[c // caps, c % caps:c % caps + 1, 0:1] for c in range(ncap)]
    starts = [jnp.zeros((1, 1), F32)]
    for c in range(ncap):
        starts.append(starts[-1] + counts[c])

    def dp_peers(body):
        def step(o, _):
            peer = lax.rem(dp + o, nd)
            body(peer, nd - 1 - o)
            return 0

        lax.fori_loop(1, nd, step, 0)

    def ranked(t):
        y, z = lax.rem(my_group + t // grp + 2, nd), lax.rem(my_q + t + grp // 2, grp)
        return y * grp + z

    def mp_peers(body):
        def one(t):
            peer = ranked(t)
            body(peer, lax.rem(mp - peer - 1 + 2 * nm, nm))

        itself = (nd - 2) * grp + grp // 2
        each(0, itself, one)
        each(itself + 1, nm, one)

    half_rows = pl.ds(pl.multiple_of((my_group // 2) * (batch // 2), batch // 2), batch // 2)

    strip_cols = pl.ds(pl.multiple_of(my_q * piece + lax.rem(my_group, 2) * strip, strip), strip)

    def positions():
        loaded(tok_buf, 0)
        lane = lax.broadcasted_iota(jnp.int32, (8, ncap * slots), 1)
        cap = lane // slots
        pos = jnp.full((8, ncap * slots), -1.0, F32)
        for c in range(ncap):
            at = (lane - c * slots).astype(F32)
            pos = jnp.where(jnp.logical_and(cap == c, at < counts[c]), starts[c] + at, pos)
        pos_buf[...] = pos

    def pack_rows(b):
        row = lax.broadcasted_iota(jnp.int32, (batch // 2, ncap * slots), 0)
        row = (row + (b * batch + (my_group // 2) * (batch // 2))).astype(F32)
        picks = jnp.where(row == pos_buf[0:1], 1.0, 0.0).astype(BF16)
        tokens = tok_buf[...].reshape(ncap * slots, strip)
        x_buf[b, half_rows, strip_cols] = jnp.dot(picks, tokens, preferred_element_type=F32).astype(BF16)

    def pack_send(b):
        here = x_buf.at[b, half_rows, strip_cols]
        mp_peers(lambda peer, slot: send(here, here, cs.at[b], xr.at[b], (sec, dp, peer)))

    ahead = min(2, micro)

    @pl.when(sec == 0)
    def _():
        positions()
        lax.fori_loop(0, ahead, lambda b, _: (pack_rows(b), 0)[1], 0)

    partners = nd - 1 + nm - 1 + jnp.where(sec < last, nm, 0) + jnp.where(mp == root, nd * grp, 0)
    partners = partners + jnp.where(is_final, nf - 1 + ns * nd - 1, 0)
    pl.semaphore_wait(barrier, partners)

    @pl.when(sec == 0)
    def _():
        lax.fori_loop(0, ahead, lambda b, _: (pack_send(b), 0)[1], 0)

    vtiles = w_f2.shape[1] // 128

    def image_layer():
        loaded(patches, 8)
        loaded(w_f1, 1)
        rows = patches[0].astype(F32)
        scale = lax.rsqrt(jnp.mean(rows * rows, -1, keepdims=True) + 1e-05)
        vnormed = (rows * scale * vgain_ref[...]).astype(BF16)
        hidden = jnp.dot(vnormed, w_f1[...], preferred_element_type=F32)
        vinner = (0.5 * hidden * (1.0 + lax.erf(hidden * (0.5 ** 0.5)))).astype(BF16)
        vsum = jnp.sum(vinner.astype(F32), 0, keepdims=True)
        high = vsum.astype(BF16)
        low = (vsum - high.astype(F32)).astype(BF16)
        loaded(w_f2, 2)
        two = jnp.concatenate([jnp.broadcast_to(high, (8, high.shape[1])), jnp.broadcast_to(low, (8, low.shape[1]))], 0)
        prod = jnp.dot(two, w_f2[...], preferred_element_type=F32)
        part = prod[0:1] + prod[8:9] + jnp.where(mp == 0, 1.0, 0.0) * jnp.sum(rows, 0, keepdims=True)
        for i in range(vtiles):
            im1_own[pl.ds(i, 1), :] = part[:, 128 * i:128 * (i + 1)]

        @pl.when(mp != root)
        def _():
            slot = lax.rem(mp - root - 1 + 2 * nm, nm)
            send(im1_own, im1.at[slot], im1_s, im1_r, (sec, dp, root))

        @pl.when(mp == root)
        def _():
            drain(im1, im1_r)
            im2_own[...] = im1_own[...] + jnp.sum(im1[...], 0)

            def to_final(t, _):
                d, q = t // grp, lax.rem(t, grp)
                send(im2_own, im2.at[sec * nd + dp], im2_s, im2_r, (last, d, grp * d + q))
                return 0

            lax.fori_loop(0, nd * grp, to_final, 0)

    @pl.when(sec > 0)
    def _():
        image_layer()

    loaded(w_gu.at[:, pl.ds(0, width)], 3)
    loaded(w_gu.at[:, pl.ds(width, width)], 4)
    gain = gain_ref[0:1, pl.ds(pl.multiple_of(dp * dl, dl), dl)]

    def members(first, width):
        row = lax.broadcasted_iota(jnp.int32, (ncap, width), 0)
        token = (lax.broadcasted_iota(jnp.int32, (ncap, width), 1) + first).astype(F32)
        lo = jnp.zeros((ncap, width), F32)
        hi = jnp.zeros((ncap, width), F32)
        for c in range(ncap):
            lo = jnp.where(row == c, starts[c], lo)
            hi = jnp.where(row == c, starts[c + 1], hi)
        return jnp.where(jnp.logical_and(token >= lo, token < hi), 1.0, 0.0).astype(BF16)

    right, left, far = lax.rem(dp + 1, nd), lax.rem(dp + nd - 1, nd), lax.rem(dp + 2, nd)
    full = 2 * width + 128
    low_cols, high_cols = pl.ds(0, width), pl.ds(width, width + 128)

    def products(rows, out, first_done=None):
        x = rows.astype(F32)
        scaled = (x * gain).astype(BF16)
        if first_done is None:
            out[:, pl.ds(0, 2 * width)] = jnp.dot(
                scaled, w_gu[...], preferred_element_type=F32).astype(BF16)
        else:
            out[:, pl.ds(0, width)] = jnp.dot(
                scaled, w_gu[:, 0:width], preferred_element_type=F32).astype(BF16)
            first_done()
            out[:, pl.ds(width, width)] = jnp.dot(
                scaled, w_gu[:, width:2 * width], preferred_element_type=F32).astype(BF16)
        total = jnp.sum(x * x, -1, keepdims=True)
        high = total.astype(BF16).astype(F32)
        lane = lax.broadcasted_iota(jnp.int32, (x.shape[0], 128), 1)
        out[:, pl.ds(2 * width, 128)] = jnp.where(lane < 64, high, total - high).astype(BF16)

    def stage_far(b):
        @pl.when(sec == 0)
        def _():
            drain(s_buf.at[b], xr.at[b])

        @pl.when(sec > 0)
        def _():
            drain(x_buf.at[b], xr.at[b])

        products(x_buf[b, chunk(far), :], far_buf.at[b], lambda: send(
            far_buf.at[b, :, low_cols], ra_buf.at[b], pa_s.at[b], pa_r.at[b], (sec, right, mp)))
        send(far_buf.at[b, :, high_cols], rb_buf.at[b], pb_s.at[b], pb_r.at[b], (sec, left, mp))

    def stage_near(b):
        near = jnp.concatenate([x_buf[b, chunk(c), :] for c in (right, left, dp)], 0)
        products(near, p_buf.at[b])

    to_right, to_left, to_self = pl.ds(0, length), pl.ds(length, length), pl.ds(2 * length, length)

    def stage_relay(b):
        drain(ra_buf.at[b], pa_r.at[b])
        p_buf[b, to_right, low_cols] = (
            p_buf[b, to_right, low_cols].astype(F32) + ra_buf[b].astype(F32)).astype(BF16)
        send(p_buf.at[b, to_right], r_buf.at[b, 0], pc_s.at[b], pc_r.at[b], (sec, right, mp))
        drain(rb_buf.at[b], pb_r.at[b])
        p_buf[b, to_left, high_cols] = (
            p_buf[b, to_left, high_cols].astype(F32) + rb_buf[b].astype(F32)).astype(BF16)
        send(p_buf.at[b, to_left], r_buf.at[b, 1], pd_s2.at[b], pd_r2.at[b], (sec, left, mp))

    def stage_b(b):
        drain(r_buf.at[b, 0], pc_r.at[b])
        drain(r_buf.at[b, 1], pd_r2.at[b])
        total = p_buf[b, to_self, :].astype(F32) + r_buf[b, 0].astype(F32) + r_buf[b, 1].astype(F32)
        squares = total[:, 2 * width:2 * width + 1] + total[:, 2 * width + 64:2 * width + 65]
        scale = lax.rsqrt(squares * (1.0 / dim) + 1e-05)
        gate = total[:, :width] * scale
        upper = total[:, width:2 * width] * scale
        inner = (gate * jax.nn.sigmoid(gate) * upper).astype(BF16)

        @pl.when(sec < last)
        def _():
            i_buf[b, chunk(dp), :] = inner
            here = i_buf.at[b, chunk(dp)]
            for o in (2, 1, nd - 1):
                send(here, here, iss.at[b], ir.at[nd - 1 - o, b], (sec, lax.rem(dp + o, nd), mp))

        @pl.when(sec == last)
        def _():
            @pl.when(b == 0)
            def _():
                pin[...] = jnp.zeros(pin.shape, F32)
                mean_h[...] = jnp.zeros(mean_h.shape, F32)

            mine = members(b * batch + dp * length, length)
            pin[...] = pin[...] + jnp.dot(mine, inner, preferred_element_type=F32)

    def down(b, offsets):
        sources = [lax.rem(dp + o, nd) for o in offsets]
        for o, source in zip(offsets, sources):
            if o:
                drain(i_buf.at[b, chunk(source)], ir.at[o - 1, b])
        out = jnp.dot(jnp.concatenate([i_buf[b, chunk(c), :] for c in sources], 0), w_dn[...],
                      preferred_element_type=F32).astype(BF16)
        for at, source in enumerate(sources):
            q_buf[b, chunk(source), :] = out[at * length:(at + 1) * length]

            def to_owner(o, source=source):
                z = lax.rem(my_q + o + grp // 2, grp)
                owner = source * grp + z

                @pl.when(owner != mp)
                def _():
                    slot = lax.rem(mp - owner - 1 + 2 * nm, nm)
                    send(q_buf.at[b, chunk(source), pl.ds(pl.multiple_of(z * piece, piece), piece)],
                         s_buf.at[b, slot], qs.at[b], qr.at[b], (sec, dp, owner))

            each(0, grp, to_owner)

    def stage_down_near(b):
        down(b, (0, 1, nd - 1))

    def stage_down_far(b):
        down(b, (2,))

    def stage_d(b):
        drain(s_buf.at[b], qr.at[b])
        total = x_buf[b, rows_y, cols_z].astype(F32) + q_buf[b, rows_y, cols_z].astype(F32)
        for i in range(nm - 1):
            total = total + s_buf[b, i].astype(F32)
        h_buf[b] = total.astype(BF16)

        each(0, nm, lambda t: send(
            h_buf.at[b], x_buf.at[b, rows_y, cols_z], hs.at[b], xr.at[b], (sec + 1, dp, ranked(t))))

    def tick(i, _):
        def at(stage, back, also=True):
            @pl.when(jnp.logical_and(also, jnp.logical_and(i >= back, i < micro + back)))
            def _():
                stage(i - back)

        inside = sec < last
        at(stage_far, 0)
        at(stage_b, 1)
        at(stage_near, 0)

        @pl.when(jnp.logical_and(sec == 0, i + 2 < micro))
        def _():
            pack_rows(i + 2)
            pack_send(i + 2)

        at(stage_relay, 0)

        @pl.when(jnp.logical_and(inside, i == 1))
        def _():
            loaded(w_dn, 5)

        at(stage_down_near, 1, inside)
        at(stage_d, 2, inside)
        at(stage_down_far, 1, inside)
        return 0

    lax.fori_loop(0, micro + 2, tick, 0)

    @pl.when(sec == 0)
    def _():
        image_layer()

    loaded(w_tp, 6)
    loaded(w_ip, 7)

    def shares():
        row = lax.broadcasted_iota(jnp.int32, (ncap, 1), 0)
        count = jnp.ones((ncap, 1), F32)
        for c in range(ncap):
            count = jnp.where(row == c, counts[c], count)
        return 1.0 / count

    @pl.when(sec == last)
    def _():
        loaded(w_dn, 5)
        pin_o[nd - 1] = (pin[...] * shares()).astype(BF16)
        dp_peers(lambda peer, slot: send(pin_o.at[nd - 1], pin_o.at[slot], pin_s, pin_r, (sec, peer, mp)))

        @pl.when(is_final)
        def _():
            def mean_of(b, _):
                mean_h[...] = mean_h[...] + jnp.dot(
                    members(b * batch, batch), x_buf[b, :, cols_z], preferred_element_type=F32)
                return 0

            lax.fori_loop(0, micro, mean_of, 0)
            drain(im2, im2_r)
            imrow[...] = jnp.zeros(imrow.shape, F32)
            for d in range(nd):
                image = im2[d]
                for s in range(1, ns):
                    image = image + im2[s * nd + d]
                for i in range(vtiles):
                    imrow[d:d + 1, 128 * i:128 * (i + 1)] = image[i:i + 1, :]

        drain(pin_o.at[pl.ds(0, nd - 1)], pin_r)
        pooled = pin_o[0].astype(F32)
        for i in range(1, nd):
            pooled = pooled + pin_o[i].astype(F32)
        out = jnp.dot(pooled.astype(BF16), w_dn[...], preferred_element_type=F32)
        for q in range(grp):
            pd[q] = out[:, q * piece:(q + 1) * piece]

        def to_final(q, _):
            target = grp * dp + q

            @pl.when(target != mp)
            def _():
                slot = lax.rem(mp - target - 1 + 2 * nm, nm)
                send(pd.at[q], pdr.at[slot], pd_s.at[q], pd_r, (sec, dp, target))
            return 0

        lax.fori_loop(0, grp, to_final, 0, unroll=True)

    def fan_target(t):
        s, y = t // nd, lax.rem(t, nd)
        target = y * grp + my_q
        return s, target, jnp.logical_and(s == last, target == mp)

    @pl.when(is_final)
    def _():
        drain(pdr, pd_r)
        total = pd[my_q]
        for i in range(nm - 1):
            total = total + pdr[i]
        total = total + mean_h[...] * shares()
        emb[...] = jnp.dot(total.astype(BF16), w_tp[...], preferred_element_type=F32).astype(BF16)

        def to_others(o, _):
            f = lax.rem(me_f + o, nf)
            d, q = f // grp, lax.rem(f, grp)
            send(emb, embr.at[nf - 1 - o], e_s, e_r, (last, d, grp * d + q))
            return 0

        lax.fori_loop(1, nf, to_others, 0, unroll=True)
        pooled = (imrow[...] * (1.0 / (ns * patch_ref.shape[1]))).astype(BF16)
        image = jnp.dot(pooled, w_ip[...], preferred_element_type=F32)
        iu = image * lax.rsqrt(jnp.sum(image * image, -1, keepdims=True) + 1e-06)

        nrow = ncap
        row = lax.broadcasted_iota(jnp.int32, (nrow, 8), 0)
        col = lax.broadcasted_iota(jnp.int32, (nrow, 8), 1)
        gids = jnp.full((nrow, 8), -1, jnp.int32)
        for k in range(ncap):
            gids = jnp.where(row == k, gid_ref[k], gids)
        match = jnp.where(gids == col, 1.0, 0.0)
        real = jnp.where(col < nd, 1.0, 0.0)

        drain(embr, e_r)
        total = emb[...].astype(F32)
        for i in range(nf - 1):
            total = total + embr[i].astype(F32)
        cu = total * lax.rsqrt(jnp.sum(total * total, -1, keepdims=True) + 1e-06)
        logits = jnp.zeros((nrow, 8), F32)
        for j in range(nd):
            logits = jnp.where(col == j, 10.0 * jnp.sum(cu * iu[j:j + 1], -1, keepdims=True), logits)
        expo = jnp.exp(logits) * real
        good = expo * match
        by_row = jnp.sum(expo, 1, keepdims=True)
        by_row = jnp.where(by_row > 0, by_row, 1.0)
        by_col = jnp.sum(expo, 0, keepdims=True)
        by_col = jnp.where(by_col > 0, by_col, 1.0)
        good_col = jnp.sum(good, 0, keepdims=True)
        good_col = jnp.where(good_col > 0, good_col, 1.0)
        def whole(array):
            return jnp.sum(jnp.sum(array, 0, keepdims=True), 1, keepdims=True)

        forward = whole(jnp.log(by_row)) - whole(logits * match * real)
        backward = whole(jnp.log(by_col) - jnp.log(good_col))
        loss = 0.5 * (forward / ncap + backward / nd)
        slope = 5.0 * (expo / by_row - match * real + expo / by_col - good / good_col)
        gcap = jnp.zeros(cu.shape, F32)
        gimg = jnp.zeros((1, cu.shape[1]), F32)
        for j in range(nd):
            gcap = gcap + slope[:, j:j + 1] * iu[j:j + 1]
            gimg = gimg + jnp.where(dp == j, 1.0, 0.0) * jnp.sum(slope[:, j:j + 1] * cu, 0, keepdims=True)
        mine = jnp.zeros((caps, cu.shape[1]), F32)
        for d in range(nd):
            mine = mine + jnp.where(dp == d, 1.0, 0.0) * gcap[caps * d:caps * d + caps]
        outb[0:caps, :] = mine
        outb[caps:caps + 1, :] = gimg
        outb[caps + 1:8, :] = jnp.broadcast_to(loss, (7 - caps, cu.shape[1]))

        def fan(t, _):
            s, target, home = fan_target(t)

            @pl.when(jnp.logical_not(home))
            def _():
                send(outb, outb, out_s.at[t], out_r, (s, dp, target))
            return 0

        lax.fori_loop(0, ns * nd, fan, 0, unroll=True)

    @pl.when(mp != root)
    def _():
        drain(im1_own, im1_s)

    @pl.when(mp == root)
    def _():
        drain(im2, im2_s)

    def sent_batch(b, _):
        @pl.when(sec == 0)
        def _():
            drain(s_buf.at[b], cs.at[b])

        drain(ra_buf.at[b], pa_s.at[b])
        drain(rb_buf.at[b], pb_s.at[b])
        drain(r_buf.at[b, 0], pc_s.at[b])
        drain(r_buf.at[b, 1], pd_s2.at[b])

        @pl.when(sec < last)
        def _():
            drain(i_buf.at[b, pl.ds(0, batch - length)], iss.at[b])
            drain(s_buf.at[b], qs.at[b])
            drain(x_buf.at[b], hs.at[b])
        return 0

    lax.fori_loop(0, micro, sent_batch, 0)

    @pl.when(sec == last)
    def _():
        drain(pin_o.at[pl.ds(0, nd - 1)], pin_s)

        def sent_pd(q, _):
            @pl.when(grp * dp + q != mp)
            def _():
                drain(pd.at[0], pd_s.at[q])
            return 0

        lax.fori_loop(0, grp, sent_pd, 0)

    @pl.when(jnp.logical_not(is_final))
    def _():
        drain(outb, out_r)

    loss_ref[...] = outb[caps + 1:caps + 2, 0:128]
    gcap_ref[...] = outb[0:caps, :]
    gimg_ref[...] = outb[caps:caps + 1, :]

    @pl.when(is_final)
    def _():
        drain(embr, e_s)

        def sent_fan(t, _):
            _, _, home = fan_target(t)

            @pl.when(jnp.logical_not(home))
            def _():
                drain(outb, out_s.at[t])
            return 0

        lax.fori_loop(0, ns * nd, sent_fan, 0)


def front_kernel(sizes, rooms, tok_ref, len_ref, strips_ref, lens_ref, which_ref, lens, len_s, len_r, tok_s, tok_r, home_s):
    ns, nd, nm = sizes
    grp = nm // nd
    caps, _, piece = tok_ref.shape
    strip = piece // 2
    sec, dp, mp = lax.axis_index("section"), lax.axis_index("dp"), lax.axis_index("mp")
    my_group, my_q = mp // grp, lax.rem(mp, grp)
    home = jnp.logical_and(sec == 0, jnp.logical_and(my_group == 0, dp == 0))
    want_sec = my_group
    barrier = pltpu.get_barrier_semaphore()

    def hello(where):
        pl.semaphore_signal(barrier, inc=1, device_id=where, device_id_type=MESH)

    for o in range(1, nd):
        hello((sec, lax.rem(dp + o, nd), mp))

    @pl.when(sec == 0)
    def _():
        for d in range(nd):
            @pl.when(jnp.logical_not(jnp.logical_and(want_sec == 0, jnp.logical_and(dp == 0, d == 0))))
            def _():
                hello((want_sec, d, dp * grp + my_q))

    row = lax.broadcasted_iota(jnp.int32, (8, 128), 0)
    mine = jnp.zeros((8, 128), F32)
    for i in range(caps):
        mine = jnp.where(row == i, len_ref[i].astype(F32), mine)
    lens[dp] = mine

    source = tok_ref.at[:, :, pl.ds(pl.multiple_of(lax.rem(sec, 2) * strip, strip), strip)]
    slab = strips_ref.at[dp]

    @pl.when(home)
    def _():
        pltpu.make_async_copy(source, slab, home_s).start()
        pl.semaphore_wait(barrier, nd - 1)

    @pl.when(jnp.logical_not(home))
    def _():
        pl.semaphore_wait(barrier, nd)

    for o in range(1, nd):
        pltpu.make_async_remote_copy(
            src_ref=lens.at[dp], dst_ref=lens.at[dp], send_sem=len_s.at[o - 1], recv_sem=len_r.at[nd - 1 - o],
            device_id=(sec, lax.rem(dp + o, nd), mp), device_id_type=MESH).start()

    @pl.when(jnp.logical_not(home))
    def _():
        pltpu.make_async_remote_copy(
            src_ref=source, dst_ref=slab, send_sem=tok_s, recv_sem=tok_r.at[dp],
            device_id=(0, my_group, sec * grp + my_q), device_id_type=MESH).start()

    for o in range(1, nd):
        other = lens.at[lax.rem(dp + o, nd)]
        pltpu.make_async_copy(other, other, len_r.at[o - 1]).wait()
    lens_ref[...] = lens[...]
    counted = jnp.sum(lens[:, :, 0:1])
    which = jnp.int32(0)
    for room in rooms[:-1]:
        which = which + (counted > room).astype(jnp.int32)
    which_ref[0, 0] = which

    @pl.when(sec == 0)
    def _():
        for d in range(nd):
            here = strips_ref.at[d]
            itself = jnp.logical_and(want_sec == 0, jnp.logical_and(dp == 0, d == 0))

            @pl.when(itself)
            def _():
                pltpu.make_async_copy(here, here, home_s).wait()

            @pl.when(jnp.logical_not(itself))
            def _():
                pltpu.make_async_copy(here, here, tok_r.at[d]).wait()

    for o in range(1, nd):
        pltpu.make_async_copy(lens.at[dp], lens.at[dp], len_s.at[o - 1]).wait()

    @pl.when(jnp.logical_not(home))
    def _():
        pltpu.make_async_copy(slab, slab, tok_s).wait()


def front(sizes, plans, tokens, lengths):
    nd = sizes[1]
    caps, slots, piece = tokens.shape
    dma = pltpu.SemaphoreType.DMA
    return pl.pallas_call(
        functools.partial(front_kernel, sizes, [micro * batch for micro, batch in plans]),
        out_shape=(
            jax.ShapeDtypeStruct((nd, caps, slots, piece // 2), BF16),
            jax.ShapeDtypeStruct((nd, 8, 128), F32),
            jax.ShapeDtypeStruct((1, 1), jnp.int32),
        ),
        in_specs=[pl.BlockSpec(memory_space=pl.ANY), pl.BlockSpec(memory_space=pltpu.SMEM)],
        out_specs=(pl.BlockSpec(memory_space=pl.ANY), pl.BlockSpec(memory_space=pltpu.VMEM),
                   pl.BlockSpec(memory_space=pltpu.SMEM)),
        scratch_shapes=[
            pltpu.VMEM((nd, 8, 128), F32),
            dma((nd - 1,)), dma((nd - 1,)), dma, dma((nd,)), dma,
        ],
        compiler_params=pltpu.CompilerParams(
            collective_id=1, has_side_effects=True, vmem_limit_bytes=60 * 2 ** 20),
        name="front",
    )(tokens, lengths)


def per_device(
    sizes, plans,
    caption_tokens, caption_lengths, group_ids, text_gain, text_gate, text_up, text_down,
    text_proj, image_patches, image_gain, image_fc1, image_fc2, image_proj,
):
    strips, lens, which = front(sizes, plans, caption_tokens, caption_lengths)
    operands = (
        strips, lens, group_ids, text_gain, text_gate, text_up, text_down,
        text_proj, image_patches, image_gain.reshape(1, -1), image_fc1, image_fc2, image_proj,
    )
    branches = [functools.partial(towers, sizes, plan, 2 + i) for i, plan in enumerate(plans)]
    return lax.switch(which[0, 0], branches, *operands)


def towers(
    sizes, plan, barrier_id,
    strips, caption_lengths, group_ids, text_gain, text_gate, text_up, text_down,
    text_proj, image_patches, image_gain, image_fc1, image_fc2, image_proj,
):
    ns, nd, nm = sizes
    grp = nm // nd
    micro, batch = plan
    _, caps, slots, strip = strips.shape
    piece = 2 * strip
    length = batch // nd
    ncap = nd * caps
    dl, width = text_gate.shape[1], text_gate.shape[2]
    dv, hv = image_fc1.shape
    embed = text_proj.shape[1]
    nf = nd * grp
    any_spec = pl.BlockSpec(memory_space=pl.ANY)
    vmem = pl.BlockSpec(memory_space=pltpu.VMEM)
    smem = pl.BlockSpec(memory_space=pltpu.SMEM)
    dma = pltpu.SemaphoreType.DMA
    loss, gcap, gimg = pl.pallas_call(
        functools.partial(kernel, sizes),
        out_shape=(
            jax.ShapeDtypeStruct((1, 128), F32),
            jax.ShapeDtypeStruct((caps, embed), F32),
            jax.ShapeDtypeStruct((1, embed), F32),
        ),
        in_specs=[any_spec, vmem, smem, vmem, any_spec, any_spec, any_spec, any_spec,
                  any_spec, vmem, any_spec, any_spec, any_spec],
        out_specs=(vmem, vmem, vmem),
        scratch_shapes=[
            pltpu.VMEM((dl, 2 * width), BF16),
            pltpu.VMEM((width, dl), BF16),
            pltpu.VMEM((piece, embed), BF16),
            pltpu.VMEM((dv, hv), BF16),
            pltpu.VMEM((hv, dv), BF16),
            pltpu.VMEM((dv, embed), BF16),
            pltpu.VMEM(image_patches.shape, BF16),
            pltpu.VMEM((nd, caps, slots, piece // 2), BF16),
            pltpu.VMEM((8, ncap * slots), F32),
            pltpu.VMEM((micro, batch, dl), BF16),
            pltpu.VMEM((micro, length, 2 * width + 128), BF16),
            pltpu.VMEM((micro, 3 * length, 2 * width + 128), BF16),
            pltpu.VMEM((micro, length, width), BF16),
            pltpu.VMEM((micro, length, width + 128), BF16),
            pltpu.VMEM((micro, 2, length, 2 * width + 128), BF16),
            pltpu.VMEM((micro, batch, width), BF16),
            pltpu.VMEM((micro, batch, dl), BF16),
            pltpu.VMEM((micro, nm - 1, length, piece), BF16),
            pltpu.VMEM((micro, length, piece), BF16),
            pltpu.VMEM((nm - 1, dv // 128, 128), F32),
            pltpu.VMEM((dv // 128, 128), F32),
            pltpu.VMEM((ns * nd, dv // 128, 128), F32),
            pltpu.VMEM((dv // 128, 128), F32),
            pltpu.VMEM((8, dv), F32),
            pltpu.VMEM((ncap, piece), F32),
            pltpu.VMEM((ncap, width), F32),
            pltpu.VMEM((nd, ncap, width), BF16),
            pltpu.VMEM((grp, ncap, piece), F32),
            pltpu.VMEM((nm - 1, ncap, piece), F32),
            pltpu.VMEM((ncap, embed), BF16),
            pltpu.VMEM((nf - 1, ncap, embed), BF16),
            pltpu.VMEM((8, embed), F32),
            dma((9,)), *([dma((micro,))] * 13), dma((nd - 1, micro)),
            dma((micro,)), dma, dma, dma, dma, dma, dma, dma((grp,)), dma, dma, dma, dma((ns * nd,)), dma,
        ],
        compiler_params=pltpu.CompilerParams(
            collective_id=barrier_id, has_side_effects=True, vmem_limit_bytes=60 * 2 ** 20),
        name=f"towers_{micro}_{batch}",
    )(
        strips, caption_lengths, group_ids, text_gain, text_gate, text_up, text_down,
        text_proj, image_patches, image_gain, image_fc1, image_fc2, image_proj,
    )
    return loss[0, 0], gcap, gimg


def solution(mesh):
    sizes = tuple(mesh.shape[axis] for axis in ("section", "dp", "mp"))
    return jax.shard_map(
        functools.partial(per_device, sizes, PLANS),
        mesh=mesh,
        in_specs=(
            P("dp", None, "mp"),
            P("dp"),
            P(),
            P("section", None),
            P("section", "dp", "mp"),
            P("section", "dp", "mp"),
            P("section", "mp", "dp"),
            P("mp", None),
            P("dp", "section", None),
            P(),
            P(None, "mp"),
            P("mp", None),
            P(),
        ),
        out_specs=(P(), P("dp", None), P("dp", None)),
        check_vma=False,
    )
```
